32 devices in a mesh: dp: 8 (over z, x), space: 4 (over y, core).
Axes of the slice: x: 2, y: 2, z: 4, core: 2. Of those that a mesh axis runs over, the one named last changes fastest.
Arguments:
- features: float32 [256, 24, 4, 384], P('dp', None, 'space'), may hold values from -11.25 to 11.25
- cotangent: float32 [256, 24, 4, 384], P('dp', None, 'space'), may hold values from -6 to 6
- segment_ids: int32 [256, 96], P('dp'), may hold values from 0 to 3, as said below
- w_expand: float32 [24, 144], replicated, may hold values from -1.25 to 1.25
- w_depth: float32 [9, 144], replicated, may hold values from -2 to 2
- w_reduce: float32 [144, 6], replicated, may hold values from -0.5 to 0.5
- w_excite: float32 [6, 144], replicated, may hold values from -2.5 to 2.5
- w_project: float32 [144, 24], replicated, may hold values from -0.5 to 0.5
- vector_params: float32 [774], replicated, may hold values from -0.5 to 1.4
- vector_moments: float32 [774], replicated, may hold values from 43690 to 174762
- big_stats: float32 [5, 144, 144], replicated, may hold values from 0 to 25165824
- in_stats: float32 [2, 24, 24], replicated, may hold values from 0 to 25165824
- sq_stats: float32 [2, 6, 6], replicated, may hold values from 0 to 25165824
- tap_stats: float32 [9, 9], replicated, may hold values from 0 to 25165824
Outputs:
- output: float32 [256, 24, 4, 384], P('dp', None, 'space')
- input_grad: float32 [256, 24, 4, 384], P('dp', None, 'space')
- grad_expand: float32 [24, 144], replicated
- grad_depth: float32 [9, 144], replicated
- grad_reduce: float32 [144, 6], replicated
- grad_excite: float32 [6, 144], replicated
- grad_project: float32 [144, 24], replicated
- new_expand: float32 [24, 144], replicated
- new_depth: float32 [9, 144], replicated
- new_reduce: float32 [144, 6], replicated
- new_excite: float32 [6, 144], replicated
- new_project: float32 [144, 24], replicated
- big_stats_new: float32 [5, 144, 144], replicated
- in_stats_new: float32 [2, 24, 24], replicated
- sq_stats_new: float32 [2, 6, 6], replicated
- tap_stats_new: float32 [9, 9], replicated
- vector_grads: float32 [774], replicated
- vector_moments_new: float32 [774], replicated
- vector_new: float32 [774], replicated
The draws below stay inside these ranges and needn't reach their ends.
Inputs may be any that keep to these rules, and one draw needn't show every extreme that they name: `segment_ids`: each slot's frames fall into 4 runs with ids 0, 1, 2, 3 in order, each of two frames or more.
All inputs are finite; a program needn't handle non-finite values.
Results may differ from the reference program's by a relative error of at most 0.0003.
Values sent between devices are 32-bit elements; how exact they have to be, the bound alone decides.
A program may use at most 256 MiB of HBM per device.

```python
import math
import jax
import jax.numpy as jnp
from jax import lax

IN = 24
EXP = 144
SQZ = 6
TAPS = 9
FRAMES = 96
BINS = 16
REGIONS = 4
ROOT_ITERS = 10
SLOTS = 256
QUADS = 4
CELLS = 384
VEC = 774
N_POS = 393216


def draw_features(key, part):
    frame_half = FRAMES // 2
    bin_width = BINS // 2
    shape = (SLOTS, IN, QUADS, CELLS)
    slot_pos = jnp.arange(SLOTS, dtype=jnp.float32) / max(SLOTS - 1, 1)
    quad_index = jnp.arange(QUADS, dtype=jnp.int32)[:, None]
    cell_index = jnp.arange(CELLS, dtype=jnp.int32)[None, :]
    frame_index = quad_index // 2 * frame_half + cell_index // bin_width
    bin_index = quad_index % 2 * bin_width + cell_index % bin_width
    position_rise = 0.5 + frame_index.astype(jnp.float32) / (FRAMES - 1) + bin_index.astype(jnp.float32) / (BINS - 1)
    base = jax.random.truncated_normal(key, -3.0, 3.0, shape, jnp.float32)
    slot_rise = 1.0 + 2.0 * slot_pos
    return 0.5 * base * slot_rise[:, None, None, None] * position_rise[None, None, :, :]


def draw_segment_ids(key, part):
    key_one, key_two, key_three = jax.random.split(key, 3)
    first_cut = jax.random.randint(key_one, (SLOTS, 1), 2, FRAMES // 2 - 1)
    second_cut = jax.random.randint(key_two, (SLOTS, 1), FRAMES // 2 + 2, FRAMES - 4)
    third_cut = jax.random.randint(key_three, (SLOTS, 1), second_cut + 2, FRAMES - 1)
    frame_index = jnp.arange(FRAMES, dtype=jnp.int32)[None, :]
    region = (frame_index >= first_cut).astype(jnp.int32) + (frame_index >= second_cut).astype(jnp.int32)
    return region + (frame_index >= third_cut).astype(jnp.int32)


def draw_vector_params(key, part):
    index = jnp.arange(VEC, dtype=jnp.int32)
    is_gain = (index < EXP) | (index >= 2 * EXP) & (index < 3 * EXP) | (index >= 4 * EXP) & (index < 4 * EXP + IN)
    spread = jax.random.uniform(key, (VEC,), jnp.float32, -1.0, 1.0)
    return jnp.where(is_gain, 1.0 + 0.4 * spread, 0.5 * spread)


def stat_stack(key, dimension, others):
    entries = jnp.exp(jax.random.uniform(key, (len(others), dimension), jnp.float32, 0.0, math.log(4.0)))
    factor = jnp.array(others, jnp.float32)[:, None] * (N_POS / 9.0)
    return (entries * factor)[:, :, None] * jnp.eye(dimension, dtype=jnp.float32)


def draw_big_stats(key, part):
    return stat_stack(key, EXP, [IN, IN, SQZ, SQZ, TAPS])


def draw_in_stats(key, part):
    return stat_stack(key, IN, [EXP, EXP])


def draw_sq_stats(key, part):
    return stat_stack(key, SQZ, [EXP, EXP])


def draw_tap_stats(key, part):
    return stat_stack(key, TAPS, [EXP])[0]


def block_scale(own_key, extent, pieces, least, largest):
    loudness, own = 1.0, jax.random.fold_in(own_key, 6)
    for dim, blocks in pieces:
        heights = jnp.exp(jax.random.uniform(jax.random.fold_in(own, dim), (blocks,), jnp.float32, least / len(pieces), largest / len(pieces)))
        loudness = loudness * jnp.repeat(heights, extent[dim] // blocks).reshape([-1 if axis == dim else 1 for axis in range(len(extent))])
    return loudness


def gaussian(own_key, extent, deviation, reach, cuts=(), kind=jnp.bfloat16):
    values = jax.random.normal(own_key, extent, jnp.float32) * deviation
    if len(cuts) > 0:
        values = block_scale(own_key, extent, cuts, -0.22, 0.18) * values
    return jnp.clip(values, min=-reach, max=reach).astype(kind)


def setup_inputs(seed: int = 0) -> dict:
    splits = jax.random.split(jax.random.key(seed), 15)
    features = draw_features(jax.random.fold_in(splits[14], 71), 0)
    cotangent = gaussian(splits[1], (SLOTS, IN, QUADS, CELLS), 1.0, 6.0, ((0, 8), (2, 4)), jnp.float32)
    segment_ids = draw_segment_ids(jax.random.fold_in(splits[14], 71), 0)
    w_expand = gaussian(splits[3], (IN, EXP), IN ** -0.5, 1.25, (), jnp.float32)
    w_depth = gaussian(splits[4], (TAPS, EXP), TAPS ** -0.5, 2.0, (), jnp.float32)
    w_reduce = gaussian(splits[5], (EXP, SQZ), EXP ** -0.5, 0.5, (), jnp.float32)
    w_excite = gaussian(splits[6], (SQZ, EXP), SQZ ** -0.5, 2.5, (), jnp.float32)
    w_project = gaussian(splits[7], (EXP, IN), EXP ** -0.5, 0.5, (), jnp.float32)
    vector_params = draw_vector_params(jax.random.fold_in(splits[14], 71), 0)
    vector_moments = jnp.clip(jnp.exp(jax.random.uniform(splits[9], (VEC,), jnp.float32, math.log(43690.0), math.log(174762.0))), 43690.0, 174762.0)
    big_stats = draw_big_stats(jax.random.fold_in(splits[14], 71), 0)
    in_stats = draw_in_stats(jax.random.fold_in(splits[14], 71), 0)
    sq_stats = draw_sq_stats(jax.random.fold_in(splits[14], 71), 0)
    tap_stats = draw_tap_stats(jax.random.fold_in(splits[14], 71), 0)
    return dict(features=features, cotangent=cotangent, segment_ids=segment_ids, w_expand=w_expand, w_depth=w_depth, w_reduce=w_reduce, w_excite=w_excite, w_project=w_project, vector_params=vector_params, vector_moments=vector_moments, big_stats=big_stats, in_stats=in_stats, sq_stats=sq_stats, tap_stats=tap_stats)


PRECISE = lax.Precision.HIGHEST
NORM_EPS = 0.001
DECAY = 0.9
STEP_FRACTION = 0.5
VECTOR_RATE = 0.15

@jax.custom_vjp
def low(v):
    return lax.optimization_barrier(v.astype(jnp.bfloat16)).astype(jnp.float32)

@jax.custom_vjp
def low_back(v):
    return v

def low_keep(v):
    return (low(v), None)

def low_pass(kept, grad):
    return (grad,)

def back_keep(v):
    return (v, None)

def back_low(kept, grad):
    return (low(grad),)
low.defvjp(low_keep, low_pass)
low_back.defvjp(back_keep, back_low)

def swish(entries):
    return entries * jax.nn.sigmoid(entries)

def exact_dot(left, right):
    return jnp.dot(left, right, precision=PRECISE)

def split_vector(vector):
    start = 4 * EXP + 2 * IN
    return (vector[0:EXP], vector[EXP:2 * EXP], vector[2 * EXP:3 * EXP], vector[3 * EXP:4 * EXP], vector[4 * EXP:4 * EXP + IN], vector[4 * EXP + IN:start], vector[start:start + SQZ], vector[start + SQZ:])

def excitation(pooled, w_reduce, reduce_bias, w_excite, excite_bias):
    squeezed = swish(jnp.einsum('sre,eq->srq', pooled, w_reduce, precision=PRECISE) + reduce_bias)
    return jax.nn.sigmoid(jnp.einsum('srq,qe->sre', squeezed, w_excite, precision=PRECISE) + excite_bias)

def inverse_root(matrix):
    dimension = matrix.shape[0]
    identity = jnp.eye(dimension, dtype=matrix.dtype)
    scaling = 2.5 / jnp.sqrt(jnp.sum(matrix * matrix))
    current = scaling * matrix
    result = jnp.sqrt(jnp.sqrt(scaling)) * identity
    for iteration in range(ROOT_ITERS):
        factor = 1.25 * identity - 0.25 * current
        result = exact_dot(result, factor)
        square = exact_dot(factor, factor)
        current = exact_dot(exact_dot(square, square), current)
    return result

def precondition(weight, gradient, left_root, right_root):
    direction = exact_dot(exact_dot(left_root, gradient), right_root)
    step_rate = STEP_FRACTION / math.sqrt(weight.shape[0])
    return weight - step_rate * direction * lax.rsqrt(jnp.mean(direction * direction) + 1e-06)

def renew(old_stat, fresh):
    return DECAY * old_stat + (1.0 - DECAY) * fresh

def to_grid(array):
    slot_count, channels = (array.shape[0], array.shape[1])
    frame_half, bin_width = (FRAMES // 2, BINS // 2)
    shaped = array.reshape(slot_count, channels, 2, 2, frame_half, bin_width)
    return shaped.transpose(0, 1, 2, 4, 3, 5).reshape(slot_count, channels, FRAMES, BINS)

def from_grid(array):
    slot_count, channels = (array.shape[0], array.shape[1])
    frame_half, bin_width = (FRAMES // 2, BINS // 2)
    shaped = array.reshape(slot_count, channels, 2, frame_half, 2, bin_width)
    return shaped.transpose(0, 1, 2, 4, 3, 5).reshape(slot_count, channels, 4, frame_half * bin_width)

def normalize(array, gain, shift, axes):
    center = lax.optimization_barrier(jnp.mean(array, axis=axes, keepdims=True))
    centered = array - center
    spread = lax.optimization_barrier(jnp.mean(centered * centered, axis=axes, keepdims=True))
    return centered * lax.rsqrt(spread + NORM_EPS) * gain.reshape(center.shape) + shift.reshape(center.shape)

def depthwise(hidden, kernel, segment_ids):
    frame_count, bin_count = (hidden.shape[1], hidden.shape[2])
    padded = jnp.pad(hidden, ((0, 0), (1, 1), (1, 1), (0, 0)))
    padded_ids = jnp.pad(segment_ids, ((0, 0), (1, 1)), constant_values=-1)
    result = jnp.zeros_like(hidden)
    for row_step in (-1, 0, 1):
        matches = (padded_ids[:, 1 + row_step:1 + row_step + frame_count] == segment_ids).astype(hidden.dtype)
        for col_step in (-1, 0, 1):
            tap_index = (row_step + 1) * 3 + col_step + 1
            window = padded[:, 1 + row_step:1 + row_step + frame_count, 1 + col_step:1 + col_step + bin_count, :]
            result = result + kernel[tap_index] * window * matches[:, :, None, None]
    return result

def forward(features, w_expand, w_depth, w_reduce, w_excite, w_project, vector_params, segment_ids):
    gain_one, shift_one, gain_two, shift_two, gain_three, shift_three, reduce_bias, excite_bias = split_vector(vector_params)
    inputs = to_grid(features)
    expanded = jnp.einsum('sifb,ie->sfbe', inputs, w_expand, precision=PRECISE)
    hidden_one = swish(normalize(expanded, gain_one, shift_one, (0, 1, 2)))
    mixed = depthwise(hidden_one, w_depth, segment_ids)
    hidden_two = swish(normalize(mixed, gain_two, shift_two, (0, 1, 2)))
    regions_hot = (segment_ids[:, :, None] == jnp.arange(REGIONS, dtype=jnp.int32)).astype(hidden_two.dtype)
    region_counts = lax.optimization_barrier(jnp.sum(regions_hot, axis=1)) * BINS
    pooled = jnp.einsum('sfbe,sfr->sre', hidden_two, regions_hot, precision=PRECISE) / region_counts[:, :, None]
    gate = excitation(pooled, w_reduce, reduce_bias, w_excite, excite_bias)
    gated = hidden_two * jnp.einsum('sfr,sre->sfe', regions_hot, gate, precision=PRECISE)[:, :, None, :]
    projected = jnp.einsum('sfbe,eo->sofb', gated, w_project, precision=PRECISE)
    return from_grid(inputs + normalize(projected, gain_three, shift_three, (0, 2, 3)))

def reference(features, cotangent, segment_ids, w_expand, w_depth, w_reduce, w_excite, w_project, vector_params, vector_moments, big_stats, in_stats, sq_stats, tap_stats):

    def apply_block(feat, wexp, wdep, wred, wexc, wpro, vecs):
        return forward(feat, wexp, wdep, wred, wexc, wpro, vecs, segment_ids)
    output, pullback = jax.vjp(apply_block, features, w_expand, w_depth, w_reduce, w_excite, w_project, vector_params)
    input_grad, grad_expand, grad_depth, grad_reduce, grad_excite, grad_project, vector_grads = pullback(cotangent)
    big_new = renew(big_stats, jnp.stack([exact_dot(grad_expand.T, grad_expand), exact_dot(grad_project, grad_project.T), exact_dot(grad_reduce, grad_reduce.T), exact_dot(grad_excite.T, grad_excite), exact_dot(grad_depth.T, grad_depth)]))
    in_new = renew(in_stats, jnp.stack([exact_dot(grad_expand, grad_expand.T), exact_dot(grad_project.T, grad_project)]))
    sq_new = renew(sq_stats, jnp.stack([exact_dot(grad_reduce.T, grad_reduce), exact_dot(grad_excite, grad_excite.T)]))
    tap_new = renew(tap_stats, exact_dot(grad_depth, grad_depth.T))
    big_roots = [inverse_root(big_new[index]) for index in range(5)]
    new_expand = precondition(w_expand, grad_expand, inverse_root(in_new[0]), big_roots[0])
    new_depth = precondition(w_depth, grad_depth, inverse_root(tap_new), big_roots[4])
    new_reduce = precondition(w_reduce, grad_reduce, big_roots[2], inverse_root(sq_new[0]))
    new_excite = precondition(w_excite, grad_excite, inverse_root(sq_new[1]), big_roots[3])
    new_project = precondition(w_project, grad_project, big_roots[1], inverse_root(in_new[1]))
    moments_new = DECAY * vector_moments + (1.0 - DECAY) * vector_grads * vector_grads
    vector_new = vector_params - VECTOR_RATE * vector_grads / (jnp.sqrt(moments_new) + 1e-08)
    return (output, input_grad, grad_expand, grad_depth, grad_reduce, grad_excite, grad_project, new_expand, new_depth, new_reduce, new_excite, new_project, big_new, in_new, sq_new, tap_new, vector_grads, moments_new, vector_new)
```

```python
import functools
import math

import jax
import jax.numpy as jnp
from jax import lax
from jax.experimental import pallas as pl
from jax.experimental.pallas import tpu as pltpu
from jax.sharding import PartitionSpec as P

IN = 24
EXP = 144
SQZ = 6
TAPS = 9
FRAMES = 96
BINS = 16
REGIONS = 4
QUADS = 4
ROOT_ITERS = 10
NORM_EPS = 0.001
DECAY = 0.9
FRESH = 1.0 - DECAY
STEP_FRACTION = 0.5
VECTOR_RATE = 0.15

LANES = 128
HALF_W = 6
WIDE = 2 * HALF_W
ROWS = IN * 3
GROUP = 8
BULK = 16

F32 = jnp.float32
BF16 = jnp.bfloat16
FULL = lax.Precision.HIGHEST
MID = lax.Precision.HIGH
MESH = pl.DeviceIdType.MESH


def mm(left, right, dims, precision=None):
    return lax.dot_general(
        left, right, ((dims[:1], dims[1:]), ((), ())), precision=precision, preferred_element_type=F32
    )


def nn(left, right, precision=None):
    return mm(left, right, (1, 0), precision)


def nt(left, right, precision=None):
    return mm(left, right, (1, 1), precision)


def tn(left, right, precision=None):
    return mm(left, right, (0, 0), precision)


def halves(value):
    high = value.astype(BF16)
    return high, (value - high.astype(F32)).astype(BF16)


def column(rows, index, width):
    pick = (lax.broadcasted_iota(jnp.int32, (rows.shape[0], LANES), 0) == index).astype(F32)
    return tn(rows, pick, FULL)[:width]


def lane_sums(table):
    return nt(jnp.ones((8, table.shape[1]), F32), table, FULL)[0:1]


def split_row(row):
    return jnp.concatenate(
        [row[:, :LANES], jnp.concatenate([row[:, LANES:], jnp.zeros((1, 2 * LANES - EXP), F32)], axis=1)], axis=0
    )


def join_row(pair):
    return jnp.concatenate([pair[0:1], pair[1:2, : EXP - LANES]], axis=1)


def tile_quad(n):
    return 2 * ((n % HALF_W) // 3) + n // HALF_W


def on_lane(n):
    return pl.ds(n * LANES, LANES)


def block_kernel(
    n_dev, n_space, slots, n_pos,
    feat, cot, ids_ref, w_exp, w_dep, w_red_t, w_exc, w_pro_t, prm, big, in_st, sq_st, tap_st,
    out, ing, gs_out, nw_out, vr_out,
    xloc, xq, cq, xs, v1, a2, hh, dn2, dh, a3, hot, dcat, tab, msk, reg, acc, w1t, wlow,
    small, pooled, gates, dgate, bulk, bulk_in, bulk_all, rb1, rb, nws, fold,
    loc_sem, x_send, x_recv, c_send, c_recv, o_send, o_recv, g_send, g_recv,
    r_send, r_recv, own_sem,
):
    space = lax.axis_index("space")
    me = lax.axis_index("dp") * n_space + space
    n_loc = float(slots * FRAMES * BINS)
    total = float(n_pos)

    def device(index):
        return (lax.div(index, n_space), lax.rem(index, n_space))

    def peer(step):
        return lax.rem(space + step, QUADS)

    def space_device(step):
        return (lax.axis_index("dp"), peer(step))

    barrier = pltpu.get_barrier_semaphore()

    def greet(step, carry):
        pl.semaphore_signal(
            barrier, inc=1, device_id=device(lax.rem(me + step, n_dev)), device_id_type=MESH
        )
        return carry

    lax.fori_loop(1, n_dev, greet, 0)
    loads = [
        pltpu.make_async_copy(feat.at[pl.ds(slots * q, slots)], xloc.at[q], loc_sem.at[q]) for q in range(QUADS)
    ]
    for load in loads:
        load.start()
    own_x = pltpu.make_async_copy(feat.at[pl.ds(slots * space, slots)], xq.at[space], own_sem.at[0])
    own_c = pltpu.make_async_copy(cot.at[pl.ds(slots * space, slots)], cq.at[space], own_sem.at[1])
    own_x.start()
    own_c.start()

    lane = lax.broadcasted_iota(jnp.int32, (8, LANES), 1)
    low_bin = lax.rem(lane, 8) == 0
    high_bin = lax.rem(lane, 8) == 7
    first_row = lane < 8
    last_row = lane >= LANES - 8
    zero_tile = jnp.zeros((8, LANES), F32)

    half_lanes = HALF_W * LANES
    own_ids = ids_ref[pl.ds(pl.multiple_of(slots * space, 8), slots), :].astype(F32)
    spread = (
        lax.broadcasted_iota(jnp.int32, (FRAMES, half_lanes), 1) // 8
        == lax.broadcasted_iota(jnp.int32, (FRAMES, half_lanes), 0)
    )
    wide_ids = nn(own_ids.astype(BF16), spread.astype(F32).astype(BF16))
    wide_lane = lax.broadcasted_iota(jnp.int32, (slots, half_lanes), 1)
    before = pltpu.roll(wide_ids, 8, 1)
    after = pltpu.roll(wide_ids, half_lanes - 8, 1)
    from_ok = jnp.where((before == wide_ids) & (wide_lane >= 8), 1.0, 0.0)
    to_ok = jnp.where((after == wide_ids) & (wide_lane < half_lanes - 8), 1.0, 0.0)
    for s in range(slots):
        msk[0, s] = jnp.broadcast_to(from_ok[s : s + 1], (8, half_lanes))
        msk[1, s] = jnp.broadcast_to(to_ok[s : s + 1], (8, half_lanes))
        for r in range(REGIONS):
            reg[r, s] = jnp.broadcast_to((wide_ids[s : s + 1] == float(r)).astype(F32), (8, half_lanes))
    row_index = lax.broadcasted_iota(jnp.int32, (slots * REGIONS, half_lanes), 0)
    row_region = lax.rem(row_index, REGIONS).astype(F32)
    counts = jnp.zeros((slots * REGIONS, 1), F32)
    for s in range(slots):
        row = jnp.where(
            (lax.div(row_index, REGIONS) == s) & (wide_ids[s : s + 1] == row_region), 1.0, 0.0
        )
        counts = counts + 2.0 * jnp.sum(row, axis=1, keepdims=True)
        hot[s, :, :half_lanes] = row.astype(BF16)
        hot[s, :, half_lanes:] = row.astype(BF16)
    taps = w_dep[...]
    for t in range(TAPS):
        tab[t] = column(taps, t, EXP)

    for load in loads:
        load.wait()
    first = jnp.concatenate([xloc[0, 0, pl.ds(k, IN, stride=3), :] for k in range(3)], axis=1)
    shift_col = nn(first, jnp.ones((3 * LANES, LANES), F32), FULL) * (1.0 / (3 * LANES))
    shift_row = nt(jnp.ones((8, 3 * LANES), F32), first, FULL)[0:1] * (1.0 / (3 * LANES))
    one_rows = (lax.broadcasted_iota(jnp.int32, (8, LANES), 0) == 0).astype(F32)

    def gram_step(s, gram):
        parts = []
        for q in range(QUADS):
            for k in range(3):
                parts.append(
                    jnp.concatenate([xloc[q, s, pl.ds(k, IN, stride=3), :] - shift_col, one_rows], axis=0)
                )
        high, low = halves(jnp.concatenate(parts, axis=1))
        both = jnp.concatenate([high, low], axis=0)
        return gram + nt(both, both)

    gram = lax.fori_loop(0, slots, gram_step, jnp.zeros((64, 64), F32))
    gram = gram[:32, :32] + gram[32:, :32] + gram[:32, 32:] + gram[32:, 32:]
    off_row = gram[IN : IN + 1, :IN] * (1.0 / n_loc)
    off_col = gram[:IN, IN : IN + 1] * (1.0 / n_loc)
    local_m2 = gram[:IN, :IN] - n_loc * off_col * off_row
    fold[...] = jnp.zeros((IN, LANES), F32)
    fold[:, :IN] = local_m2
    packed = jnp.zeros((6, LANES), F32)
    for g in range(4):
        piece = fold[pl.ds(g, 6, stride=4), :]
        packed = packed + (pltpu.roll(piece, 32 * g, 1) if g else piece)
    rb1[me, 0:6, :] = packed
    rb1[me, 6:7, :] = jnp.concatenate([shift_row + off_row, jnp.zeros((1, LANES - IN), F32)], axis=1)
    rb1[me, 7:8, :] = jnp.zeros((1, LANES), F32)

    pl.semaphore_wait(barrier, n_dev - 1)

    def spread_start(source, target, index):
        def send(step, carry):
            pltpu.make_async_remote_copy(
                src_ref=source, dst_ref=target, send_sem=r_send.at[index], recv_sem=r_recv.at[index],
                device_id=device(lax.rem(me + step, n_dev)), device_id_type=MESH,
            ).start()
            return carry

        lax.fori_loop(1, n_dev, send, 0)

    def spread_wait(window, index):
        done = pltpu.make_async_remote_copy(
            src_ref=window, dst_ref=window, send_sem=r_send.at[index], recv_sem=r_recv.at[index],
            device_id=device(me), device_id_type=MESH,
        )
        done.wait_send()
        done.wait_recv()

    def quad_copy(source, target, send, recv, step, s):
        return pltpu.make_async_remote_copy(
            src_ref=source, dst_ref=target, send_sem=send.at[step, s], recv_sem=recv.at[step, s],
            device_id=space_device(step), device_id_type=MESH,
        )

    def x_copy(step, s):
        return quad_copy(feat.at[slots * peer(step) + s], xq.at[space, s], x_send, x_recv, step, s)

    def c_copy(step, s):
        return quad_copy(cot.at[slots * peer(step) + s], cq.at[space, s], c_send, c_recv, step, s)

    def o_copy(step, s):
        return quad_copy(xloc.at[peer(step), s], out.at[slots * space + s], o_send, o_recv, step, s)

    def g_copy(step, s):
        return quad_copy(xq.at[peer(step), s], ing.at[slots * space + s], g_send, g_recv, step, s)

    spread_start(rb1.at[me], rb1.at[me], 0)

    def x_start(s, carry):
        for step in range(1, QUADS):
            x_copy(step, s).start()
        return carry

    lax.fori_loop(0, slots, x_start, 0)

    spread_wait(rb1.at[pl.ds(0, n_dev - 1)], 0)
    gathered = jnp.sum(rb1[...], axis=0)
    means = rb1[:, 6, :]
    mean_row = jnp.sum(means, axis=0, keepdims=True) * (1.0 / n_dev)
    apart = means - mean_row
    between = tn(apart, apart, FULL)[:IN, :IN]
    for g in range(4):
        piece = gathered[0:6]
        piece = pltpu.roll(piece, LANES - 32 * g, 1) if g else piece
        fold[pl.ds(g, 6, stride=4), :] = piece
    moment = fold[:, :IN] + n_loc * between
    eye24 = (
        lax.broadcasted_iota(jnp.int32, (IN, IN), 0) == lax.broadcasted_iota(jnp.int32, (IN, IN), 1)
    )
    mean_col = nn(jnp.where(eye24, mean_row[:, :IN], 0.0), jnp.ones((IN, LANES), F32), FULL)
    weight = w_exp[...]
    moment_w = nn(moment, weight, FULL)
    scale1 = lax.rsqrt(jnp.sum(moment_w * weight, axis=0, keepdims=True) * (1.0 / total) + NORM_EPS)
    grow1 = prm[0:1, :] * scale1
    shaped = jnp.concatenate(
        [weight * (0.5 * grow1), 0.5 * prm[1:2, :], jnp.zeros((7, EXP), F32)], axis=0
    )
    shaped_high = shaped.astype(BF16).astype(F32)
    w1t[...] = jnp.transpose(
        jnp.concatenate([shaped_high, shaped_high, shaped - shaped_high], axis=0)
    ).astype(BF16)

    own_x.wait()
    acc[0] = jnp.zeros((EXP, LANES), F32)

    def x_tile(s, n):
        return xq[tile_quad(n), s, pl.ds(n % 3, IN, stride=3), :]

    def c_tile(s, n):
        return cq[tile_quad(n), s, pl.ds(n % 3, IN, stride=3), :]

    def later_bin(low, high):
        return (
            jnp.where(high_bin, pltpu.roll(high, 7, 1), pltpu.roll(low, LANES - 1, 1)),
            jnp.where(high_bin, 0.0, pltpu.roll(high, LANES - 1, 1)),
        )

    def earlier_bin(low, high):
        return (
            jnp.where(low_bin, 0.0, pltpu.roll(low, 1, 1)),
            jnp.where(low_bin, pltpu.roll(low, LANES - 7, 1), pltpu.roll(high, 1, 1)),
        )

    def from_before(tiles, k):
        return pltpu.roll(jnp.where(last_row, tiles[max(k - 1, 0)], tiles[k]), 8, 1)

    def from_after(tiles, k):
        return pltpu.roll(jnp.where(first_row, tiles[min(k + 1, HALF_W - 1)], tiles[k]), LANES - 8, 1)

    def forward_slot(s, carry):
        for step in range(1, QUADS):
            x_copy(step, s).wait_recv()
        for n in range(WIDE):
            tile = jnp.concatenate([x_tile(s, n) - mean_col, one_rows], axis=0)
            high, low = halves(tile)
            xs[s, 0:32, on_lane(n)] = high
            xs[s, 32:64, on_lane(n)] = low
            xs[s, 64:96, on_lane(n)] = high
        for step in range(1, QUADS):
            c_copy(step, s).start()
        v1[s] = nn(w1t[...], xs[s])

        def taps_step(j, carry):
            rows = pl.ds(pl.multiple_of(8 * j, 8), 8)
            wt = [tab[t, rows, :] for t in range(TAPS)]
            keep = [[[None] * HALF_W for _ in range(2)] for _ in range(3)]
            for k in range(HALF_W):
                pair = []
                for half in range(2):
                    v = v1[s, rows, on_lane(half * HALF_W + k)]
                    pair.append(v + v * jnp.tanh(v))
                nxt = later_bin(*pair)
                prv = earlier_bin(*pair)
                for half in range(2):
                    for p in range(3):
                        keep[p][half][k] = (
                            wt[3 * p] * prv[half] + wt[3 * p + 1] * pair[half] + wt[3 * p + 2] * nxt[half]
                        )
            got = zero_tile
            for k in range(HALF_W):
                back_ok = msk[0, s, :, on_lane(k)]
                fore_ok = msk[1, s, :, on_lane(k)]
                for half in range(2):
                    value = (
                        keep[1][half][k]
                        + back_ok * from_before(keep[0][half], k)
                        + fore_ok * from_after(keep[2][half], k)
                    )
                    a2[s, rows, on_lane(half * HALF_W + k)] = value
                    got = got + value
            acc[0, rows, :] = acc[0, rows, :] + got
            return carry

        lax.fori_loop(0, EXP // 8, taps_step, 0)
        return carry

    lax.fori_loop(0, slots, forward_slot, 0)

    acc[1] = nn(acc[0], jnp.ones((LANES, LANES), F32), FULL) * (1.0 / n_loc)
    acc[2] = jnp.zeros((EXP, LANES), F32)

    def square_step(s, carry):
        def tile_step(j, carry):
            rows = pl.ds(pl.multiple_of(8 * j, 8), 8)
            center = acc[1, rows, :]
            got = zero_tile
            for n in range(WIDE):
                off = a2[s, rows, on_lane(n)] - center
                got = got + off * off
            acc[2, rows, :] = acc[2, rows, :] + got
            return carry

        return lax.fori_loop(0, EXP // 8, tile_step, carry)

    lax.fori_loop(0, slots, square_step, 0)
    rb[0, me, 0:2, :] = split_row(lane_sums(acc[0]) * (1.0 / n_loc))
    rb[0, me, 2:4, :] = split_row(lane_sums(acc[2]))
    spread_start(rb.at[0, me], rb.at[0, me], 1)
    spread_wait(rb.at[0, pl.ds(0, n_dev - 1)], 1)
    sums = jnp.sum(rb[0], axis=0)
    mean2 = sums[0:2] * (1.0 / n_dev)
    gaps = rb[0][:, 0:2, :] - mean2[None]
    spread2 = sums[2:4] + n_loc * jnp.sum(gaps * gaps, axis=0)
    scale2 = lax.rsqrt(join_row(spread2) * (1.0 / total) + NORM_EPS)
    mean2 = join_row(mean2)
    rows8 = jnp.concatenate(
        [mean2, 0.5 * prm[2:3, :] * scale2, 0.5 * prm[3:4, :], jnp.zeros((5, EXP), F32)], axis=0
    )
    for i in range(3):
        tab[TAPS + i] = column(rows8, i, EXP)

    pooled[...] = jnp.zeros((slots * REGIONS, EXP), F32)

    def activate_slot(s, carry):
        def step(j, carry):
            rows = pl.ds(pl.multiple_of(16 * j, 16), 16)
            low_rows = pl.ds(pl.multiple_of(EXP + 16 * j, 16), 16)
            center, grow, lift = (tab[TAPS + i, rows, :] for i in range(3))
            for n in range(WIDE):
                off = a2[s, rows, on_lane(n)] - center
                a2[s, rows, on_lane(n)] = off
                v = off * grow + lift
                high, low = halves(v + v * jnp.tanh(v))
                hh[s, rows, on_lane(n)] = high
                hh[s, low_rows, on_lane(n)] = low
            return carry

        lax.fori_loop(0, EXP // 16, step, 0)
        pooled[...] = pooled[...] + nt(hot[s], hh[s, 0:EXP, :]) + nt(hot[s], hh[s, EXP:, :])
        return carry

    lax.fori_loop(0, slots, activate_slot, 0)

    per_count = 1.0 / counts
    mean_pool = pooled[...] * per_count
    squeeze = nt(mean_pool, w_red_t[...], FULL) + prm[6:7, :SQZ]
    squeeze_sig = jax.nn.sigmoid(squeeze)
    squeezed = squeeze * squeeze_sig
    gate = jax.nn.sigmoid(nn(squeezed, w_exc[...], FULL) + prm[7:8, :])
    for s in range(slots):
        gates[s] = gate[REGIONS * s : REGIONS * (s + 1)]

    def gated_weights(s):
        project = w_pro_t[...]
        rows = gates[s]
        return jnp.concatenate([project * rows[r : r + 1] for r in range(REGIONS)], axis=0)

    def region_tile(r, s, n):
        return jnp.concatenate([reg[r, s, :, on_lane(n % HALF_W)]] * (IN // 8), axis=0)

    def project_slot(s, carry):
        total_a, total_c = carry
        high, low = halves(gated_weights(s))
        body = nn(jnp.concatenate([high, low], axis=0), hh[s, 0:EXP, :])
        body = body[:96] + body[96:] + nn(high, hh[s, EXP:, :])
        for step in range(1, QUADS):
            c_copy(step, s).wait_recv()
        for n in range(WIDE):
            value = jnp.zeros((IN, LANES), F32)
            for r in range(REGIONS):
                value = value + (
                    body[IN * r : IN * (r + 1), n * LANES : (n + 1) * LANES]
                    * region_tile(r, s, n)
                )
            a3[s, :, on_lane(n)] = value
            total_a = total_a + value
            total_c = total_c + c_tile(s, n)
        return total_a, total_c

    own_c.wait()
    zero24 = jnp.zeros((IN, LANES), F32)
    total_a, total_c = lax.fori_loop(0, slots, project_slot, (zero24, zero24))
    center3 = nn(total_a, jnp.ones((LANES, LANES), F32), FULL) * (1.0 / n_loc)

    def third_step(s, carry):
        square, cross = carry
        for n in range(WIDE):
            off = a3[s, :, on_lane(n)] - center3
            square = square + off * off
            cross = cross + off * c_tile(s, n)
        return square, cross

    square3, cross3 = lax.fori_loop(0, slots, third_step, (zero24, zero24))

    def pad_row(row):
        return jnp.concatenate([row, jnp.zeros((1, LANES - IN), F32)], axis=1)

    rb[1, me] = jnp.concatenate(
        [
            pad_row(lane_sums(total_a) * (1.0 / n_loc)),
            pad_row(lane_sums(square3)),
            pad_row(lane_sums(total_c)),
            pad_row(lane_sums(cross3)),
        ],
        axis=0,
    )
    spread_start(rb.at[1, me], rb.at[1, me], 2)
    spread_wait(rb.at[1, pl.ds(0, n_dev - 1)], 2)
    third = rb[1]
    sums = jnp.sum(third, axis=0)
    mean3 = sums[0:1] * (1.0 / n_dev)
    gaps = third[:, 0, :] - mean3
    spread3 = sums[1:2] + n_loc * jnp.sum(gaps * gaps, axis=0, keepdims=True)
    scale3 = lax.rsqrt(spread3 * (1.0 / total) + NORM_EPS)
    bias3_grad = sums[2:3]
    cross_sum = sums[3:4] + jnp.sum(third[:, 2, :] * gaps, axis=0, keepdims=True)
    gain3_grad = scale3 * cross_sum
    grow3 = prm[4:5, :LANES] * scale3
    rows8 = jnp.concatenate(
        [
            mean3,
            grow3,
            prm[5:6, :LANES],
            grow3 * bias3_grad * (1.0 / total),
            grow3 * scale3 * gain3_grad * (1.0 / total),
            jnp.zeros((3, LANES), F32),
        ],
        axis=0,
    )
    mean3_c, grow3_c, lift3_c, flat3_c, lean3_c = (column(rows8, i, IN) for i in range(5))

    small[0] = jnp.zeros((IN, EXP), F32)

    def back_slot(s, carry):
        for n in range(WIDE):
            off = a3[s, :, on_lane(n)] - mean3_c
            xloc[tile_quad(n), s, pl.ds(n % 3, IN, stride=3), :] = x_tile(s, n) + off * grow3_c + lift3_c
            grad = grow3_c * c_tile(s, n) - flat3_c - off * lean3_c
            high, low = halves(
                jnp.concatenate(
                    [grad * region_tile(r, s, n) for r in range(REGIONS)], axis=0
                )
            )
            dcat[s, 0:96, on_lane(n)] = high
            dcat[s, 128:224, on_lane(n)] = low
        dcat[s, 96:128, :] = hot[s]
        dcat[s, 224:256, :] = hot[s]
        for step in range(1, QUADS):
            o_copy(step, s).start()
        main = nt(dcat[s, 0:224, :], hh[s, 0:EXP, :])
        main = main[0:96] + main[128:224] + nt(dcat[s, 0:96, :], hh[s, EXP:, :])
        project = w_pro_t[...]
        gp = small[0]
        rows = gates[s]
        for r in range(REGIONS):
            part = main[IN * r : IN * (r + 1)]
            dgate[s, r : r + 1, :] = jnp.sum(part * project, axis=0, keepdims=True)
            gp = gp + part * rows[r : r + 1]
        small[0] = gp
        return carry

    lax.fori_loop(0, slots, back_slot, 0)
    own_o = pltpu.make_async_copy(xloc.at[space], out.at[pl.ds(slots * space, slots)], own_sem.at[2])
    own_o.start()

    dgate_rows = jnp.concatenate([dgate[s] for s in range(slots)], axis=0)
    dpre_x = dgate_rows * gate * (1.0 - gate)
    excite_grad = tn(squeezed, dpre_x, FULL)
    excite_bias_grad = jnp.sum(dpre_x, axis=0, keepdims=True)
    dsqueezed = nt(dpre_x, w_exc[...], FULL)
    dpre_r = dsqueezed * squeeze_sig * (1.0 + squeeze * (1.0 - squeeze_sig))
    reduce_grad = tn(dpre_r, mean_pool, FULL)
    reduce_bias_grad = jnp.sum(dpre_r, axis=0, keepdims=True)
    dpool = nn(dpre_r, w_red_t[...], FULL) * per_count
    pooled[...] = 0.5 * dpool

    acc[0] = jnp.zeros((EXP, LANES), F32)
    acc[1] = jnp.zeros((EXP, LANES), F32)

    def second_back_slot(s, carry):
        high, low = halves(0.5 * gated_weights(s))
        pool_high, pool_low = halves(pooled[...])
        left = jnp.concatenate([high, pool_high, high, pool_low], axis=0)
        dh[...] = tn(left, dcat[s]) + tn(low, dcat[s, 0:96, :])

        def step(j, carry):
            rows = pl.ds(pl.multiple_of(8 * j, 8), 8)
            grow, lift = (tab[TAPS + i, rows, :] for i in (1, 2))
            plain, cross = zero_tile, zero_tile
            for n in range(WIDE):
                off = a2[s, rows, on_lane(n)]
                v = off * grow + lift
                u = 1.0 + jnp.tanh(v)
                d = dh[rows, on_lane(n)] * (u + (v * u) * (2.0 - u))
                dn2[s, rows, on_lane(n)] = d
                plain = plain + d
                cross = cross + d * off
            acc[0, rows, :] = acc[0, rows, :] + plain
            acc[1, rows, :] = acc[1, rows, :] + cross
            return carry

        lax.fori_loop(0, EXP // 8, step, 0)
        return carry

    lax.fori_loop(0, slots, second_back_slot, 0)
    rb[2, me, 0:2, :] = split_row(lane_sums(acc[0]))
    rb[2, me, 2:4, :] = split_row(lane_sums(acc[1]))
    spread_start(rb.at[2, me], rb.at[2, me], 3)
    spread_wait(rb.at[2, pl.ds(0, n_dev - 1)], 3)
    sums = jnp.sum(rb[2], axis=0)
    bias2_grad = join_row(sums[0:2])
    cross2 = join_row(sums[2:4])
    gain2_grad = cross2 * scale2
    grow2 = prm[2:3, :] * scale2
    rows8 = jnp.concatenate(
        [
            grow2,
            -grow2 * scale2 * gain2_grad * (1.0 / total),
            -grow2 * bias2_grad * (1.0 / total),
            jnp.zeros((5, EXP), F32),
        ],
        axis=0,
    )
    for i in range(3):
        tab[TAPS + i] = column(rows8, i, EXP)

    for t in range(TAPS):
        acc[t] = jnp.zeros((EXP, LANES), F32)
    small[1] = jnp.zeros((IN, EXP), F32)
    small[2] = jnp.zeros((IN, EXP), F32)

    def taps_back_slot(s, carry):
        def step(j, carry):
            rows = pl.ds(pl.multiple_of(8 * j, 8), 8)
            wt = [tab[t, rows, :] for t in range(TAPS)]
            k1, k2, k3 = (tab[TAPS + i, rows, :] for i in range(3))
            grads = [[], []]
            for half in range(2):
                for k in range(HALF_W):
                    where = on_lane(half * HALF_W + k)
                    grads[half].append(k1 * dn2[s, rows, where] + k2 * a2[s, rows, where] + k3)
            sums = [zero_tile] * TAPS
            for k in range(HALF_W):
                back_ok = msk[0, s, :, on_lane(k)]
                fore_ok = msk[1, s, :, on_lane(k)]
                vs, us, hs = [], [], []
                for half in range(2):
                    v = v1[s, rows, on_lane(half * HALF_W + k)]
                    u = 1.0 + jnp.tanh(v)
                    vs.append(v)
                    us.append(u)
                    hs.append(v * u)
                near = [earlier_bin(*hs), hs, later_bin(*hs)]
                mix = [[], [], []]
                for half in range(2):
                    moved = [
                        fore_ok * from_after(grads[half], k),
                        grads[half][k],
                        back_ok * from_before(grads[half], k),
                    ]
                    for q in range(3):
                        mix[q].append(
                            wt[q] * moved[0] + wt[3 + q] * moved[1] + wt[6 + q] * moved[2]
                        )
                        for p in range(3):
                            sums[3 * p + q] = sums[3 * p + q] + moved[p] * near[q][half]
                left = later_bin(*mix[0])
                right = earlier_bin(*mix[2])
                for half in range(2):
                    d = (left[half] + mix[1][half] + right[half]) * (
                        us[half] + hs[half] * (2.0 - us[half])
                    )
                    dh[rows, on_lane(half * HALF_W + k)] = d
            for t in range(TAPS):
                acc[t, rows, :] = acc[t, rows, :] + sums[t]
            return carry

        lax.fori_loop(0, EXP // 8, step, 0)

        def pack(j, carry):
            rows = pl.ds(pl.multiple_of(16 * j, 16), 16)
            low_rows = pl.ds(pl.multiple_of(EXP + 16 * j, 16), 16)
            for n in range(WIDE):
                high, low = halves(0.5 * dh[rows, on_lane(n)])
                hh[s, rows, on_lane(n)] = high
                hh[s, low_rows, on_lane(n)] = low
            return carry

        lax.fori_loop(0, EXP // 16, pack, 0)
        main = nt(xs[s, 0:64, :], hh[s, 0:EXP, :])
        main = main[0:32] + main[32:64] + nt(xs[s, 0:32, :], hh[s, EXP:, :])
        small[1] = small[1] + main[0:IN]
        small[2, 0:8, :] = small[2, 0:8, :] + main[IN:32]
        return carry

    lax.fori_loop(0, slots, taps_back_slot, 0)

    stacked = [small[0], small[1], small[2, 0:8, :]]
    tail = [lane_sums(acc[t]) for t in range(TAPS)]
    tail.append(excite_bias_grad)
    tail.append(jnp.concatenate([reduce_bias_grad, jnp.zeros((1, EXP - SQZ), F32)], axis=1))
    tail.append(jnp.zeros((5, EXP), F32))
    stacked.append(jnp.concatenate(tail, axis=0))
    for part in (excite_grad, reduce_grad):
        stacked.append(jnp.concatenate([part, jnp.zeros((8 - SQZ, EXP), F32)], axis=0))
    stacked = jnp.concatenate(stacked, axis=0)
    n_heads = 11
    for i in range(n_heads):
        bulk[i] = stacked[8 * i : 8 * i + 8, :LANES]
    ends = [stacked[8 * i : 8 * i + 8, LANES:] for i in range(n_heads)]
    bulk[n_heads] = jnp.concatenate(ends[:8], axis=1)
    bulk[n_heads + 1] = jnp.concatenate(ends[8:] + [jnp.zeros((8, LANES - 16 * (n_heads - 8)), F32)], axis=1)
    for i in range(n_heads + 2, BULK):
        bulk[i] = zero_tile
    each = BULK // GROUP
    base = lax.div(me, GROUP) * GROUP
    place = lax.rem(me, GROUP)

    def group_copy(source, target, index, step):
        return pltpu.make_async_remote_copy(
            src_ref=source, dst_ref=target, send_sem=r_send.at[index], recv_sem=r_recv.at[index],
            device_id=device(base + lax.rem(place + step, GROUP)), device_id_type=MESH,
        )

    for step in range(1, GROUP):
        other = lax.rem(place + step, GROUP)
        group_copy(bulk.at[pl.ds(each * other, each)], bulk_in.at[place], 4, step).start()
    bulk_in[place] = bulk[pl.ds(each * place, each)]
    done = group_copy(bulk_in.at[pl.ds(0, GROUP - 1)], bulk_in.at[pl.ds(0, GROUP - 1)], 4, 1)
    done.wait_send()
    done.wait_recv()
    bulk_all[me] = jnp.sum(bulk_in[...], axis=0)
    spread_start(bulk_all.at[me], bulk_all.at[me], 5)
    spread_wait(bulk_all.at[pl.ds(0, n_dev - 1)], 5)
    summed = []
    for i in range(n_heads + 2):
        tile = zero_tile
        for g in range(n_dev // GROUP):
            tile = tile + bulk_all[g * GROUP + i // each, i % each]
        summed.append(tile)

    def row_tile(i):
        rest = summed[n_heads + i // 8][:, 16 * (i % 8) : 16 * (i % 8) + 16]
        return jnp.concatenate([summed[i], rest], axis=1)

    project_grad = jnp.concatenate([row_tile(i) for i in range(3)], axis=0)
    expand_cross = jnp.concatenate([row_tile(i) for i in range(3, 6)], axis=0)
    bias1_grad = row_tile(6)[0:1]
    depth_tiles = jnp.concatenate([row_tile(7), row_tile(8)], axis=0)
    excite_tile = row_tile(9)
    reduce_tile = row_tile(10)
    cross1 = jnp.sum(expand_cross * weight, axis=0, keepdims=True)
    gain1_grad = scale1 * cross1
    lean1 = scale1 * gain1_grad * (1.0 / total)
    expand_grad = grow1 * (expand_cross - lean1 * moment_w)
    zero_rows = jnp.zeros((16, EXP), F32)
    gs_out[0] = expand_grad
    gs_out[1] = project_grad
    gs_out[2] = jnp.concatenate([reduce_tile, zero_rows], axis=0)
    gs_out[3] = jnp.concatenate([excite_tile, zero_rows], axis=0)
    row16 = lax.broadcasted_iota(jnp.int32, (16, EXP), 0)
    gs_out[4] = jnp.concatenate([jnp.where(row16 < TAPS, depth_tiles, 0.0), zero_rows[:8]], axis=0)
    vr_out[...] = jnp.concatenate(
        [
            gain1_grad,
            bias1_grad,
            gain2_grad,
            bias2_grad,
            jnp.concatenate([gain3_grad, jnp.zeros((1, EXP - LANES), F32)], axis=1),
            jnp.concatenate([bias3_grad, jnp.zeros((1, EXP - LANES), F32)], axis=1),
            depth_tiles[TAPS + 1 : TAPS + 2],
            depth_tiles[TAPS : TAPS + 1],
        ],
        axis=0,
    )

    for step in range(1, QUADS):
        def o_done(s, carry, step=step):
            o_copy(step, s).wait_send()
            x_copy(step, s).wait_send()
            c_copy(step, s).wait_send()
            return carry

        lax.fori_loop(0, slots, o_done, 0)
    grown = weight * grow1
    grown_high = grown.astype(BF16)
    grown_both = jnp.concatenate([grown_high.astype(F32), grown - grown_high.astype(F32)], axis=0).astype(BF16)
    lean_map = -nt(grown * lean1, weight, FULL)
    flat_col = -jnp.sum(grown * (bias1_grad * (1.0 / total)), axis=1, keepdims=True)
    side = jnp.concatenate([lean_map, flat_col, jnp.zeros((IN, 7), F32)], axis=1)
    side_high = side.astype(BF16).astype(F32)
    wlow[...] = jnp.concatenate([side_high, side_high, side - side_high], axis=1).astype(BF16)

    def last_slot(s, carry):
        main = nn(grown_both, hh[s, 0:EXP, :])
        main = main[:IN] + main[IN:] + nn(grown_high, hh[s, EXP:, :]) + nn(wlow[...], xs[s])
        for n in range(WIDE):
            xq[tile_quad(n), s, pl.ds(n % 3, IN, stride=3), :] = (
                c_tile(s, n) + main[:, n * LANES : (n + 1) * LANES]
            )
        for step in range(1, QUADS):
            g_copy(step, s).start()
        return carry

    lax.fori_loop(0, slots, last_slot, 0)
    own_g = pltpu.make_async_copy(xq.at[space], ing.at[pl.ds(slots * space, slots)], own_sem.at[3])
    own_g.start()

    mine = jnp.minimum(place, 4)
    grad = gs_out[mine]
    turned = (mine == 1) | (mine == 2)
    small[...] = jnp.zeros(small.shape, F32)
    small[0, :, :IN] = in_st[0]
    small[1, :, :IN] = jnp.transpose(in_st[1])
    small[2, :SQZ, :SQZ] = jnp.transpose(sq_st[0])
    small[3, :SQZ, :SQZ] = sq_st[1]
    small[4, :TAPS, :TAPS] = tap_st[...]
    old_big = big[mine]
    old_big = jnp.where(turned, jnp.transpose(old_big), old_big)
    big_m = DECAY * old_big + FRESH * tn(grad, grad, FULL)
    small_m = DECAY * small[mine][:, :IN] + FRESH * nt(grad, grad, FULL)
    big_eye = (
        lax.broadcasted_iota(jnp.int32, (EXP, EXP), 0) == lax.broadcasted_iota(jnp.int32, (EXP, EXP), 1)
    ).astype(F32)
    small_eye = eye24.astype(F32)
    big_c = 2.5 * lax.rsqrt(jnp.sum(jnp.sum(big_m * big_m, axis=0, keepdims=True), axis=1, keepdims=True))
    small_c = 2.5 * lax.rsqrt(jnp.sum(jnp.sum(small_m * small_m, axis=0, keepdims=True), axis=1, keepdims=True))
    big_m = big_c * big_m
    small_m = small_c * small_m
    direction = jnp.sqrt(jnp.sqrt(big_c)) * grad
    small_h = jnp.sqrt(jnp.sqrt(small_c)) * small_eye

    def root_step(i, carry):
        big_m, small_m, direction, small_h = carry
        big_k = 1.25 * big_eye - 0.25 * big_m
        small_k = 1.25 * small_eye - 0.25 * small_m
        direction = nn(direction, big_k, FULL)
        small_h = nn(small_h, small_k, FULL)
        big_k = nn(big_k, big_k, FULL)
        small_k = nn(small_k, small_k, FULL)
        big_k = nn(big_k, big_k, FULL)
        small_k = nn(small_k, small_k, FULL)
        return nn(big_k, big_m, FULL), nn(small_k, small_m, FULL), direction, small_h

    _, _, direction, small_h = lax.fori_loop(
        0, ROOT_ITERS, root_step, (big_m, small_m, direction, small_h)
    )
    direction = nn(small_h, direction, FULL)
    short = jnp.where(mine < 2, float(IN), jnp.where(mine == 4, float(TAPS), float(SQZ)))
    lead = jnp.where(turned, float(EXP), short)
    power = jnp.sum(jnp.sum(direction * direction, axis=0, keepdims=True), axis=1, keepdims=True)
    power = power / jnp.full((1, 1), short * float(EXP), F32)
    step_size = STEP_FRACTION * lax.rsqrt(jnp.full((1, 1), lead, F32)) * lax.rsqrt(power + 1e-06)
    small[0] = weight
    small[1] = w_pro_t[...]
    for i, source in ((2, w_red_t), (3, w_exc), (4, w_dep)):
        small[i] = jnp.zeros((IN, EXP), F32)
        small[i, : source.shape[0], :] = source[...]
    nws[place] = small[mine] - step_size * direction
    for step in range(1, GROUP):
        group_copy(nws.at[place], nws.at[place], 6, step).start()
    done = group_copy(nws.at[pl.ds(0, GROUP - 1)], nws.at[pl.ds(0, GROUP - 1)], 6, 1)
    done.wait_send()
    done.wait_recv()
    nw_out[...] = nws[0:5]

    for step in range(1, QUADS):
        def all_done(s, carry, step=step):
            o_copy(step, s).wait_recv()
            g_copy(step, s).wait()
            return carry

        lax.fori_loop(0, slots, all_done, 0)
    own_o.wait()
    own_g.wait()


def finish_kernel(
    gs, nw, big, in_st, sq_st, tap_st,
    ge, gd, gr_t, gx, gp_t, ne, nd, nr_t, nx, np_t, big_new, in_new, sq_new, tap_new,
):
    ge[...], gp_t[...], gr_t[...], gx[...], gd[...] = gs[0], gs[1], gs[2, :SQZ], gs[3, :SQZ], gs[4, :TAPS]
    ne[...], np_t[...], nr_t[...], nx[...], nd[...] = nw[0], nw[1], nw[2, :SQZ], nw[3, :SQZ], nw[4, :TAPS]
    for i in range(5):
        grad = gs[i]
        big_new[i] = DECAY * big[i] + FRESH * tn(grad, grad, FULL)
        inner = FRESH * nt(grad, grad, FULL)
        if i < 2:
            in_new[i] = DECAY * in_st[i] + inner
        elif i < 4:
            sq_new[i - 2] = DECAY * sq_st[i - 2] + inner[:SQZ, :SQZ]
        else:
            tap_new[...] = DECAY * tap_st[...] + inner[:TAPS, :TAPS]


def on_device(
    n_dev, n_space,
    features, cotangent, segment_ids, w_expand, w_depth, w_reduce, w_excite, w_project,
    vector_params, vector_moments, big_stats, in_stats, sq_stats, tap_stats,
):
    slot_count = features.shape[0]
    slots = slot_count // QUADS
    n_pos = slot_count * (n_dev // n_space) * FRAMES * BINS
    cuts = [0, EXP, 2 * EXP, 3 * EXP, 4 * EXP, 4 * EXP + IN, 4 * EXP + 2 * IN, 4 * EXP + 2 * IN + SQZ]
    cuts.append(cuts[-1] + EXP)
    pieces = [vector_params[a:b] for a, b in zip(cuts[:-1], cuts[1:])]
    prm = jnp.stack([jnp.pad(piece, (0, EXP - piece.shape[0])) for piece in pieces])
    vm = pl.BlockSpec(memory_space=pltpu.VMEM)
    hbm = pl.BlockSpec(memory_space=pl.ANY)
    grid_shape = jax.ShapeDtypeStruct((slot_count, ROWS, LANES), F32)
    wide = WIDE * LANES
    vmem = pltpu.VMEM
    dma = pltpu.SemaphoreType.DMA
    out, ing, gs, nw, vr = pl.pallas_call(
        functools.partial(block_kernel, n_dev, n_space, slots, n_pos),
        out_shape=(
            grid_shape,
            grid_shape,
            jax.ShapeDtypeStruct((5, IN, EXP), F32),
            jax.ShapeDtypeStruct((5, IN, EXP), F32),
            jax.ShapeDtypeStruct((8, EXP), F32),
        ),
        in_specs=[hbm, hbm] + [vm] * 11,
        out_specs=(hbm, hbm, vm, vm, vm),
        scratch_shapes=[
            vmem((QUADS, slots, ROWS, LANES), F32),
            vmem((QUADS, slots, ROWS, LANES), F32),
            vmem((QUADS, slots, ROWS, LANES), F32),
            vmem((slots, 96, wide), BF16),
            vmem((slots, EXP, wide), F32),
            vmem((slots, EXP, wide), F32),
            vmem((slots, 2 * EXP, wide), BF16),
            vmem((slots, EXP, wide), F32),
            vmem((EXP, wide), F32),
            vmem((slots, IN, wide), F32),
            vmem((slots, slots * REGIONS, wide), BF16),
            vmem((slots, 256, wide), BF16),
            vmem((TAPS + 3, EXP, LANES), F32),
            vmem((2, slots, 8, HALF_W * LANES), F32),
            vmem((REGIONS, slots, 8, HALF_W * LANES), F32),
            vmem((TAPS, EXP, LANES), F32),
            vmem((EXP, 96), BF16),
            vmem((IN, 96), BF16),
            vmem((5, IN, EXP), F32),
            vmem((slots * REGIONS, EXP), F32),
            vmem((slots, REGIONS, EXP), F32),
            vmem((slots, REGIONS, EXP), F32),
            vmem((BULK, 8, LANES), F32),
            vmem((GROUP, BULK // GROUP, 8, LANES), F32),
            vmem((n_dev, BULK // GROUP, 8, LANES), F32),
            vmem((n_dev, 8, LANES), F32),
            vmem((3, n_dev, 4, LANES), F32),
            vmem((GROUP, IN, EXP), F32),
            vmem((IN, LANES), F32),
            dma((QUADS,)),
        ]
        + [dma((QUADS, slots))] * 8
        + [dma((8,)), dma((8,)), dma((4,))],
        compiler_params=pltpu.CompilerParams(
            collective_id=0, has_side_effects=True, vmem_limit_bytes=60 << 20
        ),
    )(
        features.reshape(slot_count, ROWS, LANES),
        cotangent.reshape(slot_count, ROWS, LANES),
        segment_ids, w_expand, w_depth, w_reduce.T, w_excite, w_project.T, prm,
        big_stats, in_stats, sq_stats, tap_stats,
    )
    shape = jax.ShapeDtypeStruct
    ge, gd, gr_t, gx, gp_t, ne, nd, nr_t, nx, np_t, big_new, in_new, sq_new, tap_new = pl.pallas_call(
        finish_kernel,
        out_shape=tuple(
            shape(dims, F32)
            for dims in [(IN, EXP), (TAPS, EXP), (SQZ, EXP), (SQZ, EXP), (IN, EXP)] * 2
            + [(5, EXP, EXP), (2, IN, IN), (2, SQZ, SQZ), (TAPS, TAPS)]
        ),
        in_specs=[vm] * 6,
        out_specs=(vm,) * 14,
    )(gs, nw, big_stats, in_stats, sq_stats, tap_stats)
    vector_grads = jnp.concatenate([vr[i, : cuts[i + 1] - cuts[i]] for i in range(8)])
    moments_new = DECAY * vector_moments + FRESH * vector_grads * vector_grads
    vector_new = vector_params - VECTOR_RATE * vector_grads / (jnp.sqrt(moments_new) + 1e-08)
    return (
        out.reshape(features.shape), ing.reshape(features.shape),
        ge, gd, gr_t.T, gx, gp_t.T, ne, nd, nr_t.T, nx, np_t.T,
        big_new, in_new, sq_new, tap_new, vector_grads, moments_new, vector_new,
    )


def solution(mesh):
    field = P("dp", None, "space", None)
    return jax.shard_map(
        functools.partial(on_device, mesh.shape["dp"] * mesh.shape["space"], mesh.shape["space"]),
        mesh=mesh,
        in_specs=(field, field, P("dp", None)) + (P(),) * 11,
        out_specs=(field, field) + (P(),) * 17,
        check_vma=False,
    )
```

```python
import functools
import math

import jax
import jax.numpy as jnp
from jax import lax
from jax.experimental import pallas as pl
from jax.experimental.pallas import tpu as pltpu
from jax.sharding import PartitionSpec as P

IN = 24
EXP = 144
SQZ = 6
TAPS = 9
FRAMES = 96
BINS = 16
REGIONS = 4
QUADS = 4
ROOT_ITERS = 10
NORM_EPS = 0.001
DECAY = 0.9
FRESH = 1.0 - DECAY
STEP_FRACTION = 0.5
VECTOR_RATE = 0.15
PARTS = (EXP, EXP, EXP, EXP, IN, IN, SQZ, EXP)

LANES = 128
HALF_W = 6
WIDE = 2 * HALF_W
ROWS = IN * 3
GROUP = 8
BULK = 16

F32 = jnp.float32
BF16 = jnp.bfloat16
FULL = lax.Precision.HIGHEST
MID = lax.Precision.HIGH
MESH = pl.DeviceIdType.MESH


def mm(left, right, dims, precision=None):
    return lax.dot_general(
        left, right, ((dims[:1], dims[1:]), ((), ())), precision=precision, preferred_element_type=F32
    )


def nn(left, right, precision=None):
    return mm(left, right, (1, 0), precision)


def nt(left, right, precision=None):
    return mm(left, right, (1, 1), precision)


def tn(left, right, precision=None):
    return mm(left, right, (0, 0), precision)


def halves(value):
    high = value.astype(BF16)
    return high, (value - high.astype(F32)).astype(BF16)


def column(rows, index, width):
    pick = (lax.broadcasted_iota(jnp.int32, (rows.shape[0], LANES), 0) == index).astype(F32)
    return tn(rows, pick, FULL)[:width]


def lane_sums(table):
    return nt(jnp.ones((8, table.shape[1]), F32), table, FULL)[0:1]


def split_row(row):
    return jnp.concatenate(
        [row[:, :LANES], jnp.concatenate([row[:, LANES:], jnp.zeros((1, 2 * LANES - EXP), F32)], axis=1)], axis=0
    )


def join_row(pair):
    return jnp.concatenate([pair[0:1], pair[1:2, : EXP - LANES]], axis=1)


def tile_quad(n):
    return 2 * ((n % HALF_W) // 3) + n // HALF_W


def on_lane(n):
    return pl.ds(n * LANES, LANES)


def block_kernel(
    n_dev, n_space, slots, n_pos,
    feat, cot, ids_ref, w_exp, w_dep, w_red_t, w_exc, w_pro_t, vec, big, in_st, sq_st, tap_st,
    out, ing, gs_out, nw_out, vr_out,
    xloc, xq, cq, xs, x3, c3, v1, a2, hh, dn2, dh, dm, dp, a3, hot, dcat, tab, msk, reg, acc, w1t, wlow, prm,
    small, pooled, gates, dgate, bulk, bulk_in, bulk_all, rb1, rb, nws, fold,
    loc_sem, x_send, x_recv, c_send, c_recv, o_send, o_recv, g_send, g_recv,
    r_send, r_recv, own_sem,
):
    space = lax.axis_index("space")
    me = lax.axis_index("dp") * n_space + space
    n_loc = float(slots * FRAMES * BINS)
    total = float(n_pos)

    def device(index):
        return (lax.div(index, n_space), lax.rem(index, n_space))

    def peer(step):
        return lax.rem(space + step, QUADS)

    def space_device(step):
        return (lax.axis_index("dp"), peer(step))

    barrier = pltpu.get_barrier_semaphore()

    def greet(step, carry):
        pl.semaphore_signal(
            barrier, inc=1, device_id=device(lax.rem(me + step, n_dev)), device_id_type=MESH
        )
        return carry

    lax.fori_loop(1, n_dev, greet, 0)
    loads = [
        pltpu.make_async_copy(feat.at[pl.ds(slots * q, slots)], xloc.at[q], loc_sem.at[q]) for q in range(QUADS)
    ]
    for load in loads:
        load.start()
    own_x = pltpu.make_async_copy(feat.at[pl.ds(slots * space, slots)], xq.at[space], own_sem.at[0])
    own_c = pltpu.make_async_copy(cot.at[pl.ds(slots * space, slots)], cq.at[space], own_sem.at[1])
    own_x.start()
    own_c.start()

    for load in loads:
        load.wait()
    first = jnp.concatenate([xloc[0, 0, pl.ds(k, IN, stride=3), :] for k in range(3)], axis=1)
    shift_col = nn(first, jnp.ones((3 * LANES, LANES), F32), FULL) * (1.0 / (3 * LANES))
    shift_row = nt(jnp.ones((8, 3 * LANES), F32), first, FULL)[0:1] * (1.0 / (3 * LANES))
    one_rows = (lax.broadcasted_iota(jnp.int32, (8, LANES), 0) == 0).astype(F32)

    def gram_step(s, gram):
        parts = []
        for q in range(QUADS):
            for k in range(3):
                parts.append(
                    jnp.concatenate([xloc[q, s, pl.ds(k, IN, stride=3), :] - shift_col, one_rows], axis=0)
                )
        high, low = halves(jnp.concatenate(parts, axis=1))
        both = jnp.concatenate([high, low], axis=0)
        return gram + nt(both, both)

    gram = lax.fori_loop(0, slots, gram_step, jnp.zeros((64, 64), F32))
    gram = gram[:32, :32] + gram[32:, :32] + gram[:32, 32:] + gram[32:, 32:]
    off_row = gram[IN : IN + 1, :IN] * (1.0 / n_loc)
    off_col = gram[:IN, IN : IN + 1] * (1.0 / n_loc)
    local_m2 = gram[:IN, :IN] - n_loc * off_col * off_row
    fold[...] = jnp.zeros((IN, LANES), F32)
    fold[:, :IN] = local_m2
    packed = jnp.zeros((6, LANES), F32)
    for g in range(4):
        piece = fold[pl.ds(g, 6, stride=4), :]
        packed = packed + (pltpu.roll(piece, 32 * g, 1) if g else piece)
    rb1[me, 0:6, :] = packed
    rb1[me, 6:7, :] = jnp.concatenate([shift_row + off_row, jnp.zeros((1, LANES - IN), F32)], axis=1)
    rb1[me, 7:8, :] = jnp.zeros((1, LANES), F32)

    pl.semaphore_wait(barrier, n_dev - 1)

    def spread_start(source, target, index):
        def send(step, carry):
            pltpu.make_async_remote_copy(
                src_ref=source, dst_ref=target, send_sem=r_send.at[index], recv_sem=r_recv.at[index],
                device_id=device(lax.rem(me + step, n_dev)), device_id_type=MESH,
            ).start()
            return carry

        lax.fori_loop(1, n_dev, send, 0)

    def spread_wait(window, index):
        done = pltpu.make_async_remote_copy(
            src_ref=window, dst_ref=window, send_sem=r_send.at[index], recv_sem=r_recv.at[index],
            device_id=device(me), device_id_type=MESH,
        )
        done.wait_send()
        done.wait_recv()

    def quad_copy(source, target, send, recv, step, s):
        return pltpu.make_async_remote_copy(
            src_ref=source, dst_ref=target, send_sem=send.at[step, s], recv_sem=recv.at[step, s],
            device_id=space_device(step), device_id_type=MESH,
        )

    def x_copy(step, s):
        return quad_copy(feat.at[slots * peer(step) + s], xq.at[space, s], x_send, x_recv, step, s)

    def c_copy(step, s):
        return quad_copy(cot.at[slots * peer(step) + s], cq.at[space, s], c_send, c_recv, step, s)

    def o_copy(step, s):
        return quad_copy(xloc.at[peer(step), s], out.at[slots * space + s], o_send, o_recv, step, s)

    def g_copy(step, s):
        return quad_copy(xq.at[peer(step), s], ing.at[slots * space + s], g_send, g_recv, step, s)

    spread_start(rb1.at[me], rb1.at[me], 0)

    def x_start(s, carry):
        for step in range(1, QUADS):
            x_copy(step, s).start()
        return carry

    lax.fori_loop(0, slots, x_start, 0)

    lane = lax.broadcasted_iota(jnp.int32, (8, LANES), 1)
    low_bin = lax.rem(lane, 8) == 0
    high_bin = lax.rem(lane, 8) == 7
    first_row = lane < 8
    second_row = (lane >= 8) & (lane < 16)
    last_row = lane >= LANES - 8
    zero_tile = jnp.zeros((8, LANES), F32)

    half_lanes = HALF_W * LANES
    own_ids = ids_ref[pl.ds(pl.multiple_of(slots * space, 8), slots), :].astype(F32)
    spread = (
        lax.broadcasted_iota(jnp.int32, (FRAMES, half_lanes), 1) // 8
        == lax.broadcasted_iota(jnp.int32, (FRAMES, half_lanes), 0)
    )
    wide_ids = nn(own_ids.astype(BF16), spread.astype(F32).astype(BF16))
    wide_lane = lax.broadcasted_iota(jnp.int32, (slots, half_lanes), 1)
    before = pltpu.roll(wide_ids, 8, 1)
    after = pltpu.roll(wide_ids, half_lanes - 8, 1)
    from_ok = jnp.where((before == wide_ids) & (wide_lane >= 8), 1.0, 0.0)
    to_ok = jnp.where((after == wide_ids) & (wide_lane < half_lanes - 8), 1.0, 0.0)
    def both_halves(rows):
        turned = [pltpu.roll(rows[:, n * LANES : (n + 1) * LANES], 8, 1) for n in range(HALF_W)]
        return jnp.concatenate([rows] + turned, axis=1)

    marks = [both_halves(rows) for rows in (from_ok, to_ok)]
    regions = [both_halves((wide_ids == float(r)).astype(F32)) for r in range(REGIONS)]
    for s in range(slots):
        for i in range(2):
            msk[i, s] = jnp.broadcast_to(marks[i][s : s + 1], (8, WIDE * LANES))
        for r in range(REGIONS):
            reg[r, s] = jnp.broadcast_to(regions[r][s : s + 1], (8, WIDE * LANES))
    row_index = lax.broadcasted_iota(jnp.int32, (slots * REGIONS, WIDE * LANES), 0)
    counts = jnp.zeros((slots * REGIONS, 1), F32)
    for s in range(slots):
        row = jnp.zeros((slots * REGIONS, WIDE * LANES), F32)
        for r in range(REGIONS):
            row = jnp.where(row_index == REGIONS * s + r, regions[r][s : s + 1], row)
        counts = counts + jnp.sum(row, axis=1, keepdims=True)
        hot[s] = row.astype(BF16)
    taps = w_dep[...]
    for t in range(TAPS):
        tab[t] = column(taps, t, EXP)

    start = 0
    prm[...] = jnp.zeros((8, EXP), F32)
    for i, width in enumerate(PARTS):
        prm[i : i + 1, :width] = vec[:, start : start + width]
        start = start + width

    spread_wait(rb1.at[pl.ds(0, n_dev - 1)], 0)
    gathered = jnp.sum(rb1[...], axis=0)
    means = rb1[:, 6, :]
    mean_row = jnp.sum(means, axis=0, keepdims=True) * (1.0 / n_dev)
    apart = means - mean_row
    between = tn(apart, apart, FULL)[:IN, :IN]
    for g in range(4):
        piece = gathered[0:6]
        piece = pltpu.roll(piece, LANES - 32 * g, 1) if g else piece
        fold[pl.ds(g, 6, stride=4), :] = piece
    moment = fold[:, :IN] + n_loc * between
    eye24 = (
        lax.broadcasted_iota(jnp.int32, (IN, IN), 0) == lax.broadcasted_iota(jnp.int32, (IN, IN), 1)
    )
    mean_col = nn(jnp.where(eye24, mean_row[:, :IN], 0.0), jnp.ones((IN, LANES), F32), FULL)
    weight = w_exp[...]
    moment_w = nn(moment, weight, FULL)
    scale1 = lax.rsqrt(jnp.sum(moment_w * weight, axis=0, keepdims=True) * (1.0 / total) + NORM_EPS)
    grow1 = prm[0:1, :] * scale1
    shaped = jnp.concatenate(
        [weight * (0.5 * grow1), 0.5 * prm[1:2, :], jnp.zeros((7, EXP), F32)], axis=0
    )
    shaped_high = shaped.astype(BF16).astype(F32)
    w1t[...] = jnp.transpose(
        jnp.concatenate([shaped_high, shaped_high, shaped - shaped_high], axis=0)
    ).astype(BF16)

    own_x.wait()
    acc[0] = jnp.zeros((EXP, LANES), F32)

    def fetch(quads, s, n):
        tile = quads[tile_quad(n), s, pl.ds(n % 3, IN, stride=3), :]
        return tile if n < HALF_W else pltpu.roll(tile, 8, 1)

    def place_back(quads, s, n, tile):
        tile = tile if n < HALF_W else pltpu.roll(tile, LANES - 8, 1)
        quads[tile_quad(n), s, pl.ds(n % 3, IN, stride=3), :] = tile

    def later_bin(low, high):
        return (
            pltpu.roll(jnp.where(low_bin, high, low), LANES - 1, 1),
            jnp.where(high_bin, 0.0, pltpu.roll(high, LANES - 1, 1)),
        )

    def earlier_bin(low, high):
        return (
            jnp.where(low_bin, 0.0, pltpu.roll(low, 1, 1)),
            pltpu.roll(jnp.where(high_bin, low, high), 1, 1),
        )

    def from_before(tiles, k, half):
        edge = first_row if half else last_row
        return pltpu.roll(jnp.where(edge, tiles[(k - 1) % HALF_W], tiles[k]), 8, 1)

    def from_after(tiles, k, half):
        edge = second_row if half else first_row
        return pltpu.roll(jnp.where(edge, tiles[(k + 1) % HALF_W], tiles[k]), LANES - 8, 1)

    def forward_slot(s, carry):
        for step in range(1, QUADS):
            x_copy(step, s).wait_recv()
        for n in range(WIDE):
            tile = fetch(xq, s, n)
            x3[s, :, on_lane(n)] = tile
            high, low = halves(jnp.concatenate([tile - mean_col, one_rows], axis=0))
            xs[s, 0:32, on_lane(n)] = high
            xs[s, 32:64, on_lane(n)] = low
            xs[s, 64:96, on_lane(n)] = high
        for step in range(1, QUADS):
            c_copy(step, s).start()
        v1[s] = nn(w1t[...], xs[s])

        def bins_step(j, carry):
            rows = pl.ds(pl.multiple_of(8 * j, 8), 8)
            wt = [tab[t, rows, :] for t in range(TAPS)]
            for k in range(HALF_W):
                pair = []
                for half in range(2):
                    v = v1[s, rows, on_lane(half * HALF_W + k)]
                    pair.append(v + v * jnp.tanh(v))
                nxt = later_bin(*pair)
                prv = earlier_bin(*pair)
                for half in range(2):
                    for p, target in enumerate((dm, dh, dp)):
                        target[rows, on_lane(half * HALF_W + k)] = (
                            wt[3 * p] * prv[half] + wt[3 * p + 1] * pair[half] + wt[3 * p + 2] * nxt[half]
                        )
            return carry

        def frames_step(j, carry):
            rows = pl.ds(pl.multiple_of(8 * j, 8), 8)
            got = zero_tile
            for half in range(2):
                prior = [dm[rows, on_lane(half * HALF_W + k)] for k in range(HALF_W)]
                later = [dp[rows, on_lane(half * HALF_W + k)] for k in range(HALF_W)]
                for k in range(HALF_W):
                    where = on_lane(half * HALF_W + k)
                    value = (
                        dh[rows, where]
                        + msk[0, s, :, where] * from_before(prior, k, half)
                        + msk[1, s, :, where] * from_after(later, k, half)
                    )
                    a2[s, rows, where] = value
                    got = got + value
            acc[0, rows, :] = acc[0, rows, :] + got
            return carry

        lax.fori_loop(0, EXP // 8, bins_step, 0, unroll=9)
        lax.fori_loop(0, EXP // 8, frames_step, 0, unroll=9)
        return carry

    lax.fori_loop(0, slots, forward_slot, 0)

    acc[1] = nn(acc[0], jnp.ones((LANES, LANES), F32), FULL) * (1.0 / n_loc)
    acc[2] = jnp.zeros((EXP, LANES), F32)

    def square_step(s, carry):
        def tile_step(j, carry):
            rows = pl.ds(pl.multiple_of(8 * j, 8), 8)
            center = acc[1, rows, :]
            got = zero_tile
            for n in range(WIDE):
                off = a2[s, rows, on_lane(n)] - center
                got = got + off * off
            acc[2, rows, :] = acc[2, rows, :] + got
            return carry

        return lax.fori_loop(0, EXP // 8, tile_step, carry, unroll=3)

    lax.fori_loop(0, slots, square_step, 0)
    rb[0, me, 0:2, :] = split_row(lane_sums(acc[0]) * (1.0 / n_loc))
    rb[0, me, 2:4, :] = split_row(lane_sums(acc[2]))
    spread_start(rb.at[0, me], rb.at[0, me], 1)
    spread_wait(rb.at[0, pl.ds(0, n_dev - 1)], 1)
    sums = jnp.sum(rb[0], axis=0)
    mean2 = sums[0:2] * (1.0 / n_dev)
    gaps = rb[0][:, 0:2, :] - mean2[None]
    spread2 = sums[2:4] + n_loc * jnp.sum(gaps * gaps, axis=0)
    scale2 = lax.rsqrt(join_row(spread2) * (1.0 / total) + NORM_EPS)
    mean2 = join_row(mean2)
    rows8 = jnp.concatenate(
        [mean2, 0.5 * prm[2:3, :] * scale2, 0.5 * prm[3:4, :], jnp.zeros((5, EXP), F32)], axis=0
    )
    for i in range(3):
        tab[TAPS + i] = column(rows8, i, EXP)

    pooled[...] = jnp.zeros((slots * REGIONS, EXP), F32)

    def activate_slot(s, carry):
        def step(j, carry):
            rows = pl.ds(pl.multiple_of(16 * j, 16), 16)
            low_rows = pl.ds(pl.multiple_of(EXP + 16 * j, 16), 16)
            center, grow, lift = (tab[TAPS + i, rows, :] for i in range(3))
            for n in range(WIDE):
                off = a2[s, rows, on_lane(n)] - center
                a2[s, rows, on_lane(n)] = off
                v = off * grow + lift
                high, low = halves(v + v * jnp.tanh(v))
                hh[s, rows, on_lane(n)] = high
                hh[s, low_rows, on_lane(n)] = low
            return carry

        lax.fori_loop(0, EXP // 16, step, 0, unroll=3)
        pooled[...] = pooled[...] + nt(hot[s], hh[s, 0:EXP, :]) + nt(hot[s], hh[s, EXP:, :])
        return carry

    lax.fori_loop(0, slots, activate_slot, 0)

    per_count = 1.0 / counts
    mean_pool = pooled[...] * per_count
    squeeze = nt(mean_pool, w_red_t[...], FULL) + prm[6:7, :SQZ]
    squeeze_sig = jax.nn.sigmoid(squeeze)
    squeezed = squeeze * squeeze_sig
    gate = jax.nn.sigmoid(nn(squeezed, w_exc[...], FULL) + prm[7:8, :])
    for s in range(slots):
        gates[s] = gate[REGIONS * s : REGIONS * (s + 1)]

    def gated_weights(s):
        project = w_pro_t[...]
        rows = gates[s]
        return jnp.concatenate([project * rows[r : r + 1] for r in range(REGIONS)], axis=0)

    def region_tile(r, s, n):
        return jnp.concatenate([reg[r, s, :, on_lane(n)]] * (IN // 8), axis=0)

    def project_slot(s, carry):
        total_a, total_c = carry
        high, low = halves(gated_weights(s))
        body = nn(jnp.concatenate([high, low], axis=0), hh[s, 0:EXP, :])
        body = body[:96] + body[96:] + nn(high, hh[s, EXP:, :])
        for step in range(1, QUADS):
            c_copy(step, s).wait_recv()
        for n in range(WIDE):
            value = jnp.zeros((IN, LANES), F32)
            for r in range(REGIONS):
                value = value + (
                    body[IN * r : IN * (r + 1), n * LANES : (n + 1) * LANES]
                    * region_tile(r, s, n)
                )
            a3[s, :, on_lane(n)] = value
            total_a = total_a + value
            upstream = fetch(cq, s, n)
            c3[s, :, on_lane(n)] = upstream
            total_c = total_c + upstream
        return total_a, total_c

    own_c.wait()
    zero24 = jnp.zeros((IN, LANES), F32)
    total_a, total_c = lax.fori_loop(0, slots, project_slot, (zero24, zero24))
    center3 = nn(total_a, jnp.ones((LANES, LANES), F32), FULL) * (1.0 / n_loc)

    def third_step(s, carry):
        square, cross = carry
        for n in range(WIDE):
            off = a3[s, :, on_lane(n)] - center3
            square = square + off * off
            cross = cross + off * c3[s, :, on_lane(n)]
        return square, cross

    square3, cross3 = lax.fori_loop(0, slots, third_step, (zero24, zero24))

    def pad_row(row):
        return jnp.concatenate([row, jnp.zeros((1, LANES - IN), F32)], axis=1)

    rb[1, me] = jnp.concatenate(
        [
            pad_row(lane_sums(total_a) * (1.0 / n_loc)),
            pad_row(lane_sums(square3)),
            pad_row(lane_sums(total_c)),
            pad_row(lane_sums(cross3)),
        ],
        axis=0,
    )
    spread_start(rb.at[1, me], rb.at[1, me], 2)
    spread_wait(rb.at[1, pl.ds(0, n_dev - 1)], 2)
    third = rb[1]
    sums = jnp.sum(third, axis=0)
    mean3 = sums[0:1] * (1.0 / n_dev)
    gaps = third[:, 0, :] - mean3
    spread3 = sums[1:2] + n_loc * jnp.sum(gaps * gaps, axis=0, keepdims=True)
    scale3 = lax.rsqrt(spread3 * (1.0 / total) + NORM_EPS)
    bias3_grad = sums[2:3]
    cross_sum = sums[3:4] + jnp.sum(third[:, 2, :] * gaps, axis=0, keepdims=True)
    gain3_grad = scale3 * cross_sum
    grow3 = prm[4:5, :LANES] * scale3
    rows8 = jnp.concatenate(
        [
            mean3,
            grow3,
            prm[5:6, :LANES],
            grow3 * bias3_grad * (1.0 / total),
            grow3 * scale3 * gain3_grad * (1.0 / total),
            jnp.zeros((3, LANES), F32),
        ],
        axis=0,
    )
    mean3_c, grow3_c, lift3_c, flat3_c, lean3_c = (column(rows8, i, IN) for i in range(5))

    small[0] = jnp.zeros((IN, EXP), F32)

    def back_slot(s, carry):
        for n in range(WIDE):
            off = a3[s, :, on_lane(n)] - mean3_c
            place_back(xloc, s, n, x3[s, :, on_lane(n)] + off * grow3_c + lift3_c)
            grad = grow3_c * c3[s, :, on_lane(n)] - flat3_c - off * lean3_c
            high, low = halves(
                jnp.concatenate(
                    [grad * region_tile(r, s, n) for r in range(REGIONS)], axis=0
                )
            )
            dcat[s, 0:96, on_lane(n)] = high
            dcat[s, 128:224, on_lane(n)] = low
        dcat[s, 96:128, :] = hot[s]
        dcat[s, 224:256, :] = hot[s]
        for step in range(1, QUADS):
            o_copy(step, s).start()
        main = nt(dcat[s, 0:224, :], hh[s, 0:EXP, :])
        main = main[0:96] + main[128:224] + nt(dcat[s, 0:96, :], hh[s, EXP:, :])
        project = w_pro_t[...]
        gp = small[0]
        rows = gates[s]
        for r in range(REGIONS):
            part = main[IN * r : IN * (r + 1)]
            dgate[s, r : r + 1, :] = jnp.sum(part * project, axis=0, keepdims=True)
            gp = gp + part * rows[r : r + 1]
        small[0] = gp
        return carry

    lax.fori_loop(0, slots, back_slot, 0)
    own_o = pltpu.make_async_copy(xloc.at[space], out.at[pl.ds(slots * space, slots)], own_sem.at[2])
    own_o.start()

    dgate_rows = jnp.concatenate([dgate[s] for s in range(slots)], axis=0)
    dpre_x = dgate_rows * gate * (1.0 - gate)
    excite_grad = tn(squeezed, dpre_x, FULL)
    excite_bias_grad = jnp.sum(dpre_x, axis=0, keepdims=True)
    dsqueezed = nt(dpre_x, w_exc[...], FULL)
    dpre_r = dsqueezed * squeeze_sig * (1.0 + squeeze * (1.0 - squeeze_sig))
    reduce_grad = tn(dpre_r, mean_pool, FULL)
    reduce_bias_grad = jnp.sum(dpre_r, axis=0, keepdims=True)
    dpool = nn(dpre_r, w_red_t[...], FULL) * per_count
    pooled[...] = 0.5 * dpool

    acc[0] = jnp.zeros((EXP, LANES), F32)
    acc[1] = jnp.zeros((EXP, LANES), F32)

    def second_back_slot(s, carry):
        high, low = halves(0.5 * gated_weights(s))
        pool_high, pool_low = halves(pooled[...])
        left = jnp.concatenate([high, pool_high, high, pool_low], axis=0)
        dh[...] = tn(left, dcat[s]) + tn(low, dcat[s, 0:96, :])

        def step(j, carry):
            rows = pl.ds(pl.multiple_of(8 * j, 8), 8)
            grow, lift = (tab[TAPS + i, rows, :] for i in (1, 2))
            plain, cross = zero_tile, zero_tile
            for n in range(WIDE):
                off = a2[s, rows, on_lane(n)]
                v = off * grow + lift
                u = 1.0 + jnp.tanh(v)
                d = dh[rows, on_lane(n)] * (u + (v * u) * (2.0 - u))
                dn2[s, rows, on_lane(n)] = d
                plain = plain + d
                cross = cross + d * off
            acc[0, rows, :] = acc[0, rows, :] + plain
            acc[1, rows, :] = acc[1, rows, :] + cross
            return carry

        lax.fori_loop(0, EXP // 8, step, 0, unroll=6)
        return carry

    lax.fori_loop(0, slots, second_back_slot, 0)
    rb[2, me, 0:2, :] = split_row(lane_sums(acc[0]))
    rb[2, me, 2:4, :] = split_row(lane_sums(acc[1]))
    spread_start(rb.at[2, me], rb.at[2, me], 3)
    spread_wait(rb.at[2, pl.ds(0, n_dev - 1)], 3)
    sums = jnp.sum(rb[2], axis=0)
    bias2_grad = join_row(sums[0:2])
    cross2 = join_row(sums[2:4])
    gain2_grad = cross2 * scale2
    grow2 = prm[2:3, :] * scale2
    rows8 = jnp.concatenate(
        [
            grow2,
            -grow2 * scale2 * gain2_grad * (1.0 / total),
            -grow2 * bias2_grad * (1.0 / total),
            jnp.zeros((5, EXP), F32),
        ],
        axis=0,
    )
    for i in range(3):
        tab[TAPS + i] = column(rows8, i, EXP)

    for t in range(TAPS):
        acc[t] = jnp.zeros((EXP, LANES), F32)
    small[1] = jnp.zeros((IN, EXP), F32)
    small[2] = jnp.zeros((IN, EXP), F32)

    def taps_back_slot(s, carry):
        def frames_step(j, carry):
            rows = pl.ds(pl.multiple_of(8 * j, 8), 8)
            k1, k2, k3 = (tab[TAPS + i, rows, :] for i in range(3))
            for half in range(2):
                grads = []
                for k in range(HALF_W):
                    where = on_lane(half * HALF_W + k)
                    grads.append(k1 * dn2[s, rows, where] + k2 * a2[s, rows, where] + k3)
                for k in range(HALF_W):
                    where = on_lane(half * HALF_W + k)
                    dn2[s, rows, where] = grads[k]
                    dm[rows, where] = msk[1, s, :, where] * from_after(grads, k, half)
                    dp[rows, where] = msk[0, s, :, where] * from_before(grads, k, half)
            return carry

        def bins_step(j, carry):
            rows = pl.ds(pl.multiple_of(8 * j, 8), 8)
            wt = [tab[t, rows, :] for t in range(TAPS)]
            for k in range(HALF_W):
                mix = [[], [], []]
                us, hs = [], []
                for half in range(2):
                    where = on_lane(half * HALF_W + k)
                    moved = [dm[rows, where], dn2[s, rows, where], dp[rows, where]]
                    for q in range(3):
                        mix[q].append(wt[q] * moved[0] + wt[3 + q] * moved[1] + wt[6 + q] * moved[2])
                    v = v1[s, rows, where]
                    u = 1.0 + jnp.tanh(v)
                    us.append(u)
                    hs.append(v * u)
                left = later_bin(*mix[0])
                right = earlier_bin(*mix[2])
                for half in range(2):
                    dh[rows, on_lane(half * HALF_W + k)] = (left[half] + mix[1][half] + right[half]) * (
                        us[half] + hs[half] * (2.0 - us[half])
                    )
            return carry

        def taps_step(j, carry):
            rows = pl.ds(pl.multiple_of(8 * j, 8), 8)
            sums = [zero_tile] * TAPS
            for k in range(HALF_W):
                hs = []
                for half in range(2):
                    v = v1[s, rows, on_lane(half * HALF_W + k)]
                    hs.append(v + v * jnp.tanh(v))
                near = [earlier_bin(*hs), hs, later_bin(*hs)]
                for half in range(2):
                    where = on_lane(half * HALF_W + k)
                    moved = [dm[rows, where], dn2[s, rows, where], dp[rows, where]]
                    for q in range(3):
                        for p in range(3):
                            sums[3 * p + q] = sums[3 * p + q] + moved[p] * near[q][half]
            for t in range(TAPS):
                acc[t, rows, :] = acc[t, rows, :] + sums[t]
            return carry

        lax.fori_loop(0, EXP // 8, frames_step, 0, unroll=9)
        lax.fori_loop(0, EXP // 8, bins_step, 0, unroll=9)
        lax.fori_loop(0, EXP // 8, taps_step, 0, unroll=6)

        def pack(j, carry):
            rows = pl.ds(pl.multiple_of(16 * j, 16), 16)
            low_rows = pl.ds(pl.multiple_of(EXP + 16 * j, 16), 16)
            for n in range(WIDE):
                high, low = halves(0.5 * dh[rows, on_lane(n)])
                hh[s, rows, on_lane(n)] = high
                hh[s, low_rows, on_lane(n)] = low
            return carry

        lax.fori_loop(0, EXP // 16, pack, 0, unroll=3)
        main = nt(xs[s, 0:64, :], hh[s, 0:EXP, :])
        main = main[0:32] + main[32:64] + nt(xs[s, 0:32, :], hh[s, EXP:, :])
        small[1] = small[1] + main[0:IN]
        small[2, 0:8, :] = small[2, 0:8, :] + main[IN:32]
        return carry

    lax.fori_loop(0, slots, taps_back_slot, 0)

    stacked = [small[0], small[1]]
    cross1 = jnp.sum(small[1] * weight, axis=0, keepdims=True)
    rb[3, me, 0:2, :] = split_row(small[2, 0:1, :])
    rb[3, me, 2:4, :] = split_row(cross1)
    tail = [lane_sums(acc[t]) for t in range(TAPS)]
    tail.append(excite_bias_grad)
    tail.append(jnp.concatenate([reduce_bias_grad, jnp.zeros((1, EXP - SQZ), F32)], axis=1))
    tail.append(jnp.zeros((5, EXP), F32))
    stacked.append(jnp.concatenate(tail, axis=0))
    for part in (excite_grad, reduce_grad):
        stacked.append(jnp.concatenate([part, jnp.zeros((8 - SQZ, EXP), F32)], axis=0))
    stacked = jnp.concatenate(stacked, axis=0)
    n_heads = 10
    for i in range(n_heads):
        bulk[i] = stacked[8 * i : 8 * i + 8, :LANES]
    ends = [stacked[8 * i : 8 * i + 8, LANES:] for i in range(n_heads)]
    bulk[n_heads] = jnp.concatenate(ends[:8], axis=1)
    bulk[n_heads + 1] = jnp.concatenate(ends[8:] + [jnp.zeros((8, LANES - 16 * (n_heads - 8)), F32)], axis=1)
    for i in range(n_heads + 2, BULK):
        bulk[i] = zero_tile
    each = BULK // GROUP
    base = lax.div(me, GROUP) * GROUP
    place = lax.rem(me, GROUP)

    def group_copy(source, target, index, step):
        return pltpu.make_async_remote_copy(
            src_ref=source, dst_ref=target, send_sem=r_send.at[index], recv_sem=r_recv.at[index],
            device_id=device(base + lax.rem(place + step, GROUP)), device_id_type=MESH,
        )

    for step in range(1, GROUP):
        other = lax.rem(place + step, GROUP)
        group_copy(bulk.at[pl.ds(each * other, each)], bulk_in.at[place], 4, step).start()
    bulk_in[place] = bulk[pl.ds(each * place, each)]
    spread_start(rb.at[3, me], rb.at[3, me], 7)
    done = group_copy(bulk_in.at[pl.ds(0, GROUP - 1)], bulk_in.at[pl.ds(0, GROUP - 1)], 4, 1)
    done.wait_send()
    done.wait_recv()
    bulk_all[me] = jnp.sum(bulk_in[...], axis=0)
    spread_start(bulk_all.at[me], bulk_all.at[me], 5)
    spread_wait(rb.at[3, pl.ds(0, n_dev - 1)], 7)
    sums = jnp.sum(rb[3], axis=0)
    bias1_grad = join_row(sums[0:2])
    gain1_grad = scale1 * join_row(sums[2:4])
    lean1 = scale1 * gain1_grad * (1.0 / total)

    for step in range(1, QUADS):
        def o_done(s, carry, step=step):
            o_copy(step, s).wait_send()
            x_copy(step, s).wait_send()
            c_copy(step, s).wait_send()
            return carry

        lax.fori_loop(0, slots, o_done, 0)
    grown = weight * grow1
    grown_high = grown.astype(BF16)
    grown_both = jnp.concatenate([grown_high.astype(F32), grown - grown_high.astype(F32)], axis=0).astype(BF16)
    lean_map = -nt(grown * lean1, weight, FULL)
    flat_col = -jnp.sum(grown * (bias1_grad * (1.0 / total)), axis=1, keepdims=True)
    side = jnp.concatenate([lean_map, flat_col, jnp.zeros((IN, 7), F32)], axis=1)
    side_high = side.astype(BF16).astype(F32)
    wlow[...] = jnp.concatenate([side_high, side_high, side - side_high], axis=1).astype(BF16)

    def last_slot(s, carry):
        main = nn(grown_both, hh[s, 0:EXP, :])
        main = main[:IN] + main[IN:] + nn(grown_high, hh[s, EXP:, :]) + nn(wlow[...], xs[s])
        for n in range(WIDE):
            place_back(xq, s, n, c3[s, :, on_lane(n)] + main[:, n * LANES : (n + 1) * LANES])
        for step in range(1, QUADS):
            g_copy(step, s).start()
        return carry

    lax.fori_loop(0, slots, last_slot, 0)
    own_g = pltpu.make_async_copy(xq.at[space], ing.at[pl.ds(slots * space, slots)], own_sem.at[3])
    own_g.start()

    spread_wait(bulk_all.at[pl.ds(0, n_dev - 1)], 5)
    summed = []
    for i in range(n_heads + 2):
        tile = zero_tile
        for g in range(n_dev // GROUP):
            tile = tile + bulk_all[g * GROUP + i // each, i % each]
        summed.append(tile)

    def row_tile(i):
        rest = summed[n_heads + i // 8][:, 16 * (i % 8) : 16 * (i % 8) + 16]
        return jnp.concatenate([summed[i], rest], axis=1)

    project_grad = jnp.concatenate([row_tile(i) for i in range(3)], axis=0)
    expand_cross = jnp.concatenate([row_tile(i) for i in range(3, 6)], axis=0)
    depth_tiles = jnp.concatenate([row_tile(6), row_tile(7)], axis=0)
    excite_tile = row_tile(8)
    reduce_tile = row_tile(9)
    expand_grad = grow1 * (expand_cross - lean1 * moment_w)
    zero_rows = jnp.zeros((16, EXP), F32)
    gs_out[0] = expand_grad
    gs_out[1] = project_grad
    gs_out[2] = jnp.concatenate([reduce_tile, zero_rows], axis=0)
    gs_out[3] = jnp.concatenate([excite_tile, zero_rows], axis=0)
    row16 = lax.broadcasted_iota(jnp.int32, (16, EXP), 0)
    gs_out[4] = jnp.concatenate([jnp.where(row16 < TAPS, depth_tiles, 0.0), zero_rows[:8]], axis=0)
    vr_out[...] = jnp.concatenate(
        [
            gain1_grad,
            bias1_grad,
            gain2_grad,
            bias2_grad,
            jnp.concatenate([gain3_grad, jnp.zeros((1, EXP - LANES), F32)], axis=1),
            jnp.concatenate([bias3_grad, jnp.zeros((1, EXP - LANES), F32)], axis=1),
            depth_tiles[TAPS + 1 : TAPS + 2],
            depth_tiles[TAPS : TAPS + 1],
        ],
        axis=0,
    )

    mine = jnp.minimum(place, 4)
    grad = gs_out[mine]
    turned = (mine == 1) | (mine == 2)
    small[...] = jnp.zeros(small.shape, F32)
    small[0, :, :IN] = in_st[0]
    small[1, :, :IN] = jnp.transpose(in_st[1])
    small[2, :SQZ, :SQZ] = jnp.transpose(sq_st[:, 0, :])
    small[3, :SQZ, :SQZ] = sq_st[:, 1, :]
    small[4, :TAPS, :TAPS] = tap_st[...]
    old_big = big[mine]
    old_big = jnp.where(turned, jnp.transpose(old_big), old_big)
    big_m = DECAY * old_big + FRESH * tn(grad, grad, FULL)
    small_m = DECAY * small[mine][:, :IN] + FRESH * nt(grad, grad, FULL)
    big_eye = (
        lax.broadcasted_iota(jnp.int32, (EXP, EXP), 0) == lax.broadcasted_iota(jnp.int32, (EXP, EXP), 1)
    ).astype(F32)
    small_eye = eye24.astype(F32)
    big_c = 2.5 * lax.rsqrt(jnp.sum(jnp.sum(big_m * big_m, axis=0, keepdims=True), axis=1, keepdims=True))
    small_c = 2.5 * lax.rsqrt(jnp.sum(jnp.sum(small_m * small_m, axis=0, keepdims=True), axis=1, keepdims=True))
    big_m = big_c * big_m
    small_m = small_c * small_m
    direction = jnp.sqrt(jnp.sqrt(big_c)) * grad
    small_h = jnp.sqrt(jnp.sqrt(small_c)) * small_eye

    def root_step(i, carry):
        big_m, small_m, direction, small_h = carry
        big_k = 1.25 * big_eye - 0.25 * big_m
        small_k = 1.25 * small_eye - 0.25 * small_m
        direction = nn(direction, big_k, MID)
        small_h = nn(small_h, small_k, MID)
        big_k = nn(big_k, big_k, MID)
        small_k = nn(small_k, small_k, MID)
        big_k = nn(big_k, big_k, MID)
        small_k = nn(small_k, small_k, MID)
        return nn(big_k, big_m, MID), nn(small_k, small_m, MID), direction, small_h

    _, _, direction, small_h = lax.fori_loop(
        0, ROOT_ITERS, root_step, (big_m, small_m, direction, small_h)
    )
    direction = nn(small_h, direction, FULL)
    short = jnp.where(mine < 2, float(IN), jnp.where(mine == 4, float(TAPS), float(SQZ)))
    lead = jnp.where(turned, float(EXP), short)
    power = jnp.sum(jnp.sum(direction * direction, axis=0, keepdims=True), axis=1, keepdims=True)
    power = power / jnp.full((1, 1), short * float(EXP), F32)
    step_size = STEP_FRACTION * lax.rsqrt(jnp.full((1, 1), lead, F32)) * lax.rsqrt(power + 1e-06)
    small[0] = weight
    small[1] = w_pro_t[...]
    for i, source in ((2, w_red_t), (3, w_exc), (4, w_dep)):
        small[i] = jnp.zeros((IN, EXP), F32)
        small[i, : source.shape[0], :] = source[...]
    nws[place] = small[mine] - step_size * direction
    for step in range(1, GROUP):
        group_copy(nws.at[place], nws.at[place], 6, step).start()
    done = group_copy(nws.at[pl.ds(0, GROUP - 1)], nws.at[pl.ds(0, GROUP - 1)], 6, 1)
    done.wait_send()
    done.wait_recv()
    nw_out[...] = nws[0:5]

    for step in range(1, QUADS):
        def all_done(s, carry, step=step):
            o_copy(step, s).wait_recv()
            g_copy(step, s).wait()
            return carry

        lax.fori_loop(0, slots, all_done, 0)
    own_o.wait()
    own_g.wait()


def finish_kernel(
    gs, nw, vr, big, in_st, sq_st, tap_st, vec, vec_m, field_a, field_b,
    out, ing, ge, gd, gr_t, gx, gp_t, ne, nd, nr_t, nx, np_t, big_new, in_new, sq_new, tap_new, vg, vm, vn, held, sem,
):
    fields = ((field_a, out), (field_b, ing))
    loads = [pltpu.make_async_copy(source, held.at[i], sem.at[i]) for i, (source, _) in enumerate(fields)]
    stores = [pltpu.make_async_copy(held.at[i], target, sem.at[i]) for i, (_, target) in enumerate(fields)]
    for load in loads:
        load.start()
    ge[...], gp_t[...], gr_t[...], gx[...], gd[...] = gs[0], gs[1], gs[2, :SQZ], gs[3, :SQZ], gs[4, :TAPS]
    ne[...], np_t[...], nr_t[...], nx[...], nd[...] = nw[0], nw[1], nw[2, :SQZ], nw[3, :SQZ], nw[4, :TAPS]
    start = 0
    for i, width in enumerate(PARTS):
        vg[:, start : start + width] = vr[i : i + 1, :width]
        start = start + width
    grads = vg[...]
    moments = DECAY * vec_m[...] + FRESH * grads * grads
    vm[...] = moments
    vn[...] = vec[...] - VECTOR_RATE * grads / (jnp.sqrt(moments) + 1e-08)
    for load, store in zip(loads, stores):
        load.wait()
        store.start()
    for i in range(5):
        grad = gs[i]
        big_new[i] = DECAY * big[i] + FRESH * tn(grad, grad, FULL)
        inner = FRESH * nt(grad, grad, FULL)
        if i < 2:
            in_new[i] = DECAY * in_st[i] + inner
        elif i < 4:
            sq_new[:, i - 2, :] = DECAY * sq_st[:, i - 2, :] + inner[:SQZ, :SQZ]
        else:
            tap_new[...] = DECAY * tap_st[...] + inner[:TAPS, :TAPS]
    for store in stores:
        store.wait()


def on_device(
    n_dev, n_space,
    features, cotangent, segment_ids, w_expand, w_depth, w_reduce, w_excite, w_project,
    vector_params, vector_moments, big_stats, in_stats, sq_stats, tap_stats,
):
    slot_count = features.shape[0]
    slots = slot_count // QUADS
    n_pos = slot_count * (n_dev // n_space) * FRAMES * BINS
    vm = pl.BlockSpec(memory_space=pltpu.VMEM)
    vec = vector_params.reshape(1, -1)
    sq_rows = sq_stats.transpose(1, 0, 2)
    hbm = pl.BlockSpec(memory_space=pl.ANY)
    grid_shape = jax.ShapeDtypeStruct((slot_count, ROWS, LANES), F32)
    wide = WIDE * LANES
    vmem = pltpu.VMEM
    dma = pltpu.SemaphoreType.DMA
    out, ing, gs, nw, vr = pl.pallas_call(
        functools.partial(block_kernel, n_dev, n_space, slots, n_pos),
        out_shape=(
            grid_shape,
            grid_shape,
            jax.ShapeDtypeStruct((5, IN, EXP), F32),
            jax.ShapeDtypeStruct((5, IN, EXP), F32),
            jax.ShapeDtypeStruct((8, EXP), F32),
        ),
        in_specs=[hbm, hbm] + [vm] * 11,
        out_specs=(hbm, hbm, vm, vm, vm),
        scratch_shapes=[
            vmem((QUADS, slots, ROWS, LANES), F32),
            vmem((QUADS, slots, ROWS, LANES), F32),
            vmem((QUADS, slots, ROWS, LANES), F32),
            vmem((slots, 96, wide), BF16),
            vmem((slots, IN, wide), F32),
            vmem((slots, IN, wide), F32),
            vmem((slots, EXP, wide), F32),
            vmem((slots, EXP, wide), F32),
            vmem((slots, 2 * EXP, wide), BF16),
            vmem((slots, EXP, wide), F32),
            vmem((EXP, wide), F32),
            vmem((EXP, wide), F32),
            vmem((EXP, wide), F32),
            vmem((slots, IN, wide), F32),
            vmem((slots, slots * REGIONS, wide), BF16),
            vmem((slots, 256, wide), BF16),
            vmem((TAPS + 3, EXP, LANES), F32),
            vmem((2, slots, 8, wide), F32),
            vmem((REGIONS, slots, 8, wide), F32),
            vmem((TAPS, EXP, LANES), F32),
            vmem((EXP, 96), BF16),
            vmem((IN, 96), BF16),
            vmem((8, EXP), F32),
            vmem((5, IN, EXP), F32),
            vmem((slots * REGIONS, EXP), F32),
            vmem((slots, REGIONS, EXP), F32),
            vmem((slots, REGIONS, EXP), F32),
            vmem((BULK, 8, LANES), F32),
            vmem((GROUP, BULK // GROUP, 8, LANES), F32),
            vmem((n_dev, BULK // GROUP, 8, LANES), F32),
            vmem((n_dev, 8, LANES), F32),
            vmem((4, n_dev, 4, LANES), F32),
            vmem((GROUP, IN, EXP), F32),
            vmem((IN, LANES), F32),
            dma((QUADS,)),
        ]
        + [dma((QUADS, slots))] * 8
        + [dma((8,)), dma((8,)), dma((4,))],
        compiler_params=pltpu.CompilerParams(
            collective_id=0, has_side_effects=True, vmem_limit_bytes=60 << 20
        ),
    )(
        features.reshape(slot_count, ROWS, LANES),
        cotangent.reshape(slot_count, ROWS, LANES),
        segment_ids, w_expand, w_depth, w_reduce.T, w_excite, w_project.T, vec,
        big_stats, in_stats, sq_rows, tap_stats,
    )
    shape = jax.ShapeDtypeStruct
    (
        out, ing, ge, gd, gr_t, gx, gp_t, ne, nd, nr_t, nx, np_t, big_new, in_new, sq_new, tap_new, vg, vm_new, vn
    ) = pl.pallas_call(
        finish_kernel,
        out_shape=(grid_shape, grid_shape) + tuple(
            shape(dims, F32)
            for dims in [(IN, EXP), (TAPS, EXP), (SQZ, EXP), (SQZ, EXP), (IN, EXP)] * 2
            + [(5, EXP, EXP), (2, IN, IN), (SQZ, 2, SQZ), (TAPS, TAPS)]
            + [vec.shape] * 3
        ),
        in_specs=[vm] * 9 + [hbm] * 2,
        out_specs=(hbm, hbm) + (vm,) * 17,
        scratch_shapes=[vmem((2,) + grid_shape.shape, F32), dma((2,))],
        compiler_params=pltpu.CompilerParams(vmem_limit_bytes=32 << 20),
    )(gs, nw, vr, big_stats, in_stats, sq_rows, tap_stats, vec, vector_moments.reshape(1, -1), out, ing)
    return (
        out.reshape(features.shape), ing.reshape(features.shape),
        ge, gd, gr_t.T, gx, gp_t.T, ne, nd, nr_t.T, nx, np_t.T,
        big_new, in_new, sq_new.transpose(1, 0, 2), tap_new, vg.reshape(-1), vm_new.reshape(-1), vn.reshape(-1),
    )


def solution(mesh):
    field = P("dp", None, "space", None)
    return jax.shard_map(
        functools.partial(on_device, mesh.shape["dp"] * mesh.shape["space"], mesh.shape["space"]),
        mesh=mesh,
        in_specs=(field, field, P("dp", None)) + (P(),) * 11,
        out_specs=(field, field) + (P(),) * 17,
        check_vma=False,
    )
```

```python
import functools
import math

import jax
import jax.numpy as jnp
from jax import lax
from jax.experimental import pallas as pl
from jax.experimental.pallas import tpu as pltpu
from jax.sharding import PartitionSpec as P

IN = 24
EXP = 144
SQZ = 6
TAPS = 9
FRAMES = 96
BINS = 16
REGIONS = 4
QUADS = 4
ROOT_ITERS = 10
NORM_EPS = 0.001
DECAY = 0.9
FRESH = 1.0 - DECAY
STEP_FRACTION = 0.5
VECTOR_RATE = 0.15
PARTS = (EXP, EXP, EXP, EXP, IN, IN, SQZ, EXP)

LANES = 128
HALF_W = 6
WIDE = 2 * HALF_W
ROWS = IN * 3
GROUP = 8
BULK = 16

F32 = jnp.float32
BF16 = jnp.bfloat16
FULL = lax.Precision.HIGHEST
MID = lax.Precision.HIGH
MESH = pl.DeviceIdType.MESH


def mm(left, right, dims, precision=None):
    return lax.dot_general(
        left, right, ((dims[:1], dims[1:]), ((), ())), precision=precision, preferred_element_type=F32
    )


def nn(left, right, precision=None):
    return mm(left, right, (1, 0), precision)


def nt(left, right, precision=None):
    return mm(left, right, (1, 1), precision)


def tn(left, right, precision=None):
    return mm(left, right, (0, 0), precision)


def halves(value):
    high = value.astype(BF16)
    return high, (value - high.astype(F32)).astype(BF16)


def column(rows, index, width):
    pick = (lax.broadcasted_iota(jnp.int32, (rows.shape[0], LANES), 0) == index).astype(F32)
    return tn(rows, pick, FULL)[:width]


def lane_sums(table):
    return nt(jnp.ones((8, table.shape[1]), F32), table, FULL)[0:1]


def split_row(row):
    return jnp.concatenate(
        [row[:, :LANES], jnp.concatenate([row[:, LANES:], jnp.zeros((1, 2 * LANES - EXP), F32)], axis=1)], axis=0
    )


def join_row(pair):
    return jnp.concatenate([pair[0:1], pair[1:2, : EXP - LANES]], axis=1)


def tile_quad(n):
    return 2 * ((n % HALF_W) // 3) + n // HALF_W


def on_lane(n):
    return pl.ds(n * LANES, LANES)


def block_kernel(
    n_dev, n_space, slots, n_pos,
    feat, cot, ids_ref, w_exp, w_dep, w_red_t, w_exc, w_pro_t, vec, big, in_st, sq_st, tap_st,
    out, ing, gs_out, nw_out, vr_out,
    xloc, xq, cq, xs, x3, c3, v1, a2, hh, dn2, dh, dm, dp, a3, hot, dcat, tab, msk, reg, acc, w1t, wlow, prm,
    small, pooled, gates, dgate, bulk, bulk_in, bulk_all, rb1, rb, nws, fold,
    loc_sem, x_send, x_recv, c_send, c_recv, o_send, o_recv, g_send, g_recv,
    r_send, r_recv, own_sem,
):
    space = lax.axis_index("space")
    me = lax.axis_index("dp") * n_space + space
    n_loc = float(slots * FRAMES * BINS)
    total = float(n_pos)

    def device(index):
        return (lax.div(index, n_space), lax.rem(index, n_space))

    def peer(step):
        return lax.rem(space + step, QUADS)

    def space_device(step):
        return (lax.axis_index("dp"), peer(step))

    barrier = pltpu.get_barrier_semaphore()

    def greet(step, carry):
        pl.semaphore_signal(
            barrier, inc=1, device_id=device(lax.rem(me + step, n_dev)), device_id_type=MESH
        )
        return carry

    lax.fori_loop(1, n_dev, greet, 0)
    loads = [
        pltpu.make_async_copy(feat.at[pl.ds(slots * q, slots)], xloc.at[q], loc_sem.at[q]) for q in range(QUADS)
    ]
    for load in loads:
        load.start()
    own_x = pltpu.make_async_copy(feat.at[pl.ds(slots * space, slots)], xq.at[space], own_sem.at[0])
    own_c = pltpu.make_async_copy(cot.at[pl.ds(slots * space, slots)], cq.at[space], own_sem.at[1])
    own_x.start()
    own_c.start()

    for load in loads:
        load.wait()
    first = jnp.concatenate([xloc[0, 0, pl.ds(k, IN, stride=3), :] for k in range(3)], axis=1)
    shift_col = nn(first, jnp.ones((3 * LANES, LANES), F32), FULL) * (1.0 / (3 * LANES))
    shift_row = nt(jnp.ones((8, 3 * LANES), F32), first, FULL)[0:1] * (1.0 / (3 * LANES))
    one_rows = (lax.broadcasted_iota(jnp.int32, (8, LANES), 0) == 0).astype(F32)

    def gram_step(s, gram):
        parts = []
        for q in range(QUADS):
            for k in range(3):
                parts.append(
                    jnp.concatenate([xloc[q, s, pl.ds(k, IN, stride=3), :] - shift_col, one_rows], axis=0)
                )
        high, low = halves(jnp.concatenate(parts, axis=1))
        both = jnp.concatenate([high, low], axis=0)
        return gram + nt(both, both)

    gram = lax.fori_loop(0, slots, gram_step, jnp.zeros((64, 64), F32), unroll=True)
    gram = gram[:32, :32] + gram[32:, :32] + gram[:32, 32:] + gram[32:, 32:]
    off_row = gram[IN : IN + 1, :IN] * (1.0 / n_loc)
    off_col = gram[:IN, IN : IN + 1] * (1.0 / n_loc)
    local_m2 = gram[:IN, :IN] - n_loc * off_col * off_row
    fold[...] = jnp.zeros((IN, LANES), F32)
    fold[:, :IN] = local_m2
    packed = jnp.zeros((6, LANES), F32)
    for g in range(4):
        piece = fold[pl.ds(g, 6, stride=4), :]
        packed = packed + (pltpu.roll(piece, 32 * g, 1) if g else piece)
    rb1[me, 0:6, :] = packed
    rb1[me, 6:7, :] = jnp.concatenate([shift_row + off_row, jnp.zeros((1, LANES - IN), F32)], axis=1)
    rb1[me, 7:8, :] = jnp.zeros((1, LANES), F32)

    pl.semaphore_wait(barrier, n_dev - 1)

    def spread_start(source, target, index):
        def send(step, carry):
            pltpu.make_async_remote_copy(
                src_ref=source, dst_ref=target, send_sem=r_send.at[index], recv_sem=r_recv.at[index],
                device_id=device(lax.rem(me + step, n_dev)), device_id_type=MESH,
            ).start()
            return carry

        lax.fori_loop(1, n_dev, send, 0)

    def spread_wait(window, index):
        done = pltpu.make_async_remote_copy(
            src_ref=window, dst_ref=window, send_sem=r_send.at[index], recv_sem=r_recv.at[index],
            device_id=device(me), device_id_type=MESH,
        )
        done.wait_send()
        done.wait_recv()

    def quad_copy(source, target, send, recv, step, s):
        return pltpu.make_async_remote_copy(
            src_ref=source, dst_ref=target, send_sem=send.at[step, s], recv_sem=recv.at[step, s],
            device_id=space_device(step), device_id_type=MESH,
        )

    def x_copy(step, s):
        return quad_copy(feat.at[slots * peer(step) + s], xq.at[space, s], x_send, x_recv, step, s)

    def c_copy(step, s):
        return quad_copy(cot.at[slots * peer(step) + s], cq.at[space, s], c_send, c_recv, step, s)

    def o_copy(step, s):
        return quad_copy(xloc.at[peer(step), s], out.at[slots * space + s], o_send, o_recv, step, s)

    def g_copy(step, s):
        return quad_copy(xq.at[peer(step), s], ing.at[slots * space + s], g_send, g_recv, step, s)

    spread_start(rb1.at[me], rb1.at[me], 0)

    def x_start(s, carry):
        for step in range(1, QUADS):
            x_copy(step, s).start()
        return carry

    lax.fori_loop(0, slots, x_start, 0)

    lane = lax.broadcasted_iota(jnp.int32, (8, LANES), 1)
    low_bin = lax.rem(lane, 8) == 0
    high_bin = lax.rem(lane, 8) == 7
    first_row = lane < 8
    second_row = (lane >= 8) & (lane < 16)
    last_row = lane >= LANES - 8
    zero_tile = jnp.zeros((8, LANES), F32)

    half_lanes = HALF_W * LANES
    own_ids = ids_ref[pl.ds(pl.multiple_of(slots * space, 8), slots), :].astype(F32)
    spread = (
        lax.broadcasted_iota(jnp.int32, (FRAMES, half_lanes), 1) // 8
        == lax.broadcasted_iota(jnp.int32, (FRAMES, half_lanes), 0)
    )
    wide_ids = nn(own_ids.astype(BF16), spread.astype(F32).astype(BF16))
    wide_lane = lax.broadcasted_iota(jnp.int32, (slots, half_lanes), 1)
    before = pltpu.roll(wide_ids, 8, 1)
    after = pltpu.roll(wide_ids, half_lanes - 8, 1)
    from_ok = jnp.where((before == wide_ids) & (wide_lane >= 8), 1.0, 0.0)
    to_ok = jnp.where((after == wide_ids) & (wide_lane < half_lanes - 8), 1.0, 0.0)
    def both_halves(rows):
        turned = [pltpu.roll(rows[:, n * LANES : (n + 1) * LANES], 8, 1) for n in range(HALF_W)]
        return jnp.concatenate([rows] + turned, axis=1)

    marks = [both_halves(rows) for rows in (from_ok, to_ok)]
    regions = [both_halves((wide_ids == float(r)).astype(F32)) for r in range(REGIONS)]
    for s in range(slots):
        for i in range(2):
            msk[i, s] = jnp.broadcast_to(marks[i][s : s + 1], (8, WIDE * LANES))
        for r in range(REGIONS):
            reg[r, s] = jnp.broadcast_to(regions[r][s : s + 1], (8, WIDE * LANES))
    row_index = lax.broadcasted_iota(jnp.int32, (slots * REGIONS, WIDE * LANES), 0)
    counts = jnp.zeros((slots * REGIONS, 1), F32)
    for s in range(slots):
        row = jnp.zeros((slots * REGIONS, WIDE * LANES), F32)
        for r in range(REGIONS):
            row = jnp.where(row_index == REGIONS * s + r, regions[r][s : s + 1], row)
        counts = counts + jnp.sum(row, axis=1, keepdims=True)
        hot[s] = row.astype(BF16)
    taps = w_dep[...]
    for t in range(TAPS):
        tab[t] = column(taps, t, EXP)

    start = 0
    prm[...] = jnp.zeros((8, EXP), F32)
    for i, width in enumerate(PARTS):
        prm[i : i + 1, :width] = vec[pl.ds(start, width)].reshape(1, width)
        start = start + width

    spread_wait(rb1.at[pl.ds(0, n_dev - 1)], 0)
    gathered = jnp.sum(rb1[...], axis=0)
    means = rb1[:, 6, :]
    mean_row = jnp.sum(means, axis=0, keepdims=True) * (1.0 / n_dev)
    apart = means - mean_row
    between = tn(apart, apart, FULL)[:IN, :IN]
    for g in range(4):
        piece = gathered[0:6]
        piece = pltpu.roll(piece, LANES - 32 * g, 1) if g else piece
        fold[pl.ds(g, 6, stride=4), :] = piece
    moment = fold[:, :IN] + n_loc * between
    eye24 = (
        lax.broadcasted_iota(jnp.int32, (IN, IN), 0) == lax.broadcasted_iota(jnp.int32, (IN, IN), 1)
    )
    mean_col = nn(jnp.where(eye24, mean_row[:, :IN], 0.0), jnp.ones((IN, LANES), F32), FULL)
    weight = w_exp[...]
    moment_w = nn(moment, weight, FULL)
    scale1 = lax.rsqrt(jnp.sum(moment_w * weight, axis=0, keepdims=True) * (1.0 / total) + NORM_EPS)
    grow1 = prm[0:1, :] * scale1
    shaped = jnp.concatenate(
        [weight * (0.5 * grow1), 0.5 * prm[1:2, :], jnp.zeros((7, EXP), F32)], axis=0
    )
    shaped_high = shaped.astype(BF16).astype(F32)
    w1t[...] = jnp.transpose(
        jnp.concatenate([shaped_high, shaped_high, shaped - shaped_high], axis=0)
    ).astype(BF16)

    own_x.wait()
    acc[0] = jnp.zeros((EXP, LANES), F32)

    def fetch(quads, s, n):
        tile = quads[tile_quad(n), s, pl.ds(n % 3, IN, stride=3), :]
        return tile if n < HALF_W else pltpu.roll(tile, 8, 1)

    def place_back(quads, s, n, tile):
        tile = tile if n < HALF_W else pltpu.roll(tile, LANES - 8, 1)
        quads[tile_quad(n), s, pl.ds(n % 3, IN, stride=3), :] = tile

    def later_bin(low, high):
        return (
            pltpu.roll(jnp.where(low_bin, high, low), LANES - 1, 1),
            jnp.where(high_bin, 0.0, pltpu.roll(high, LANES - 1, 1)),
        )

    def earlier_bin(low, high):
        return (
            jnp.where(low_bin, 0.0, pltpu.roll(low, 1, 1)),
            pltpu.roll(jnp.where(high_bin, low, high), 1, 1),
        )

    def from_before(tiles, k, half):
        edge = first_row if half else last_row
        return pltpu.roll(jnp.where(edge, tiles[(k - 1) % HALF_W], tiles[k]), 8, 1)

    def from_after(tiles, k, half):
        edge = second_row if half else first_row
        return pltpu.roll(jnp.where(edge, tiles[(k + 1) % HALF_W], tiles[k]), LANES - 8, 1)

    def tile_rows(j, height=8):
        return pl.ds(height * j, height) if isinstance(j, int) else pl.ds(pl.multiple_of(height * j, height), height)

    def expand_slot(s):
        for n in range(WIDE):
            tile = fetch(xq, s, n)
            x3[s, :, on_lane(n)] = tile
            high, low = halves(jnp.concatenate([tile - mean_col, one_rows], axis=0))
            xs[s, 0:32, on_lane(n)] = high
            xs[s, 32:64, on_lane(n)] = low
            xs[s, 64:96, on_lane(n)] = high
        v1[s] = nn(w1t[...], xs[s])

    def x_arrived(s):
        for step in range(1, QUADS):
            x_copy(step, s).wait_recv()

    def forward_slot(s, carry):
        for step in range(1, QUADS):
            c_copy(step, s).start()

        def bins_step(j, carry):
            rows = pl.ds(pl.multiple_of(8 * j, 8), 8)
            wt = [tab[t, rows, :] for t in range(TAPS)]
            for k in range(HALF_W):
                pair = []
                for half in range(2):
                    v = v1[s, rows, on_lane(half * HALF_W + k)]
                    pair.append(v + v * jnp.tanh(v))
                nxt = later_bin(*pair)
                prv = earlier_bin(*pair)
                for half in range(2):
                    for p, target in enumerate((dm, dh, dp)):
                        target[rows, on_lane(half * HALF_W + k)] = (
                            wt[3 * p] * prv[half] + wt[3 * p + 1] * pair[half] + wt[3 * p + 2] * nxt[half]
                        )
            return carry

        def frames_step(j, carry):
            rows = tile_rows(j)
            got = zero_tile
            for half in range(2):
                prior = [dm[rows, on_lane(half * HALF_W + k)] for k in range(HALF_W)]
                later = [dp[rows, on_lane(half * HALF_W + k)] for k in range(HALF_W)]
                for k in range(HALF_W):
                    where = on_lane(half * HALF_W + k)
                    value = (
                        dh[rows, where]
                        + msk[0, s, :, where] * from_before(prior, k, half)
                        + msk[1, s, :, where] * from_after(later, k, half)
                    )
                    a2[s, rows, where] = value
                    got = got + value
            acc[0, rows, :] = acc[0, rows, :] + got
            return carry

        lax.fori_loop(0, EXP // 8, bins_step, 0, unroll=9)

        @pl.when(s < slots - 1)
        def _():
            x_arrived(s + 1)

        expand_slot(jnp.minimum(s + 1, slots - 1))
        for j in range(EXP // 8):
            frames_step(j, 0)
        return carry

    x_arrived(0)
    expand_slot(0)

    lax.fori_loop(0, slots, forward_slot, 0)

    acc[1] = nn(acc[0], jnp.ones((LANES, LANES), F32), FULL) * (1.0 / n_loc)
    acc[2] = jnp.zeros((EXP, LANES), F32)

    def square_step(s, carry):
        def tile_step(j, carry):
            rows = pl.ds(pl.multiple_of(8 * j, 8), 8)
            center = acc[1, rows, :]
            got = zero_tile
            for n in range(WIDE):
                off = a2[s, rows, on_lane(n)] - center
                got = got + off * off
            acc[2, rows, :] = acc[2, rows, :] + got
            return carry

        return lax.fori_loop(0, EXP // 8, tile_step, carry, unroll=3)

    lax.fori_loop(0, slots, square_step, 0)
    rb[0, me, 0:2, :] = split_row(lane_sums(acc[0]) * (1.0 / n_loc))
    rb[0, me, 2:4, :] = split_row(lane_sums(acc[2]))
    spread_start(rb.at[0, me], rb.at[0, me], 1)
    spread_wait(rb.at[0, pl.ds(0, n_dev - 1)], 1)
    sums = jnp.sum(rb[0], axis=0)
    mean2 = sums[0:2] * (1.0 / n_dev)
    gaps = rb[0][:, 0:2, :] - mean2[None]
    spread2 = sums[2:4] + n_loc * jnp.sum(gaps * gaps, axis=0)
    scale2 = lax.rsqrt(join_row(spread2) * (1.0 / total) + NORM_EPS)
    mean2 = join_row(mean2)
    rows8 = jnp.concatenate(
        [mean2, 0.5 * prm[2:3, :] * scale2, 0.5 * prm[3:4, :], jnp.zeros((5, EXP), F32)], axis=0
    )
    for i in range(3):
        tab[TAPS + i] = column(rows8, i, EXP)

    pooled[...] = jnp.zeros((slots * REGIONS, EXP), F32)

    def activate(s):
        for j in range(EXP // 16):
            rows, low_rows = pl.ds(16 * j, 16), pl.ds(EXP + 16 * j, 16)
            center, grow, lift = (tab[TAPS + i, rows, :] for i in range(3))
            for n in range(WIDE):
                off = a2[s, rows, on_lane(n)] - center
                a2[s, rows, on_lane(n)] = off
                v = off * grow + lift
                high, low = halves(v + v * jnp.tanh(v))
                hh[s, rows, on_lane(n)] = high
                hh[s, low_rows, on_lane(n)] = low

    def pool(s):
        pooled[...] = pooled[...] + nt(hot[s], hh[s, 0:EXP, :]) + nt(hot[s], hh[s, EXP:, :])

    def activate_slot(s, carry):
        pool(s - 1)
        activate(s)
        return carry

    activate(0)
    lax.fori_loop(1, slots, activate_slot, 0)
    pool(slots - 1)

    per_count = 1.0 / counts
    mean_pool = pooled[...] * per_count
    squeeze = nt(mean_pool, w_red_t[...], FULL) + prm[6:7, :SQZ]
    squeeze_sig = jax.nn.sigmoid(squeeze)
    squeezed = squeeze * squeeze_sig
    gate = jax.nn.sigmoid(nn(squeezed, w_exc[...], FULL) + prm[7:8, :])
    for s in range(slots):
        gates[s] = gate[REGIONS * s : REGIONS * (s + 1)]

    def gated_weights(s):
        project = w_pro_t[...]
        rows = gates[s]
        return jnp.concatenate([project * rows[r : r + 1] for r in range(REGIONS)], axis=0)

    def region_tile(r, s, n):
        return jnp.concatenate([reg[r, s, :, on_lane(n)]] * (IN // 8), axis=0)

    def project_slot(s, carry):
        total_a, total_c = carry
        high, low = halves(gated_weights(s))
        body = nn(jnp.concatenate([high, low], axis=0), hh[s, 0:EXP, :])
        body = body[:96] + body[96:] + nn(high, hh[s, EXP:, :])
        for step in range(1, QUADS):
            c_copy(step, s).wait_recv()
        for n in range(WIDE):
            value = jnp.zeros((IN, LANES), F32)
            for r in range(REGIONS):
                value = value + (
                    body[IN * r : IN * (r + 1), n * LANES : (n + 1) * LANES]
                    * region_tile(r, s, n)
                )
            a3[s, :, on_lane(n)] = value
            total_a = total_a + value
            upstream = fetch(cq, s, n)
            c3[s, :, on_lane(n)] = upstream
            total_c = total_c + upstream
        return total_a, total_c

    own_c.wait()
    zero24 = jnp.zeros((IN, LANES), F32)
    total_a, total_c = lax.fori_loop(0, slots, project_slot, (zero24, zero24))
    center3 = nn(total_a, jnp.ones((LANES, LANES), F32), FULL) * (1.0 / n_loc)

    def third_step(s, carry):
        square, cross = carry
        for n in range(WIDE):
            off = a3[s, :, on_lane(n)] - center3
            square = square + off * off
            cross = cross + off * c3[s, :, on_lane(n)]
        return square, cross

    square3, cross3 = lax.fori_loop(0, slots, third_step, (zero24, zero24))

    def pad_row(row):
        return jnp.concatenate([row, jnp.zeros((1, LANES - IN), F32)], axis=1)

    rb[1, me] = jnp.concatenate(
        [
            pad_row(lane_sums(total_a) * (1.0 / n_loc)),
            pad_row(lane_sums(square3)),
            pad_row(lane_sums(total_c)),
            pad_row(lane_sums(cross3)),
        ],
        axis=0,
    )
    spread_start(rb.at[1, me], rb.at[1, me], 2)
    spread_wait(rb.at[1, pl.ds(0, n_dev - 1)], 2)
    third = rb[1]
    sums = jnp.sum(third, axis=0)
    mean3 = sums[0:1] * (1.0 / n_dev)
    gaps = third[:, 0, :] - mean3
    spread3 = sums[1:2] + n_loc * jnp.sum(gaps * gaps, axis=0, keepdims=True)
    scale3 = lax.rsqrt(spread3 * (1.0 / total) + NORM_EPS)
    bias3_grad = sums[2:3]
    cross_sum = sums[3:4] + jnp.sum(third[:, 2, :] * gaps, axis=0, keepdims=True)
    gain3_grad = scale3 * cross_sum
    grow3 = prm[4:5, :LANES] * scale3
    rows8 = jnp.concatenate(
        [
            mean3,
            grow3,
            prm[5:6, :LANES],
            grow3 * bias3_grad * (1.0 / total),
            grow3 * scale3 * gain3_grad * (1.0 / total),
            jnp.zeros((3, LANES), F32),
        ],
        axis=0,
    )
    mean3_c, grow3_c, lift3_c, flat3_c, lean3_c = (column(rows8, i, IN) for i in range(5))

    small[0] = jnp.zeros((IN, EXP), F32)

    def project_back(s):
        for n in range(WIDE):
            off = a3[s, :, on_lane(n)] - mean3_c
            place_back(xloc, s, n, x3[s, :, on_lane(n)] + off * grow3_c + lift3_c)
            grad = grow3_c * c3[s, :, on_lane(n)] - flat3_c - off * lean3_c
            high, low = halves(
                jnp.concatenate(
                    [grad * region_tile(r, s, n) for r in range(REGIONS)], axis=0
                )
            )
            dcat[s, 0:96, on_lane(n)] = high
            dcat[s, 128:224, on_lane(n)] = low
        dcat[s, 96:128, :] = hot[s]
        dcat[s, 224:256, :] = hot[s]
        for step in range(1, QUADS):
            o_copy(step, s).start()

    def gate_back(s):
        main = nt(dcat[s, 0:224, :], hh[s, 0:EXP, :])
        main = main[0:96] + main[128:224] + nt(dcat[s, 0:96, :], hh[s, EXP:, :])
        project = w_pro_t[...]
        gp = small[0]
        rows = gates[s]
        for r in range(REGIONS):
            part = main[IN * r : IN * (r + 1)]
            dgate[s, r : r + 1, :] = jnp.sum(part * project, axis=0, keepdims=True)
            gp = gp + part * rows[r : r + 1]
        small[0] = gp

    def back_slot(s, carry):
        gate_back(s - 1)
        project_back(s)
        return carry

    project_back(0)
    lax.fori_loop(1, slots, back_slot, 0)
    gate_back(slots - 1)
    own_o = pltpu.make_async_copy(xloc.at[space], out.at[pl.ds(slots * space, slots)], own_sem.at[2])
    own_o.start()

    dgate_rows = jnp.concatenate([dgate[s] for s in range(slots)], axis=0)
    dpre_x = dgate_rows * gate * (1.0 - gate)
    excite_grad = tn(squeezed, dpre_x, FULL)
    excite_bias_grad = jnp.sum(dpre_x, axis=0, keepdims=True)
    dsqueezed = nt(dpre_x, w_exc[...], FULL)
    dpre_r = dsqueezed * squeeze_sig * (1.0 + squeeze * (1.0 - squeeze_sig))
    reduce_grad = tn(dpre_r, mean_pool, FULL)
    reduce_bias_grad = jnp.sum(dpre_r, axis=0, keepdims=True)
    dpool = nn(dpre_r, w_red_t[...], FULL) * per_count
    pooled[...] = 0.5 * dpool

    acc[0] = jnp.zeros((EXP, LANES), F32)
    acc[1] = jnp.zeros((EXP, LANES), F32)

    def activation_back(s, target):
        high, low = halves(0.5 * gated_weights(s))
        pool_high, pool_low = halves(pooled[...])
        left = jnp.concatenate([high, pool_high, high, pool_low], axis=0)
        target[...] = tn(left, dcat[s]) + tn(low, dcat[s, 0:96, :])

    def norm_back(s, source):
        for j in range(EXP // 8):
            rows = tile_rows(j)
            grow, lift = (tab[TAPS + i, rows, :] for i in (1, 2))
            plain, cross = zero_tile, zero_tile
            for n in range(WIDE):
                off = a2[s, rows, on_lane(n)]
                v = off * grow + lift
                u = 1.0 + jnp.tanh(v)
                d = source[rows, on_lane(n)] * (u + (v * u) * (2.0 - u))
                dn2[s, rows, on_lane(n)] = d
                plain = plain + d
                cross = cross + d * off
            acc[0, rows, :] = acc[0, rows, :] + plain
            acc[1, rows, :] = acc[1, rows, :] + cross

    def second_back_pair(i, carry):
        s = 2 * i
        activation_back(s + 1, dm)
        norm_back(s, dh)
        activation_back(jnp.minimum(s + 2, slots - 1), dh)
        norm_back(s + 1, dm)
        return carry

    activation_back(0, dh)
    lax.fori_loop(0, slots // 2, second_back_pair, 0)
    rb[2, me, 0:2, :] = split_row(lane_sums(acc[0]))
    rb[2, me, 2:4, :] = split_row(lane_sums(acc[1]))
    spread_start(rb.at[2, me], rb.at[2, me], 3)
    spread_wait(rb.at[2, pl.ds(0, n_dev - 1)], 3)
    sums = jnp.sum(rb[2], axis=0)
    bias2_grad = join_row(sums[0:2])
    cross2 = join_row(sums[2:4])
    gain2_grad = cross2 * scale2
    grow2 = prm[2:3, :] * scale2
    rows8 = jnp.concatenate(
        [
            grow2,
            -grow2 * scale2 * gain2_grad * (1.0 / total),
            -grow2 * bias2_grad * (1.0 / total),
            jnp.zeros((5, EXP), F32),
        ],
        axis=0,
    )
    for i in range(3):
        tab[TAPS + i] = column(rows8, i, EXP)

    for t in range(TAPS):
        acc[t] = jnp.zeros((EXP, LANES), F32)
    small[1] = jnp.zeros((IN, EXP), F32)
    small[2] = jnp.zeros((IN, EXP), F32)

    def taps_back_slot(s, carry):
        def frames_step(j, carry):
            rows = pl.ds(pl.multiple_of(8 * j, 8), 8)
            k1, k2, k3 = (tab[TAPS + i, rows, :] for i in range(3))
            for half in range(2):
                grads = []
                for k in range(HALF_W):
                    where = on_lane(half * HALF_W + k)
                    grads.append(k1 * dn2[s, rows, where] + k2 * a2[s, rows, where] + k3)
                for k in range(HALF_W):
                    where = on_lane(half * HALF_W + k)
                    dn2[s, rows, where] = grads[k]
                    dm[rows, where] = msk[1, s, :, where] * from_after(grads, k, half)
                    dp[rows, where] = msk[0, s, :, where] * from_before(grads, k, half)
            return carry

        def bins_tile(j):
            rows = pl.ds(pl.multiple_of(8 * j, 8), 8)
            out = [None] * WIDE
            wt = [tab[t, rows, :] for t in range(TAPS)]
            for k in range(HALF_W):
                mix = [[], [], []]
                us, hs = [], []
                for half in range(2):
                    where = on_lane(half * HALF_W + k)
                    moved = [dm[rows, where], dn2[s, rows, where], dp[rows, where]]
                    for q in range(3):
                        mix[q].append(wt[q] * moved[0] + wt[3 + q] * moved[1] + wt[6 + q] * moved[2])
                    v = v1[s, rows, where]
                    u = 1.0 + jnp.tanh(v)
                    us.append(u)
                    hs.append(v * u)
                left = later_bin(*mix[0])
                right = earlier_bin(*mix[2])
                for half in range(2):
                    out[half * HALF_W + k] = (left[half] + mix[1][half] + right[half]) * (
                        us[half] + hs[half] * (2.0 - us[half])
                    )
            return out

        def bins_step(j, carry):
            rows = pl.ds(pl.multiple_of(16 * j, 16), 16)
            low_rows = pl.ds(pl.multiple_of(EXP + 16 * j, 16), 16)
            for n, pair in enumerate(zip(bins_tile(2 * j), bins_tile(2 * j + 1))):
                high, low = halves(jnp.concatenate(pair, axis=0))
                hh[s, rows, on_lane(n)] = high
                hh[s, low_rows, on_lane(n)] = low
            return carry

        def taps_step(j, carry):
            rows = tile_rows(j)
            sums = [zero_tile] * TAPS
            for k in range(HALF_W):
                hs = []
                for half in range(2):
                    v = v1[s, rows, on_lane(half * HALF_W + k)]
                    hs.append(v + v * jnp.tanh(v))
                near = [earlier_bin(*hs), hs, later_bin(*hs)]
                for half in range(2):
                    where = on_lane(half * HALF_W + k)
                    moved = [dm[rows, where], dn2[s, rows, where], dp[rows, where]]
                    for q in range(3):
                        for p in range(3):
                            sums[3 * p + q] = sums[3 * p + q] + moved[p] * near[q][half]
            for t in range(TAPS):
                acc[t, rows, :] = acc[t, rows, :] + sums[t]
            return carry

        lax.fori_loop(0, EXP // 8, frames_step, 0, unroll=9)
        lax.fori_loop(0, EXP // 16, bins_step, 0, unroll=True)
        for j in range(EXP // 8):
            taps_step(j, 0)
        main = nt(xs[s, 0:64, :], hh[s, 0:EXP, :])
        main = main[0:32] + main[32:64] + nt(xs[s, 0:32, :], hh[s, EXP:, :])
        small[1] = small[1] + 0.5 * main[0:IN]
        small[2, 0:8, :] = small[2, 0:8, :] + 0.5 * main[IN:32]
        return carry

    lax.fori_loop(0, slots, taps_back_slot, 0)

    stacked = [small[0], small[1]]
    cross1 = jnp.sum(small[1] * weight, axis=0, keepdims=True)
    rb[3, me, 0:2, :] = split_row(small[2, 0:1, :])
    rb[3, me, 2:4, :] = split_row(cross1)
    tail = [lane_sums(acc[t]) for t in range(TAPS)]
    tail.append(excite_bias_grad)
    tail.append(jnp.concatenate([reduce_bias_grad, jnp.zeros((1, EXP - SQZ), F32)], axis=1))
    tail.append(jnp.zeros((5, EXP), F32))
    stacked.append(jnp.concatenate(tail, axis=0))
    for part in (excite_grad, reduce_grad):
        stacked.append(jnp.concatenate([part, jnp.zeros((8 - SQZ, EXP), F32)], axis=0))
    stacked = jnp.concatenate(stacked, axis=0)
    n_heads = 10
    for i in range(n_heads):
        bulk[i] = stacked[8 * i : 8 * i + 8, :LANES]
    ends = [stacked[8 * i : 8 * i + 8, LANES:] for i in range(n_heads)]
    bulk[n_heads] = jnp.concatenate(ends[:8], axis=1)
    bulk[n_heads + 1] = jnp.concatenate(ends[8:] + [jnp.zeros((8, LANES - 16 * (n_heads - 8)), F32)], axis=1)
    for i in range(n_heads + 2, BULK):
        bulk[i] = zero_tile
    each = BULK // GROUP
    base = lax.div(me, GROUP) * GROUP
    place = lax.rem(me, GROUP)

    def group_copy(source, target, index, step):
        return pltpu.make_async_remote_copy(
            src_ref=source, dst_ref=target, send_sem=r_send.at[index], recv_sem=r_recv.at[index],
            device_id=device(base + lax.rem(place + step, GROUP)), device_id_type=MESH,
        )

    for step in range(1, GROUP):
        other = lax.rem(place + step, GROUP)
        group_copy(bulk.at[pl.ds(each * other, each)], bulk_in.at[place], 4, step).start()
    bulk_in[place] = bulk[pl.ds(each * place, each)]
    spread_start(rb.at[3, me], rb.at[3, me], 7)
    done = group_copy(bulk_in.at[pl.ds(0, GROUP - 1)], bulk_in.at[pl.ds(0, GROUP - 1)], 4, 1)
    done.wait_send()
    done.wait_recv()
    bulk_all[me] = jnp.sum(bulk_in[...], axis=0)
    spread_start(bulk_all.at[me], bulk_all.at[me], 5)
    spread_wait(rb.at[3, pl.ds(0, n_dev - 1)], 7)
    sums = jnp.sum(rb[3], axis=0)
    bias1_grad = join_row(sums[0:2])
    gain1_grad = scale1 * join_row(sums[2:4])
    lean1 = scale1 * gain1_grad * (1.0 / total)

    for step in range(1, QUADS):
        def o_done(s, carry, step=step):
            o_copy(step, s).wait_send()
            x_copy(step, s).wait_send()
            c_copy(step, s).wait_send()
            return carry

        lax.fori_loop(0, slots, o_done, 0)
    grown = 0.5 * weight * grow1
    grown_high = grown.astype(BF16)
    grown_both = jnp.concatenate([grown_high.astype(F32), grown - grown_high.astype(F32)], axis=0).astype(BF16)
    lean_map = -2.0 * nt(grown * lean1, weight, FULL)
    flat_col = -2.0 * jnp.sum(grown * (bias1_grad * (1.0 / total)), axis=1, keepdims=True)
    side = jnp.concatenate([lean_map, flat_col, jnp.zeros((IN, 7), F32)], axis=1)
    side_high = side.astype(BF16).astype(F32)
    wlow[...] = jnp.concatenate([side_high, side_high, side - side_high], axis=1).astype(BF16)

    def last_slot(s, carry):
        main = nn(grown_both, hh[s, 0:EXP, :])
        main = main[:IN] + main[IN:] + nn(grown_high, hh[s, EXP:, :]) + nn(wlow[...], xs[s])
        for n in range(WIDE):
            place_back(xq, s, n, c3[s, :, on_lane(n)] + main[:, n * LANES : (n + 1) * LANES])
        for step in range(1, QUADS):
            g_copy(step, s).start()
        return carry

    lax.fori_loop(0, slots, last_slot, 0)
    own_g = pltpu.make_async_copy(xq.at[space], ing.at[pl.ds(slots * space, slots)], own_sem.at[3])
    own_g.start()

    spread_wait(bulk_all.at[pl.ds(0, n_dev - 1)], 5)
    summed = []
    for i in range(n_heads + 2):
        tile = zero_tile
        for g in range(n_dev // GROUP):
            tile = tile + bulk_all[g * GROUP + i // each, i % each]
        summed.append(tile)

    def row_tile(i):
        rest = summed[n_heads + i // 8][:, 16 * (i % 8) : 16 * (i % 8) + 16]
        return jnp.concatenate([summed[i], rest], axis=1)

    project_grad = jnp.concatenate([row_tile(i) for i in range(3)], axis=0)
    expand_cross = jnp.concatenate([row_tile(i) for i in range(3, 6)], axis=0)
    depth_tiles = jnp.concatenate([row_tile(6), row_tile(7)], axis=0)
    excite_tile = row_tile(8)
    reduce_tile = row_tile(9)
    expand_grad = grow1 * (expand_cross - lean1 * moment_w)
    zero_rows = jnp.zeros((16, EXP), F32)
    gs_out[0] = expand_grad
    gs_out[1] = project_grad
    gs_out[2] = jnp.concatenate([reduce_tile, zero_rows], axis=0)
    gs_out[3] = jnp.concatenate([excite_tile, zero_rows], axis=0)
    row16 = lax.broadcasted_iota(jnp.int32, (16, EXP), 0)
    gs_out[4] = jnp.concatenate([jnp.where(row16 < TAPS, depth_tiles, 0.0), zero_rows[:8]], axis=0)
    vr_out[...] = jnp.concatenate(
        [
            gain1_grad,
            bias1_grad,
            gain2_grad,
            bias2_grad,
            jnp.concatenate([gain3_grad, jnp.zeros((1, EXP - LANES), F32)], axis=1),
            jnp.concatenate([bias3_grad, jnp.zeros((1, EXP - LANES), F32)], axis=1),
            depth_tiles[TAPS + 1 : TAPS + 2],
            depth_tiles[TAPS : TAPS + 1],
        ],
        axis=0,
    )

    mine = jnp.minimum(place, 4)
    grad = gs_out[mine]
    turned = (mine == 1) | (mine == 2)
    small[...] = jnp.zeros(small.shape, F32)
    small[0, :, :IN] = in_st[0]
    small[1, :, :IN] = jnp.transpose(in_st[1])
    small[2, :SQZ, :SQZ] = jnp.transpose(sq_st[:, 0, :])
    small[3, :SQZ, :SQZ] = sq_st[:, 1, :]
    small[4, :TAPS, :TAPS] = tap_st[...]
    old_big = big[mine]
    old_big = jnp.where(turned, jnp.transpose(old_big), old_big)
    big_m = DECAY * old_big + FRESH * tn(grad, grad, FULL)
    small_m = DECAY * small[mine][:, :IN] + FRESH * nt(grad, grad, FULL)
    big_eye = (
        lax.broadcasted_iota(jnp.int32, (EXP, EXP), 0) == lax.broadcasted_iota(jnp.int32, (EXP, EXP), 1)
    ).astype(F32)
    small_eye = eye24.astype(F32)
    big_c = 2.5 * lax.rsqrt(jnp.sum(jnp.sum(big_m * big_m, axis=0, keepdims=True), axis=1, keepdims=True))
    small_c = 2.5 * lax.rsqrt(jnp.sum(jnp.sum(small_m * small_m, axis=0, keepdims=True), axis=1, keepdims=True))
    big_m = big_c * big_m
    small_m = small_c * small_m
    direction = jnp.sqrt(jnp.sqrt(big_c)) * grad
    small_h = jnp.sqrt(jnp.sqrt(small_c)) * small_eye

    def root_step(i, carry):
        big_m, small_m, direction, small_h = carry
        big_k = 1.25 * big_eye - 0.25 * big_m
        small_k = 1.25 * small_eye - 0.25 * small_m
        direction = nn(direction, big_k, MID)
        small_h = nn(small_h, small_k, MID)
        big_k = nn(big_k, big_k, MID)
        small_k = nn(small_k, small_k, MID)
        big_k = nn(big_k, big_k, MID)
        small_k = nn(small_k, small_k, MID)
        return nn(big_k, big_m, MID), nn(small_k, small_m, MID), direction, small_h

    _, _, direction, small_h = lax.fori_loop(
        0, ROOT_ITERS, root_step, (big_m, small_m, direction, small_h)
    )
    direction = nn(small_h, direction, FULL)
    short = jnp.where(mine < 2, float(IN), jnp.where(mine == 4, float(TAPS), float(SQZ)))
    lead = jnp.where(turned, float(EXP), short)
    power = jnp.sum(jnp.sum(direction * direction, axis=0, keepdims=True), axis=1, keepdims=True)
    power = power / jnp.full((1, 1), short * float(EXP), F32)
    step_size = STEP_FRACTION * lax.rsqrt(jnp.full((1, 1), lead, F32)) * lax.rsqrt(power + 1e-06)
    small[0] = weight
    small[1] = w_pro_t[...]
    for i, source in ((2, w_red_t), (3, w_exc), (4, w_dep)):
        small[i] = jnp.zeros((IN, EXP), F32)
        small[i, : source.shape[0], :] = source[...]
    nws[place] = small[mine] - step_size * direction
    for step in range(1, GROUP):
        group_copy(nws.at[place], nws.at[place], 6, step).start()
    done = group_copy(nws.at[pl.ds(0, GROUP - 1)], nws.at[pl.ds(0, GROUP - 1)], 6, 1)
    done.wait_send()
    done.wait_recv()
    nw_out[...] = nws[0:5]

    for step in range(1, QUADS):
        def all_done(s, carry, step=step):
            o_copy(step, s).wait_recv()
            g_copy(step, s).wait()
            return carry

        lax.fori_loop(0, slots, all_done, 0)
    own_o.wait()
    own_g.wait()


def finish_kernel(
    gs, nw, vr, big, in_st, sq_st, tap_st, vec, vec_m, field_a, field_b,
    out, ing, ge, gd, gr_t, gx, gp_t, ne, nd, nr_t, nx, np_t, big_new, in_new, sq_new, tap_new, vg, vm, vn, held, sem,
):
    fields = ((field_a, out), (field_b, ing))
    loads = [pltpu.make_async_copy(source, held.at[i], sem.at[i]) for i, (source, _) in enumerate(fields)]
    stores = [pltpu.make_async_copy(held.at[i], target, sem.at[i]) for i, (_, target) in enumerate(fields)]
    for load in loads:
        load.start()
    ge[...], gp_t[...], gr_t[...], gx[...], gd[...] = gs[0], gs[1], gs[2, :SQZ], gs[3, :SQZ], gs[4, :TAPS]
    ne[...], np_t[...], nr_t[...], nx[...], nd[...] = nw[0], nw[1], nw[2, :SQZ], nw[3, :SQZ], nw[4, :TAPS]
    start = 0
    for i, width in enumerate(PARTS):
        vg[pl.ds(start, width)] = vr[i : i + 1, :width].reshape(width)
        start = start + width
    grads = vg[...]
    moments = DECAY * vec_m[...] + FRESH * grads * grads
    vm[...] = moments
    vn[...] = vec[...] - VECTOR_RATE * grads / (jnp.sqrt(moments) + 1e-08)
    for load, store in zip(loads, stores):
        load.wait()
        store.start()
    for i in range(5):
        grad = gs[i]
        big_new[i] = DECAY * big[i] + FRESH * tn(grad, grad, FULL)
        inner = FRESH * nt(grad, grad, FULL)
        if i < 2:
            in_new[i] = DECAY * in_st[i] + inner
        elif i < 4:
            sq_new[:, i - 2, :] = DECAY * sq_st[:, i - 2, :] + inner[:SQZ, :SQZ]
        else:
            tap_new[...] = DECAY * tap_st[...] + inner[:TAPS, :TAPS]
    for store in stores:
        store.wait()


def on_device(
    n_dev, n_space,
    features, cotangent, segment_ids, w_expand, w_depth, w_reduce, w_excite, w_project,
    vector_params, vector_moments, big_stats, in_stats, sq_stats, tap_stats,
):
    slot_count = features.shape[0]
    slots = slot_count // QUADS
    n_pos = slot_count * (n_dev // n_space) * FRAMES * BINS
    vm = pl.BlockSpec(memory_space=pltpu.VMEM)
    sq_rows = sq_stats.transpose(1, 0, 2)
    hbm = pl.BlockSpec(memory_space=pl.ANY)
    grid_shape = jax.ShapeDtypeStruct((slot_count, ROWS, LANES), F32)
    wide = WIDE * LANES
    vmem = pltpu.VMEM
    dma = pltpu.SemaphoreType.DMA
    out, ing, gs, nw, vr = pl.pallas_call(
        functools.partial(block_kernel, n_dev, n_space, slots, n_pos),
        out_shape=(
            grid_shape,
            grid_shape,
            jax.ShapeDtypeStruct((5, IN, EXP), F32),
            jax.ShapeDtypeStruct((5, IN, EXP), F32),
            jax.ShapeDtypeStruct((8, EXP), F32),
        ),
        in_specs=[hbm, hbm] + [vm] * 11,
        out_specs=(hbm, hbm, vm, vm, vm),
        scratch_shapes=[
            vmem((QUADS, slots, ROWS, LANES), F32),
            vmem((QUADS, slots, ROWS, LANES), F32),
            vmem((QUADS, slots, ROWS, LANES), F32),
            vmem((slots, 96, wide), BF16),
            vmem((slots, IN, wide), F32),
            vmem((slots, IN, wide), F32),
            vmem((slots, EXP, wide), F32),
            vmem((slots, EXP, wide), F32),
            vmem((slots, 2 * EXP, wide), BF16),
            vmem((slots, EXP, wide), F32),
            vmem((EXP, wide), F32),
            vmem((EXP, wide), F32),
            vmem((EXP, wide), F32),
            vmem((slots, IN, wide), F32),
            vmem((slots, slots * REGIONS, wide), BF16),
            vmem((slots, 256, wide), BF16),
            vmem((TAPS + 3, EXP, LANES), F32),
            vmem((2, slots, 8, wide), F32),
            vmem((REGIONS, slots, 8, wide), F32),
            vmem((TAPS, EXP, LANES), F32),
            vmem((EXP, 96), BF16),
            vmem((IN, 96), BF16),
            vmem((8, EXP), F32),
            vmem((5, IN, EXP), F32),
            vmem((slots * REGIONS, EXP), F32),
            vmem((slots, REGIONS, EXP), F32),
            vmem((slots, REGIONS, EXP), F32),
            vmem((BULK, 8, LANES), F32),
            vmem((GROUP, BULK // GROUP, 8, LANES), F32),
            vmem((n_dev, BULK // GROUP, 8, LANES), F32),
            vmem((n_dev, 8, LANES), F32),
            vmem((4, n_dev, 4, LANES), F32),
            vmem((GROUP, IN, EXP), F32),
            vmem((IN, LANES), F32),
            dma((QUADS,)),
        ]
        + [dma((QUADS, slots))] * 8
        + [dma((8,)), dma((8,)), dma((4,))],
        compiler_params=pltpu.CompilerParams(
            collective_id=0, has_side_effects=True, vmem_limit_bytes=60 << 20
        ),
    )(
        features.reshape(slot_count, ROWS, LANES),
        cotangent.reshape(slot_count, ROWS, LANES),
        segment_ids, w_expand, w_depth, w_reduce.T, w_excite, w_project.T, vector_params,
        big_stats, in_stats, sq_rows, tap_stats,
    )
    shape = jax.ShapeDtypeStruct
    (
        out, ing, ge, gd, gr_t, gx, gp_t, ne, nd, nr_t, nx, np_t, big_new, in_new, sq_new, tap_new, vg, vm_new, vn
    ) = pl.pallas_call(
        finish_kernel,
        out_shape=(grid_shape, grid_shape) + tuple(
            shape(dims, F32)
            for dims in [(IN, EXP), (TAPS, EXP), (SQZ, EXP), (SQZ, EXP), (IN, EXP)] * 2
            + [(5, EXP, EXP), (2, IN, IN), (SQZ, 2, SQZ), (TAPS, TAPS)]
            + [vector_params.shape] * 3
        ),
        in_specs=[vm] * 9 + [hbm] * 2,
        out_specs=(hbm, hbm) + (vm,) * 17,
        scratch_shapes=[vmem((2,) + grid_shape.shape, F32), dma((2,))],
        compiler_params=pltpu.CompilerParams(vmem_limit_bytes=60 << 20),
    )(gs, nw, vr, big_stats, in_stats, sq_rows, tap_stats, vector_params, vector_moments, out, ing)
    return (
        out.reshape(features.shape), ing.reshape(features.shape),
        ge, gd, gr_t.T, gx, gp_t.T, ne, nd, nr_t.T, nx, np_t.T,
        big_new, in_new, sq_new.transpose(1, 0, 2), tap_new, vg, vm_new, vn,
    )


def solution(mesh):
    field = P("dp", None, "space", None)
    return jax.shard_map(
        functools.partial(on_device, mesh.shape["dp"] * mesh.shape["space"], mesh.shape["space"]),
        mesh=mesh,
        in_specs=(field, field, P("dp", None)) + (P(),) * 11,
        out_specs=(field, field) + (P(),) * 17,
        check_vma=False,
    )
```

```python
import functools
import math

import jax
import jax.numpy as jnp
from jax import lax
from jax.experimental import pallas as pl
from jax.experimental.pallas import tpu as pltpu
from jax.sharding import PartitionSpec as P

IN = 24
EXP = 144
SQZ = 6
TAPS = 9
FRAMES = 96
BINS = 16
REGIONS = 4
QUADS = 4
ROOT_ITERS = 10
NORM_EPS = 0.001
DECAY = 0.9
FRESH = 1.0 - DECAY
STEP_FRACTION = 0.5
VECTOR_RATE = 0.15
PARTS = (EXP, EXP, EXP, EXP, IN, IN, SQZ, EXP)

LANES = 128
HALF_W = 6
WIDE = 2 * HALF_W
ROWS = IN * 3
GROUP = 8

F32 = jnp.float32
BF16 = jnp.bfloat16
FULL = lax.Precision.HIGHEST
MID = lax.Precision.HIGH
MESH = pl.DeviceIdType.MESH


def mm(left, right, dims, precision=None):
    return lax.dot_general(
        left, right, ((dims[:1], dims[1:]), ((), ())), precision=precision, preferred_element_type=F32
    )


def nn(left, right, precision=None):
    return mm(left, right, (1, 0), precision)


def nt(left, right, precision=None):
    return mm(left, right, (1, 1), precision)


def tn(left, right, precision=None):
    return mm(left, right, (0, 0), precision)


def halves(value):
    high = value.astype(BF16)
    return high, (value - high.astype(F32)).astype(BF16)


def column(rows, index, width):
    pick = (lax.broadcasted_iota(jnp.int32, (rows.shape[0], LANES), 0) == index).astype(F32)
    return tn(rows, pick, FULL)[:width]


def lane_sums(table):
    return nt(jnp.ones((8, table.shape[1]), F32), table, FULL)[0:1]


def split_row(row):
    return jnp.concatenate(
        [row[:, :LANES], jnp.concatenate([row[:, LANES:], jnp.zeros((1, 2 * LANES - EXP), F32)], axis=1)], axis=0
    )


def join_row(pair):
    return jnp.concatenate([pair[0:1], pair[1:2, : EXP - LANES]], axis=1)


def tile_quad(n):
    return 2 * ((n % HALF_W) // 3) + n // HALF_W


def on_lane(n):
    return pl.ds(n * LANES, LANES)


def block_kernel(
    n_dev, n_space, slots, n_pos,
    feat, cot, ids_ref, w_exp, w_dep, w_red_t, w_exc, w_pro_t, vec, big, in_st, sq_st, tap_st,
    out, ing, gs_out, nw_out, vr_out,
    xloc, xq, xs, v1, a2, hh, dn2, dh, dm, dp, a3, hot, dcat, prods, tab, msk, reg, acc, w1t, wlow, prm,
    small, pooled, gates, bulk, bulk_in, bulk_all, rb1, rb, nws, fold,
    loc_sem, x_send, x_recv, c_send, c_recv, o_send, o_recv, g_send, g_recv,
    r_send, r_recv, own_sem,
):
    space = lax.axis_index("space")
    me = lax.axis_index("dp") * n_space + space
    n_loc = float(slots * FRAMES * BINS)
    total = float(n_pos)

    def device(index):
        return (lax.div(index, n_space), lax.rem(index, n_space))

    def peer(step):
        return lax.rem(space + step, QUADS)

    def space_device(step):
        return (lax.axis_index("dp"), peer(step))

    barrier = pltpu.get_barrier_semaphore()

    def greet(step, carry):
        pl.semaphore_signal(
            barrier, inc=1, device_id=device(lax.rem(me + step, n_dev)), device_id_type=MESH
        )
        return carry

    lax.fori_loop(1, n_dev, greet, 0)
    loads = [
        pltpu.make_async_copy(feat.at[pl.ds(slots * q, slots)], xloc.at[q], loc_sem.at[q]) for q in range(QUADS)
    ]
    for load in loads:
        load.start()
    own_x = pltpu.make_async_copy(feat.at[pl.ds(slots * space, slots)], xq.at[space], own_sem.at[0])
    own_c = pltpu.make_async_copy(cot.at[pl.ds(slots * space, slots)], xloc.at[space], own_sem.at[1])
    own_x.start()

    for load in loads:
        load.wait()
    first = jnp.concatenate([xloc[0, 0, pl.ds(k, IN, stride=3), :] for k in range(3)], axis=1)
    shift_col = nn(first, jnp.ones((3 * LANES, LANES), F32), FULL) * (1.0 / (3 * LANES))
    shift_row = nt(jnp.ones((8, 3 * LANES), F32), first, FULL)[0:1] * (1.0 / (3 * LANES))
    one_rows = (lax.broadcasted_iota(jnp.int32, (8, LANES), 0) == 0).astype(F32)

    def gram_step(s, gram):
        parts = []
        for q in range(QUADS):
            for k in range(3):
                parts.append(
                    jnp.concatenate([xloc[q, s, pl.ds(k, IN, stride=3), :] - shift_col, one_rows], axis=0)
                )
        high, low = halves(jnp.concatenate(parts, axis=1))
        both = jnp.concatenate([high, low], axis=0)
        return gram + nt(both, both)

    gram = lax.fori_loop(0, slots, gram_step, jnp.zeros((64, 64), F32), unroll=True)
    gram = gram[:32, :32] + gram[32:, :32] + gram[:32, 32:] + gram[32:, 32:]
    off_row = gram[IN : IN + 1, :IN] * (1.0 / n_loc)
    off_col = gram[:IN, IN : IN + 1] * (1.0 / n_loc)
    local_m2 = gram[:IN, :IN] - n_loc * off_col * off_row
    fold[...] = jnp.zeros((IN, LANES), F32)
    fold[:, :IN] = local_m2
    packed = jnp.zeros((6, LANES), F32)
    for g in range(4):
        piece = fold[pl.ds(g, 6, stride=4), :]
        packed = packed + (pltpu.roll(piece, 32 * g, 1) if g else piece)
    rb1[me, 0:6, :] = packed
    rb1[me, 6:7, :] = jnp.concatenate([shift_row + off_row, jnp.zeros((1, LANES - IN), F32)], axis=1)
    rb1[me, 7:8, :] = jnp.zeros((1, LANES), F32)

    pl.semaphore_wait(barrier, n_dev - 1)

    def spread_start(source, target, index):
        def send(step, carry):
            pltpu.make_async_remote_copy(
                src_ref=source, dst_ref=target, send_sem=r_send.at[index], recv_sem=r_recv.at[index],
                device_id=device(lax.rem(me + step, n_dev)), device_id_type=MESH,
            ).start()
            return carry

        lax.fori_loop(1, n_dev, send, 0)

    def spread_wait(window, index):
        done = pltpu.make_async_remote_copy(
            src_ref=window, dst_ref=window, send_sem=r_send.at[index], recv_sem=r_recv.at[index],
            device_id=device(me), device_id_type=MESH,
        )
        done.wait_send()
        done.wait_recv()

    def quad_copy(source, target, send, recv, step, s):
        return pltpu.make_async_remote_copy(
            src_ref=source, dst_ref=target, send_sem=send.at[step, s], recv_sem=recv.at[step, s],
            device_id=space_device(step), device_id_type=MESH,
        )

    def x_copy(step, s):
        return quad_copy(feat.at[slots * peer(step) + s], xq.at[space, s], x_send, x_recv, step, s)

    def c_copy(step, s):
        return quad_copy(cot.at[slots * peer(step) + s], xloc.at[space, s], c_send, c_recv, step, s)

    def o_copy(step, s):
        return quad_copy(xq.at[peer(step), s], out.at[slots * space + s], o_send, o_recv, step, s)

    def g_copy(step, s):
        return quad_copy(xloc.at[peer(step), s], ing.at[slots * space + s], g_send, g_recv, step, s)

    base = lax.div(me, GROUP) * GROUP
    place = lax.rem(me, GROUP)

    def group_copy(source, target, index, step):
        return pltpu.make_async_remote_copy(
            src_ref=source, dst_ref=target, send_sem=r_send.at[index], recv_sem=r_recv.at[index],
            device_id=device(base + lax.rem(place + step, GROUP)), device_id_type=MESH,
        )

    def bulk_scatter(which, heads, index):
        for i in range(GROUP):
            bulk[which, i] = heads[i][:, :LANES] if i < len(heads) else jnp.zeros((8, LANES), F32)
        ends = [head[:, LANES:] for head in heads]
        rest = jnp.zeros((8, LANES - (EXP - LANES) * len(heads)), F32)
        bulk[which, len(heads)] = jnp.concatenate(ends + [rest], axis=1)
        for step in range(1, GROUP):
            other = lax.rem(place + step, GROUP)
            group_copy(bulk.at[which, other], bulk_in.at[which, place], index, step).start()
        bulk_in[which, place] = bulk[which, place]

    def bulk_gather(which, index, out_index):
        window = bulk_in.at[which, pl.ds(0, GROUP - 1)]
        done = group_copy(window, window, index, 1)
        done.wait_send()
        done.wait_recv()
        bulk_all[which, me] = jnp.sum(bulk_in[which], axis=0)
        spread_start(bulk_all.at[which, me], bulk_all.at[which, me], out_index)

    def bulk_tiles(which, count, out_index):
        spread_wait(bulk_all.at[which, pl.ds(0, n_dev - 1)], out_index)
        summed = []
        for i in range(count + 1):
            tile = bulk_all[which, i]
            for g in range(1, n_dev // GROUP):
                tile = tile + bulk_all[which, g * GROUP + i]
            summed.append(tile)
        width = EXP - LANES
        return [
            jnp.concatenate([summed[i], summed[count][:, width * i : width * (i + 1)]], axis=1)
            for i in range(count)
        ]

    spread_start(rb1.at[me], rb1.at[me], 0)

    def x_start(s, carry):
        for step in range(1, QUADS):
            x_copy(step, s).start()
        return carry

    lax.fori_loop(0, slots, x_start, 0)

    lane = lax.broadcasted_iota(jnp.int32, (8, LANES), 1)
    low_bin = lax.rem(lane, 8) == 0
    high_bin = lax.rem(lane, 8) == 7
    first_row = lane < 8
    second_row = (lane >= 8) & (lane < 16)
    last_row = lane >= LANES - 8
    zero_tile = jnp.zeros((8, LANES), F32)

    half_lanes = HALF_W * LANES
    own_ids = ids_ref[pl.ds(pl.multiple_of(slots * space, 8), slots), :].astype(F32)
    spread = (
        lax.broadcasted_iota(jnp.int32, (FRAMES, half_lanes), 1) // 8
        == lax.broadcasted_iota(jnp.int32, (FRAMES, half_lanes), 0)
    )
    wide_ids = nn(own_ids.astype(BF16), spread.astype(F32).astype(BF16))
    wide_lane = lax.broadcasted_iota(jnp.int32, (slots, half_lanes), 1)
    before = pltpu.roll(wide_ids, 8, 1)
    after = pltpu.roll(wide_ids, half_lanes - 8, 1)
    from_ok = jnp.where((before == wide_ids) & (wide_lane >= 8), 1.0, 0.0)
    to_ok = jnp.where((after == wide_ids) & (wide_lane < half_lanes - 8), 1.0, 0.0)
    def both_halves(rows):
        turned = [pltpu.roll(rows[:, n * LANES : (n + 1) * LANES], 8, 1) for n in range(HALF_W)]
        return jnp.concatenate([rows] + turned, axis=1)

    marks = [both_halves(rows) for rows in (from_ok, to_ok)]
    regions = [both_halves((wide_ids == float(r)).astype(F32)) for r in range(REGIONS)]
    region_ids = both_halves(wide_ids)
    for s in range(slots):
        for i in range(2):
            msk[i, s] = jnp.broadcast_to(marks[i][s : s + 1], (8, WIDE * LANES))
        reg[s] = jnp.broadcast_to(region_ids[s : s + 1], (8, WIDE * LANES)).astype(jnp.int32)
    row_index = lax.broadcasted_iota(jnp.int32, (slots * REGIONS, WIDE * LANES), 0)
    counts = jnp.zeros((slots * REGIONS, 1), F32)
    for s in range(slots):
        row = jnp.zeros((slots * REGIONS, WIDE * LANES), F32)
        for r in range(REGIONS):
            row = jnp.where(row_index == REGIONS * s + r, regions[r][s : s + 1], row)
        counts = counts + jnp.sum(row, axis=1, keepdims=True)
        hot[s] = row.astype(BF16)
    taps = w_dep[...]
    for t in range(TAPS):
        tab[t] = column(taps, t, EXP)

    start = 0
    prm[...] = jnp.zeros((8, EXP), F32)
    for i, width in enumerate(PARTS):
        prm[i : i + 1, :width] = vec[pl.ds(start, width)].reshape(1, width)
        start = start + width

    spread_wait(rb1.at[pl.ds(0, n_dev - 1)], 0)
    gathered = jnp.sum(rb1[...], axis=0)
    means = rb1[:, 6, :]
    mean_row = jnp.sum(means, axis=0, keepdims=True) * (1.0 / n_dev)
    apart = means - mean_row
    between = tn(apart, apart, FULL)[:IN, :IN]
    for g in range(4):
        piece = gathered[0:6]
        piece = pltpu.roll(piece, LANES - 32 * g, 1) if g else piece
        fold[pl.ds(g, 6, stride=4), :] = piece
    moment = fold[:, :IN] + n_loc * between
    eye24 = (
        lax.broadcasted_iota(jnp.int32, (IN, IN), 0) == lax.broadcasted_iota(jnp.int32, (IN, IN), 1)
    )
    mean_col = nn(jnp.where(eye24, mean_row[:, :IN], 0.0), jnp.ones((IN, LANES), F32), FULL)
    weight = w_exp[...]
    moment_w = nn(moment, weight, FULL)
    scale1 = lax.rsqrt(jnp.sum(moment_w * weight, axis=0, keepdims=True) * (1.0 / total) + NORM_EPS)
    grow1 = prm[0:1, :] * scale1
    shaped = jnp.concatenate(
        [weight * (0.5 * grow1), 0.5 * prm[1:2, :], jnp.zeros((7, EXP), F32)], axis=0
    )
    shaped_high = shaped.astype(BF16).astype(F32)
    w1t[...] = jnp.transpose(
        jnp.concatenate([shaped_high, shaped_high, shaped - shaped_high], axis=0)
    ).astype(BF16)

    own_x.wait()
    for i in (0, 2, 3):
        acc[i] = jnp.zeros((EXP, LANES), F32)

    def fetch(quads, s, n):
        tile = quads[tile_quad(n), s, pl.ds(n % 3, IN, stride=3), :]
        return tile if n < HALF_W else pltpu.roll(tile, 8, 1)

    def add_to(quads, s, n, tile):
        tile = tile if n < HALF_W else pltpu.roll(tile, LANES - 8, 1)
        where = pl.ds(n % 3, IN, stride=3)
        quads[tile_quad(n), s, where, :] = quads[tile_quad(n), s, where, :] + tile

    def later_bin(low, high):
        return (
            pltpu.roll(jnp.where(low_bin, high, low), LANES - 1, 1),
            jnp.where(high_bin, 0.0, pltpu.roll(high, LANES - 1, 1)),
        )

    def earlier_bin(low, high):
        return (
            jnp.where(low_bin, 0.0, pltpu.roll(low, 1, 1)),
            pltpu.roll(jnp.where(high_bin, low, high), 1, 1),
        )

    def from_before(tiles, k, half):
        edge = first_row if half else last_row
        return pltpu.roll(jnp.where(edge, tiles[(k - 1) % HALF_W], tiles[k]), 8, 1)

    def from_after(tiles, k, half):
        edge = second_row if half else first_row
        return pltpu.roll(jnp.where(edge, tiles[(k + 1) % HALF_W], tiles[k]), LANES - 8, 1)

    def tile_rows(j, height=8):
        return pl.ds(height * j, height) if isinstance(j, int) else pl.ds(pl.multiple_of(height * j, height), height)

    def expand_slot(s):
        for n in range(WIDE):
            tile = fetch(xq, s, n)
            high, low = halves(jnp.concatenate([tile - mean_col, one_rows], axis=0))
            xs[s, 0:32, on_lane(n)] = high
            xs[s, 32:64, on_lane(n)] = low
            xs[s, 64:96, on_lane(n)] = high
        v1[s] = nn(w1t[...], xs[s])

    def x_arrived(s):
        for step in range(1, QUADS):
            x_copy(step, s).wait_recv()

    def forward_slot(s, carry):
        def bins_step(j, carry):
            rows = pl.ds(pl.multiple_of(8 * j, 8), 8)
            wt = [tab[t, rows, :] for t in range(TAPS)]
            for k in range(HALF_W):
                pair = []
                for half in range(2):
                    v = v1[s, rows, on_lane(half * HALF_W + k)]
                    pair.append(v + v * jnp.tanh(v))
                nxt = later_bin(*pair)
                prv = earlier_bin(*pair)
                for half in range(2):
                    for p, target in enumerate((dm, dh, dp)):
                        target[rows, on_lane(half * HALF_W + k)] = (
                            wt[3 * p] * prv[half] + wt[3 * p + 1] * pair[half] + wt[3 * p + 2] * nxt[half]
                        )
            return carry

        def frames_step(j, carry):
            rows = tile_rows(j)
            center = acc[3, rows, :]
            got, square = zero_tile, zero_tile
            for half in range(2):
                prior = [dm[rows, on_lane(half * HALF_W + k)] for k in range(HALF_W)]
                later = [dp[rows, on_lane(half * HALF_W + k)] for k in range(HALF_W)]
                for k in range(HALF_W):
                    where = on_lane(half * HALF_W + k)
                    value = (
                        dh[rows, where]
                        + msk[0, s, :, where] * from_before(prior, k, half)
                        + msk[1, s, :, where] * from_after(later, k, half)
                    )
                    a2[s, rows, where] = value
                    off = value - center
                    got = got + off
                    square = square + off * off
            acc[0, rows, :] = acc[0, rows, :] + got
            acc[2, rows, :] = acc[2, rows, :] + square
            return carry

        lax.fori_loop(0, EXP // 8, bins_step, 0, unroll=9)

        @pl.when(s < slots - 1)
        def _():
            x_arrived(s + 1)

        expand_slot(jnp.minimum(s + 1, slots - 1))
        for j in range(EXP // 8):
            frames_step(j, 0)

        @pl.when(s == 0)
        def _():
            acc[3] = nn(acc[0], jnp.ones((LANES, LANES), F32), FULL) * (1.0 / (FRAMES * BINS))

            def again(j, carry):
                rows = tile_rows(j)
                center = acc[3, rows, :]
                got, square = zero_tile, zero_tile
                for n in range(WIDE):
                    off = a2[0, rows, on_lane(n)] - center
                    got = got + off
                    square = square + off * off
                acc[0, rows, :] = got
                acc[2, rows, :] = square
                return carry

            lax.fori_loop(0, EXP // 8, again, 0, unroll=3)

        return carry

    x_arrived(0)
    expand_slot(0)

    lax.fori_loop(0, slots, forward_slot, 0)

    drift = lane_sums(acc[0]) * (1.0 / n_loc)
    rb[0, me, 0:2, :] = split_row(lane_sums(acc[3]) * (1.0 / LANES) + drift)
    rb[0, me, 2:4, :] = split_row(lane_sums(acc[2]) - n_loc * drift * drift)
    spread_start(rb.at[0, me], rb.at[0, me], 1)
    def c_start(t, carry):
        for step in range(1, QUADS):
            c_copy(step, t).start()
        return carry

    lax.fori_loop(0, slots, c_start, 0)
    own_c.start()
    spread_wait(rb.at[0, pl.ds(0, n_dev - 1)], 1)
    sums = jnp.sum(rb[0], axis=0)
    mean2 = sums[0:2] * (1.0 / n_dev)
    gaps = rb[0][:, 0:2, :] - mean2[None]
    spread2 = sums[2:4] + n_loc * jnp.sum(gaps * gaps, axis=0)
    scale2 = lax.rsqrt(join_row(spread2) * (1.0 / total) + NORM_EPS)
    mean2 = join_row(mean2)
    rows8 = jnp.concatenate(
        [mean2, 0.5 * prm[2:3, :] * scale2, 0.5 * prm[3:4, :], jnp.zeros((5, EXP), F32)], axis=0
    )
    for i in range(3):
        tab[TAPS + i] = column(rows8, i, EXP)

    pooled[...] = jnp.zeros((slots * REGIONS, EXP), F32)

    def activate(s):
        for j in range(EXP // 16):
            rows, low_rows = pl.ds(16 * j, 16), pl.ds(EXP + 16 * j, 16)
            center, grow, lift = (tab[TAPS + i, rows, :] for i in range(3))
            for n in range(WIDE):
                off = a2[s, rows, on_lane(n)] - center
                a2[s, rows, on_lane(n)] = off
                v = off * grow + lift
                high, low = halves(v + v * jnp.tanh(v))
                hh[s, rows, on_lane(n)] = high
                hh[s, low_rows, on_lane(n)] = low

    def pool(s):
        pooled[...] = pooled[...] + nt(hot[s], hh[s, 0:EXP, :]) + nt(hot[s], hh[s, EXP:, :])

    def activate_slot(s, carry):
        pool(s - 1)
        activate(s)
        return carry

    activate(0)
    lax.fori_loop(1, slots, activate_slot, 0)
    pool(slots - 1)

    per_count = 1.0 / counts
    mean_pool = pooled[...] * per_count
    squeeze = nt(mean_pool, w_red_t[...], FULL) + prm[6:7, :SQZ]
    squeeze_sig = jax.nn.sigmoid(squeeze)
    squeezed = squeeze * squeeze_sig
    gate = jax.nn.sigmoid(nn(squeezed, w_exc[...], FULL) + prm[7:8, :])
    for s in range(slots):
        gates[s] = gate[REGIONS * s : REGIONS * (s + 1)]

    def gated_weights(s):
        project = w_pro_t[...]
        rows = gates[s]
        return jnp.concatenate([project * rows[r : r + 1] for r in range(REGIONS)], axis=0)

    def region_tile(s, n):
        return jnp.concatenate([reg[s, :, on_lane(n)]] * (IN // 8), axis=0)

    def project_slot(s, carry):
        total_a, total_c = carry
        high, low = halves(gated_weights(s))
        body = nn(jnp.concatenate([high, low], axis=0), hh[s, 0:EXP, :])
        body = body[:96] + body[96:] + nn(high, hh[s, EXP:, :])
        for step in range(1, QUADS):
            c_copy(step, s).wait_recv()
        for n in range(WIDE):
            value = jnp.zeros((IN, LANES), F32)
            ids = region_tile(s, n)
            for r in range(REGIONS):
                value = jnp.where(ids == r, body[IN * r : IN * (r + 1), n * LANES : (n + 1) * LANES], value)
            a3[s, :, on_lane(n)] = value
            total_a = total_a + value
            upstream = fetch(xloc, s, n)
            total_c = total_c + upstream
        return total_a, total_c

    own_c.wait()
    zero24 = jnp.zeros((IN, LANES), F32)
    total_a, total_c = lax.fori_loop(0, slots, project_slot, (zero24, zero24))
    center3 = nn(total_a, jnp.ones((LANES, LANES), F32), FULL) * (1.0 / n_loc)

    def third_step(s, carry):
        square, cross = carry
        for n in range(WIDE):
            off = a3[s, :, on_lane(n)] - center3
            square = square + off * off
            cross = cross + off * fetch(xloc, s, n)
        return square, cross

    square3, cross3 = lax.fori_loop(0, slots, third_step, (zero24, zero24))

    def pad_row(row):
        return jnp.concatenate([row, jnp.zeros((1, LANES - IN), F32)], axis=1)

    rb[1, me] = jnp.concatenate(
        [
            pad_row(lane_sums(total_a) * (1.0 / n_loc)),
            pad_row(lane_sums(square3)),
            pad_row(lane_sums(total_c)),
            pad_row(lane_sums(cross3)),
        ],
        axis=0,
    )
    spread_start(rb.at[1, me], rb.at[1, me], 2)

    def region_parts(s):
        for n in range(WIDE):
            where = on_lane(n)
            ids = region_tile(s, n)
            masks = [ids == r for r in range(REGIONS)]
            upstream = fetch(xloc, s, n)
            off = a3[s, :, where] - center3
            high, low = halves(jnp.concatenate([jnp.where(mask, upstream, 0.0) for mask in masks], axis=0))
            dcat[s, 0:96, where] = high
            dcat[s, 128:224, where] = low
            high, low = halves(jnp.concatenate([jnp.where(mask, off, 0.0) for mask in masks], axis=0))
            dcat[s, 256:352, where] = high
            dcat[s, 352:448, where] = low
        dcat[s, 96:128, :] = hot[s]
        dcat[s, 224:256, :] = hot[s]

    def region_products(s):
        main = nt(dcat[s], hh[s, 0:EXP, :])
        rest = nt(jnp.concatenate([dcat[s, 0:96, :], dcat[s, 256:352, :]], axis=0), hh[s, EXP:, :])
        prods[0, s] = main[0:96] + main[128:224] + rest[:96]
        prods[1, s] = main[256:352] + main[352:448] + rest[96:]

    def region_slot(s, carry):
        region_products(s - 1)
        region_parts(s)
        return carry

    region_parts(0)
    lax.fori_loop(1, slots, region_slot, 0)
    region_products(slots - 1)
    spread_wait(rb.at[1, pl.ds(0, n_dev - 1)], 2)
    third = rb[1]
    sums = jnp.sum(third, axis=0)
    mean3 = sums[0:1] * (1.0 / n_dev)
    gaps = third[:, 0, :] - mean3
    spread3 = sums[1:2] + n_loc * jnp.sum(gaps * gaps, axis=0, keepdims=True)
    scale3 = lax.rsqrt(spread3 * (1.0 / total) + NORM_EPS)
    bias3_grad = sums[2:3]
    cross_sum = sums[3:4] + jnp.sum(third[:, 2, :] * gaps, axis=0, keepdims=True)
    gain3_grad = scale3 * cross_sum
    grow3 = prm[4:5, :LANES] * scale3
    rows8 = jnp.concatenate(
        [
            mean3,
            grow3,
            prm[5:6, :LANES],
            grow3 * bias3_grad * (1.0 / total),
            grow3 * scale3 * gain3_grad * (1.0 / total),
            jnp.zeros((3, LANES), F32),
        ],
        axis=0,
    )
    mean3_c, grow3_c, lift3_c, flat3_c, lean3_c = (column(rows8, i, IN) for i in range(5))
    flat3_c = -flat3_c - (center3 - mean3_c) * lean3_c

    grow3_w, lean3_w, flat3_w = (
        jnp.concatenate([tile, tile[:, : EXP - LANES]], axis=1) for tile in (grow3_c, lean3_c, flat3_c)
    )
    project = w_pro_t[...]
    sums_of_h = pooled[...]
    small[0] = jnp.zeros((IN, EXP), F32)
    gate_rows = []
    for s in range(slots):
        gp = small[0]
        for r in range(REGIONS):
            q = REGIONS * s + r
            part = (
                grow3_w * prods[0, s, IN * r : IN * (r + 1), :]
                - lean3_w * prods[1, s, IN * r : IN * (r + 1), :]
                + flat3_w * sums_of_h[q : q + 1]
            )
            gate_rows.append(jnp.sum(part * project, axis=0, keepdims=True))
            gp = gp + part * gate[q : q + 1]
        small[0] = gp
    dgate_rows = jnp.concatenate(gate_rows, axis=0)

    dpre_x = dgate_rows * gate * (1.0 - gate)
    excite_grad = tn(squeezed, dpre_x, FULL)
    excite_bias_grad = jnp.sum(dpre_x, axis=0, keepdims=True)
    dsqueezed = nt(dpre_x, w_exc[...], FULL)
    dpre_r = dsqueezed * squeeze_sig * (1.0 + squeeze * (1.0 - squeeze_sig))
    reduce_grad = tn(dpre_r, mean_pool, FULL)
    reduce_bias_grad = jnp.sum(dpre_r, axis=0, keepdims=True)
    dpool = nn(dpre_r, w_red_t[...], FULL) * per_count
    pooled[...] = 0.5 * dpool + 0.5 * gate * jnp.sum(project * flat3_w, axis=0, keepdims=True)

    side_rows = jnp.concatenate(
        [excite_bias_grad, jnp.concatenate([reduce_bias_grad, jnp.zeros((1, EXP - SQZ), F32)], axis=1)], axis=0
    )
    early = [small[0, 8 * i : 8 * i + 8, :] for i in range(3)] + [
        jnp.concatenate([part, jnp.zeros((8 - part.shape[0], EXP), F32)], axis=0)
        for part in (excite_grad, reduce_grad, side_rows)
    ]
    bulk_scatter(0, early, 4)

    acc[0] = jnp.zeros((EXP, LANES), F32)
    acc[1] = jnp.zeros((EXP, LANES), F32)

    grown_project = 0.5 * project * grow3_w
    lean_project = -0.5 * project * lean3_w

    def activation_back(s, target):
        rows = gates[s]
        high, low = halves(jnp.concatenate([grown_project * rows[r : r + 1] for r in range(REGIONS)], axis=0))
        lean_high, lean_low = halves(
            jnp.concatenate([lean_project * rows[r : r + 1] for r in range(REGIONS)], axis=0)
        )
        pool_high, pool_low = halves(pooled[...])
        left = jnp.concatenate([high, pool_high, high, pool_low], axis=0)
        target[...] = (
            tn(left, dcat[s, 0:256, :])
            + tn(jnp.concatenate([lean_high, lean_high], axis=0), dcat[s, 256:448, :])
            + tn(jnp.concatenate([low, lean_low], axis=0), jnp.concatenate([dcat[s, 0:96, :], dcat[s, 256:352, :]], axis=0))
        )

    def leave(s):
        for n in range(WIDE):
            off = a3[s, :, on_lane(n)] - mean3_c
            add_to(xq, s, n, off * grow3_c + lift3_c)

    def norm_back(s, source):
        for j in range(EXP // 8):
            rows = tile_rows(j)
            grow, lift = (tab[TAPS + i, rows, :] for i in (1, 2))
            plain, cross = zero_tile, zero_tile
            for n in range(WIDE):
                off = a2[s, rows, on_lane(n)]
                v = off * grow + lift
                u = 1.0 + jnp.tanh(v)
                d = source[rows, on_lane(n)] * (u + (v * u) * (2.0 - u))
                dn2[s, rows, on_lane(n)] = d
                plain = plain + d
                cross = cross + d * off
            acc[0, rows, :] = acc[0, rows, :] + plain
            acc[1, rows, :] = acc[1, rows, :] + cross

    def second_back_pair(i, carry):
        s = 2 * i
        activation_back(s + 1, dm)
        norm_back(s, dh)
        leave(s)
        activation_back(jnp.minimum(s + 2, slots - 1), dh)
        norm_back(s + 1, dm)
        leave(s + 1)
        return carry

    activation_back(0, dh)
    lax.fori_loop(0, slots // 2, second_back_pair, 0)
    rb[2, me, 0:2, :] = split_row(lane_sums(acc[0]))
    rb[2, me, 2:4, :] = split_row(lane_sums(acc[1]))
    spread_start(rb.at[2, me], rb.at[2, me], 3)

    def o_start(s, carry):
        for step in range(1, QUADS):
            o_copy(step, s).start()
        return carry

    lax.fori_loop(0, slots, o_start, 0)
    own_o = pltpu.make_async_copy(xq.at[space], out.at[pl.ds(slots * space, slots)], own_sem.at[2])
    own_o.start()
    spread_wait(rb.at[2, pl.ds(0, n_dev - 1)], 3)
    bulk_gather(0, 4, 5)
    sums = jnp.sum(rb[2], axis=0)
    bias2_grad = join_row(sums[0:2])
    cross2 = join_row(sums[2:4])
    gain2_grad = cross2 * scale2
    grow2 = prm[2:3, :] * scale2
    rows8 = jnp.concatenate(
        [
            grow2,
            -grow2 * scale2 * gain2_grad * (1.0 / total),
            -grow2 * bias2_grad * (1.0 / total),
            jnp.zeros((5, EXP), F32),
        ],
        axis=0,
    )
    for i in range(3):
        tab[TAPS + i] = column(rows8, i, EXP)

    for t in range(TAPS):
        acc[t] = jnp.zeros((EXP, LANES), F32)
    small[1] = jnp.zeros((IN, EXP), F32)
    small[2] = jnp.zeros((IN, EXP), F32)

    def taps_back_slot(s, carry):
        def frames_step(j, carry):
            rows = pl.ds(pl.multiple_of(8 * j, 8), 8)
            k1, k2, k3 = (tab[TAPS + i, rows, :] for i in range(3))
            for half in range(2):
                grads = []
                for k in range(HALF_W):
                    where = on_lane(half * HALF_W + k)
                    grads.append(k1 * dn2[s, rows, where] + k2 * a2[s, rows, where] + k3)
                for k in range(HALF_W):
                    where = on_lane(half * HALF_W + k)
                    dn2[s, rows, where] = grads[k]
                    dm[rows, where] = msk[1, s, :, where] * from_after(grads, k, half)
                    dp[rows, where] = msk[0, s, :, where] * from_before(grads, k, half)
            return carry

        def bins_tile(j):
            rows = pl.ds(pl.multiple_of(8 * j, 8), 8)
            out = [None] * WIDE
            wt = [tab[t, rows, :] for t in range(TAPS)]
            for k in range(HALF_W):
                mix = [[], [], []]
                us, hs = [], []
                for half in range(2):
                    where = on_lane(half * HALF_W + k)
                    moved = [dm[rows, where], dn2[s, rows, where], dp[rows, where]]
                    for q in range(3):
                        mix[q].append(wt[q] * moved[0] + wt[3 + q] * moved[1] + wt[6 + q] * moved[2])
                    v = v1[s, rows, where]
                    u = 1.0 + jnp.tanh(v)
                    us.append(u)
                    hs.append(v * u)
                left = later_bin(*mix[0])
                right = earlier_bin(*mix[2])
                for half in range(2):
                    out[half * HALF_W + k] = (left[half] + mix[1][half] + right[half]) * (
                        us[half] + hs[half] * (2.0 - us[half])
                    )
            return out

        def bins_step(j, carry):
            rows = pl.ds(pl.multiple_of(16 * j, 16), 16)
            low_rows = pl.ds(pl.multiple_of(EXP + 16 * j, 16), 16)
            for n, pair in enumerate(zip(bins_tile(2 * j), bins_tile(2 * j + 1))):
                high, low = halves(jnp.concatenate(pair, axis=0))
                hh[s, rows, on_lane(n)] = high
                hh[s, low_rows, on_lane(n)] = low
            return carry

        def taps_step(j, carry):
            rows = tile_rows(j)
            sums = [zero_tile] * TAPS
            for k in range(HALF_W):
                hs = []
                for half in range(2):
                    v = v1[s, rows, on_lane(half * HALF_W + k)]
                    hs.append(v + v * jnp.tanh(v))
                near = [earlier_bin(*hs), hs, later_bin(*hs)]
                for half in range(2):
                    where = on_lane(half * HALF_W + k)
                    moved = [dm[rows, where], dn2[s, rows, where], dp[rows, where]]
                    for q in range(3):
                        for p in range(3):
                            sums[3 * p + q] = sums[3 * p + q] + moved[p] * near[q][half]
            for t in range(TAPS):
                acc[t, rows, :] = acc[t, rows, :] + sums[t]
            return carry

        lax.fori_loop(0, EXP // 8, frames_step, 0, unroll=9)
        lax.fori_loop(0, EXP // 16, bins_step, 0, unroll=True)
        for j in range(EXP // 8):
            taps_step(j, 0)
        main = nt(xs[s, 0:64, :], hh[s, 0:EXP, :])
        main = main[0:32] + main[32:64] + nt(xs[s, 0:32, :], hh[s, EXP:, :])
        small[1] = small[1] + 0.5 * main[0:IN]
        small[2, 0:8, :] = small[2, 0:8, :] + 0.5 * main[IN:32]
        return carry

    lax.fori_loop(0, slots, taps_back_slot, 0)

    cross1 = jnp.sum(small[1] * weight, axis=0, keepdims=True)
    rb[3, me, 0:2, :] = split_row(small[2, 0:1, :])
    rb[3, me, 2:4, :] = split_row(cross1)
    tap_rows = [lane_sums(acc[t]) for t in range(TAPS)]
    late = [small[1, 8 * i : 8 * i + 8, :] for i in range(3)]
    late.append(jnp.concatenate(tap_rows[:8], axis=0))
    late.append(jnp.concatenate([tap_rows[8], jnp.zeros((7, EXP), F32)], axis=0))
    bulk_scatter(1, late, 8)
    spread_start(rb.at[3, me], rb.at[3, me], 7)
    bulk_gather(1, 8, 9)
    spread_wait(rb.at[3, pl.ds(0, n_dev - 1)], 7)
    sums = jnp.sum(rb[3], axis=0)
    bias1_grad = join_row(sums[0:2])
    gain1_grad = scale1 * join_row(sums[2:4])
    lean1 = scale1 * gain1_grad * (1.0 / total)

    for step in range(1, QUADS):
        def o_done(s, carry, step=step):
            o_copy(step, s).wait_send()
            x_copy(step, s).wait_send()
            c_copy(step, s).wait_send()
            return carry

        lax.fori_loop(0, slots, o_done, 0)
    grown = 0.5 * weight * grow1
    grown_high = grown.astype(BF16)
    grown_both = jnp.concatenate([grown_high.astype(F32), grown - grown_high.astype(F32)], axis=0).astype(BF16)
    lean_map = -2.0 * nt(grown * lean1, weight, FULL)
    flat_col = -2.0 * jnp.sum(grown * (bias1_grad * (1.0 / total)), axis=1, keepdims=True)
    side = jnp.concatenate([lean_map, flat_col, jnp.zeros((IN, 7), F32)], axis=1)
    side_high = side.astype(BF16).astype(F32)
    wlow[...] = jnp.concatenate([side_high, side_high, side - side_high], axis=1).astype(BF16)

    def last_slot(s, carry):
        main = nn(grown_both, hh[s, 0:EXP, :])
        main = main[:IN] + main[IN:] + nn(grown_high, hh[s, EXP:, :]) + nn(wlow[...], xs[s])
        for n in range(WIDE):
            add_to(xloc, s, n, main[:, n * LANES : (n + 1) * LANES])
        for step in range(1, QUADS):
            g_copy(step, s).start()
        return carry

    lax.fori_loop(0, slots, last_slot, 0)
    own_g = pltpu.make_async_copy(xloc.at[space], ing.at[pl.ds(slots * space, slots)], own_sem.at[3])
    own_g.start()

    early = bulk_tiles(0, 6, 5)
    late = bulk_tiles(1, 5, 9)
    project_grad = jnp.concatenate(early[:3], axis=0)
    excite_tile, reduce_tile, side_tile = early[3:]
    expand_cross = jnp.concatenate(late[:3], axis=0)
    depth_tiles = jnp.concatenate(late[3:], axis=0)
    expand_grad = grow1 * (expand_cross - lean1 * moment_w)
    zero_rows = jnp.zeros((16, EXP), F32)
    gs_out[0] = expand_grad
    gs_out[1] = project_grad
    gs_out[2] = jnp.concatenate([reduce_tile, zero_rows], axis=0)
    gs_out[3] = jnp.concatenate([excite_tile, zero_rows], axis=0)
    gs_out[4] = jnp.concatenate([depth_tiles, zero_rows[:8]], axis=0)
    vr_out[...] = jnp.concatenate(
        [
            gain1_grad,
            bias1_grad,
            gain2_grad,
            bias2_grad,
            jnp.concatenate([gain3_grad, jnp.zeros((1, EXP - LANES), F32)], axis=1),
            jnp.concatenate([bias3_grad, jnp.zeros((1, EXP - LANES), F32)], axis=1),
            side_tile[1:2],
            side_tile[0:1],
        ],
        axis=0,
    )

    mine = jnp.minimum(place, 4)
    grad = gs_out[mine]
    turned = (mine == 1) | (mine == 2)
    small[...] = jnp.zeros(small.shape, F32)
    small[0, :, :IN] = in_st[0]
    small[1, :, :IN] = jnp.transpose(in_st[1])
    small[2, :SQZ, :SQZ] = jnp.transpose(sq_st[:, 0, :])
    small[3, :SQZ, :SQZ] = sq_st[:, 1, :]
    small[4, :TAPS, :TAPS] = tap_st[...]
    old_big = big[mine]
    old_big = jnp.where(turned, jnp.transpose(old_big), old_big)
    big_m = DECAY * old_big + FRESH * tn(grad, grad, FULL)
    small_m = DECAY * small[mine][:, :IN] + FRESH * nt(grad, grad, FULL)
    big_eye = (
        lax.broadcasted_iota(jnp.int32, (EXP, EXP), 0) == lax.broadcasted_iota(jnp.int32, (EXP, EXP), 1)
    ).astype(F32)
    small_eye = eye24.astype(F32)
    big_c = 2.5 * lax.rsqrt(jnp.sum(jnp.sum(big_m * big_m, axis=0, keepdims=True), axis=1, keepdims=True))
    small_c = 2.5 * lax.rsqrt(jnp.sum(jnp.sum(small_m * small_m, axis=0, keepdims=True), axis=1, keepdims=True))
    big_m = big_c * big_m
    small_m = small_c * small_m
    direction = jnp.sqrt(jnp.sqrt(big_c)) * grad
    small_h = jnp.sqrt(jnp.sqrt(small_c)) * small_eye

    def root_step(i, carry):
        big_m, small_m, direction, small_h = carry
        big_k = 1.25 * big_eye - 0.25 * big_m
        small_k = 1.25 * small_eye - 0.25 * small_m
        direction = nn(direction, big_k, MID)
        small_h = nn(small_h, small_k, MID)
        big_k = nn(big_k, big_k, MID)
        small_k = nn(small_k, small_k, MID)
        big_k = nn(big_k, big_k, MID)
        small_k = nn(small_k, small_k, MID)
        return nn(big_k, big_m, MID), nn(small_k, small_m, MID), direction, small_h

    _, _, direction, small_h = lax.fori_loop(
        0, ROOT_ITERS, root_step, (big_m, small_m, direction, small_h)
    )
    direction = nn(small_h, direction, FULL)
    short = jnp.where(mine < 2, float(IN), jnp.where(mine == 4, float(TAPS), float(SQZ)))
    lead = jnp.where(turned, float(EXP), short)
    power = jnp.sum(jnp.sum(direction * direction, axis=0, keepdims=True), axis=1, keepdims=True)
    power = power / jnp.full((1, 1), short * float(EXP), F32)
    step_size = STEP_FRACTION * lax.rsqrt(jnp.full((1, 1), lead, F32)) * lax.rsqrt(power + 1e-06)
    small[0] = weight
    small[1] = w_pro_t[...]
    for i, source in ((2, w_red_t), (3, w_exc), (4, w_dep)):
        small[i] = jnp.zeros((IN, EXP), F32)
        small[i, : source.shape[0], :] = source[...]
    nws[place] = small[mine] - step_size * direction
    for step in range(1, GROUP):
        group_copy(nws.at[place], nws.at[place], 6, step).start()
    done = group_copy(nws.at[pl.ds(0, GROUP - 1)], nws.at[pl.ds(0, GROUP - 1)], 6, 1)
    done.wait_send()
    done.wait_recv()
    nw_out[...] = nws[0:5]

    for step in range(1, QUADS):
        def all_done(s, carry, step=step):
            o_copy(step, s).wait_recv()
            g_copy(step, s).wait()
            return carry

        lax.fori_loop(0, slots, all_done, 0)
    own_o.wait()
    own_g.wait()


def finish_kernel(
    gs, nw, vr, big, in_st, sq_st, tap_st, vec, vec_m, field_a, field_b,
    out, ing, ge, gd, gr_t, gx, gp_t, ne, nd, nr_t, nx, np_t, big_new, in_new, sq_new, tap_new, vg, vm, vn, held, sem,
):
    fields = ((field_a, out), (field_b, ing))
    loads = [pltpu.make_async_copy(source, held.at[i], sem.at[i]) for i, (source, _) in enumerate(fields)]
    stores = [pltpu.make_async_copy(held.at[i], target, sem.at[i]) for i, (_, target) in enumerate(fields)]
    for load in loads:
        load.start()
    ge[...], gp_t[...], gr_t[...], gx[...], gd[...] = gs[0], gs[1], gs[2, :SQZ], gs[3, :SQZ], gs[4, :TAPS]
    ne[...], np_t[...], nr_t[...], nx[...], nd[...] = nw[0], nw[1], nw[2, :SQZ], nw[3, :SQZ], nw[4, :TAPS]
    start = 0
    for i, width in enumerate(PARTS):
        vg[pl.ds(start, width)] = vr[i : i + 1, :width].reshape(width)
        start = start + width
    grads = vg[...]
    moments = DECAY * vec_m[...] + FRESH * grads * grads
    vm[...] = moments
    vn[...] = vec[...] - VECTOR_RATE * grads / (jnp.sqrt(moments) + 1e-08)
    for load, store in zip(loads, stores):
        load.wait()
        store.start()
    for i in range(5):
        grad = gs[i]
        big_new[i] = DECAY * big[i] + FRESH * tn(grad, grad, FULL)
        inner = FRESH * nt(grad, grad, FULL)
        if i < 2:
            in_new[i] = DECAY * in_st[i] + inner
        elif i < 4:
            sq_new[:, i - 2, :] = DECAY * sq_st[:, i - 2, :] + inner[:SQZ, :SQZ]
        else:
            tap_new[...] = DECAY * tap_st[...] + inner[:TAPS, :TAPS]
    for store in stores:
        store.wait()


def on_device(
    n_dev, n_space,
    features, cotangent, segment_ids, w_expand, w_depth, w_reduce, w_excite, w_project,
    vector_params, vector_moments, big_stats, in_stats, sq_stats, tap_stats,
):
    slot_count = features.shape[0]
    slots = slot_count // QUADS
    n_pos = slot_count * (n_dev // n_space) * FRAMES * BINS
    vm = pl.BlockSpec(memory_space=pltpu.VMEM)
    sq_rows = sq_stats.transpose(1, 0, 2)
    hbm = pl.BlockSpec(memory_space=pl.ANY)
    grid_shape = jax.ShapeDtypeStruct((slot_count, ROWS, LANES), F32)
    wide = WIDE * LANES
    vmem = pltpu.VMEM
    dma = pltpu.SemaphoreType.DMA
    out, ing, gs, nw, vr = pl.pallas_call(
        functools.partial(block_kernel, n_dev, n_space, slots, n_pos),
        out_shape=(
            grid_shape,
            grid_shape,
            jax.ShapeDtypeStruct((5, IN, EXP), F32),
            jax.ShapeDtypeStruct((5, IN, EXP), F32),
            jax.ShapeDtypeStruct((8, EXP), F32),
        ),
        in_specs=[hbm, hbm] + [vm] * 11,
        out_specs=(hbm, hbm, vm, vm, vm),
        scratch_shapes=[
            vmem((QUADS, slots, ROWS, LANES), F32),
            vmem((QUADS, slots, ROWS, LANES), F32),
            vmem((slots, 96, wide), BF16),
            vmem((slots, EXP, wide), F32),
            vmem((slots, EXP, wide), F32),
            vmem((slots, 2 * EXP, wide), BF16),
            vmem((slots, EXP, wide), F32),
            vmem((EXP, wide), F32),
            vmem((EXP, wide), F32),
            vmem((EXP, wide), F32),
            vmem((slots, IN, wide), F32),
            vmem((slots, slots * REGIONS, wide), BF16),
            vmem((slots, 448, wide), BF16),
            vmem((2, slots, 96, EXP), F32),
            vmem((TAPS + 3, EXP, LANES), F32),
            vmem((2, slots, 8, wide), F32),
            vmem((slots, 8, wide), jnp.int32),
            vmem((TAPS, EXP, LANES), F32),
            vmem((EXP, 96), BF16),
            vmem((IN, 96), BF16),
            vmem((8, EXP), F32),
            vmem((5, IN, EXP), F32),
            vmem((slots * REGIONS, EXP), F32),
            vmem((slots, REGIONS, EXP), F32),
            vmem((2, GROUP, 8, LANES), F32),
            vmem((2, GROUP, 8, LANES), F32),
            vmem((2, n_dev, 8, LANES), F32),
            vmem((n_dev, 8, LANES), F32),
            vmem((4, n_dev, 4, LANES), F32),
            vmem((GROUP, IN, EXP), F32),
            vmem((IN, LANES), F32),
            dma((QUADS,)),
        ]
        + [dma((QUADS, slots))] * 8
        + [dma((10,)), dma((10,)), dma((4,))],
        compiler_params=pltpu.CompilerParams(
            collective_id=0, has_side_effects=True, vmem_limit_bytes=62 << 20
        ),
    )(
        features.reshape(slot_count, ROWS, LANES),
        cotangent.reshape(slot_count, ROWS, LANES),
        segment_ids, w_expand, w_depth, w_reduce.T, w_excite, w_project.T, vector_params,
        big_stats, in_stats, sq_rows, tap_stats,
    )
    shape = jax.ShapeDtypeStruct
    (
        out, ing, ge, gd, gr_t, gx, gp_t, ne, nd, nr_t, nx, np_t, big_new, in_new, sq_new, tap_new, vg, vm_new, vn
    ) = pl.pallas_call(
        finish_kernel,
        out_shape=(grid_shape, grid_shape) + tuple(
            shape(dims, F32)
            for dims in [(IN, EXP), (TAPS, EXP), (SQZ, EXP), (SQZ, EXP), (IN, EXP)] * 2
            + [(5, EXP, EXP), (2, IN, IN), (SQZ, 2, SQZ), (TAPS, TAPS)]
            + [vector_params.shape] * 3
        ),
        in_specs=[vm] * 9 + [hbm] * 2,
        out_specs=(hbm, hbm) + (vm,) * 17,
        scratch_shapes=[vmem((2,) + grid_shape.shape, F32), dma((2,))],
        compiler_params=pltpu.CompilerParams(vmem_limit_bytes=62 << 20),
    )(gs, nw, vr, big_stats, in_stats, sq_rows, tap_stats, vector_params, vector_moments, out, ing)
    return (
        out.reshape(features.shape), ing.reshape(features.shape),
        ge, gd, gr_t.T, gx, gp_t.T, ne, nd, nr_t.T, nx, np_t.T,
        big_new, in_new, sq_new.transpose(1, 0, 2), tap_new, vg, vm_new, vn,
    )


def solution(mesh):
    field = P("dp", None, "space", None)
    return jax.shard_map(
        functools.partial(on_device, mesh.shape["dp"] * mesh.shape["space"], mesh.shape["space"]),
        mesh=mesh,
        in_specs=(field, field, P("dp", None)) + (P(),) * 11,
        out_specs=(field, field) + (P(),) * 17,
        check_vma=False,
    )
```

```python
import functools
import math

import jax
import jax.numpy as jnp
from jax import lax
from jax.experimental import pallas as pl
from jax.experimental.pallas import tpu as pltpu
from jax.sharding import PartitionSpec as P

IN = 24
EXP = 144
SQZ = 6
TAPS = 9
FRAMES = 96
BINS = 16
REGIONS = 4
QUADS = 4
ROOT_ITERS = 10
NORM_EPS = 0.001
DECAY = 0.9
FRESH = 1.0 - DECAY
STEP_FRACTION = 0.5
VECTOR_RATE = 0.15
PARTS = (EXP, EXP, EXP, EXP, IN, IN, SQZ, EXP)

LANES = 128
HALF_W = 6
WIDE = 2 * HALF_W
ROWS = IN * 3
GROUP = 8

F32 = jnp.float32
BF16 = jnp.bfloat16
FULL = lax.Precision.HIGHEST
MID = lax.Precision.HIGH
MESH = pl.DeviceIdType.MESH


def mm(left, right, dims, precision=None):
    return lax.dot_general(
        left, right, ((dims[:1], dims[1:]), ((), ())), precision=precision, preferred_element_type=F32
    )


def nn(left, right, precision=None):
    return mm(left, right, (1, 0), precision)


def nt(left, right, precision=None):
    return mm(left, right, (1, 1), precision)


def tn(left, right, precision=None):
    return mm(left, right, (0, 0), precision)


def halves(value):
    high = value.astype(BF16)
    return high, (value - high.astype(F32)).astype(BF16)


def column(rows, index, width):
    pick = (lax.broadcasted_iota(jnp.int32, (rows.shape[0], LANES), 0) == index).astype(F32)
    return tn(rows, pick, FULL)[:width]


def lane_sums(table):
    return nt(jnp.ones((8, table.shape[1]), F32), table, FULL)[0:1]


def split_row(row):
    return jnp.concatenate(
        [row[:, :LANES], jnp.concatenate([row[:, LANES:], jnp.zeros((1, 2 * LANES - EXP), F32)], axis=1)], axis=0
    )


def join_row(pair):
    return jnp.concatenate([pair[0:1], pair[1:2, : EXP - LANES]], axis=1)


def tile_quad(n):
    return 2 * ((n % HALF_W) // 3) + n // HALF_W


def on_lane(n):
    return pl.ds(n * LANES, LANES)


def block_kernel(
    n_dev, n_space, slots, n_pos,
    feat, cot, ids_ref, w_exp, w_dep, w_red_t, w_exc, w_pro_t, vec, big, in_st, sq_st, tap_st,
    out, ing, gs_out, nw_out, vr_out,
    xloc, xq, xs, v1, a2, hh, dn2, dh, dm, dp, eh, em, ep, hidden, a3, hot, dcat, prods, tab, msk, reg, acc, w1t, wlow, prm,
    small, pooled, gates, bulk, bulk_in, bulk_all, rb1, rb, nws, fold,
    loc_sem, x_send, x_recv, c_send, c_recv, o_send, o_recv, g_send, g_recv,
    r_send, r_recv, own_sem,
):
    space = lax.axis_index("space")
    me = lax.axis_index("dp") * n_space + space
    n_loc = float(slots * FRAMES * BINS)
    total = float(n_pos)

    def device(index):
        return (lax.div(index, n_space), lax.rem(index, n_space))

    def peer(step):
        return lax.rem(space + step, QUADS)

    def space_device(step):
        return (lax.axis_index("dp"), peer(step))

    barrier = pltpu.get_barrier_semaphore()

    def greet(step, carry):
        pl.semaphore_signal(
            barrier, inc=1, device_id=device(lax.rem(me + step, n_dev)), device_id_type=MESH
        )
        return carry

    lax.fori_loop(1, n_dev, greet, 0)
    loads = [
        pltpu.make_async_copy(feat.at[pl.ds(slots * q, slots)], xloc.at[q], loc_sem.at[q]) for q in range(QUADS)
    ]
    for load in loads:
        load.start()
    own_x = pltpu.make_async_copy(feat.at[pl.ds(slots * space, slots)], xq.at[space], own_sem.at[0])
    own_c = pltpu.make_async_copy(cot.at[pl.ds(slots * space, slots)], xloc.at[space], own_sem.at[1])
    own_x.start()

    for load in loads:
        load.wait()
    first = jnp.concatenate([xloc[0, 0, pl.ds(k, IN, stride=3), :] for k in range(3)], axis=1)
    shift_col = nn(first, jnp.ones((3 * LANES, LANES), F32), FULL) * (1.0 / (3 * LANES))
    shift_row = nt(jnp.ones((8, 3 * LANES), F32), first, FULL)[0:1] * (1.0 / (3 * LANES))
    one_rows = (lax.broadcasted_iota(jnp.int32, (8, LANES), 0) == 0).astype(F32)

    def gram_step(s, gram):
        parts = []
        for q in range(QUADS):
            for k in range(3):
                parts.append(
                    jnp.concatenate([xloc[q, s, pl.ds(k, IN, stride=3), :] - shift_col, one_rows], axis=0)
                )
        high, low = halves(jnp.concatenate(parts, axis=1))
        both = jnp.concatenate([high, low], axis=0)
        return gram + nt(both, both)

    gram = lax.fori_loop(0, slots, gram_step, jnp.zeros((64, 64), F32), unroll=True)
    gram = gram[:32, :32] + gram[32:, :32] + gram[:32, 32:] + gram[32:, 32:]
    off_row = gram[IN : IN + 1, :IN] * (1.0 / n_loc)
    off_col = gram[:IN, IN : IN + 1] * (1.0 / n_loc)
    local_m2 = gram[:IN, :IN] - n_loc * off_col * off_row
    fold[...] = jnp.zeros((IN, LANES), F32)
    fold[:, :IN] = local_m2
    packed = jnp.zeros((6, LANES), F32)
    for g in range(4):
        piece = fold[pl.ds(g, 6, stride=4), :]
        packed = packed + (pltpu.roll(piece, 32 * g, 1) if g else piece)
    rb1[me, 0:6, :] = packed
    rb1[me, 6:7, :] = jnp.concatenate([shift_row + off_row, jnp.zeros((1, LANES - IN), F32)], axis=1)
    rb1[me, 7:8, :] = jnp.zeros((1, LANES), F32)

    pl.semaphore_wait(barrier, n_dev - 1)

    def spread_start(source, target, index):
        def send(step, carry):
            pltpu.make_async_remote_copy(
                src_ref=source, dst_ref=target, send_sem=r_send.at[index], recv_sem=r_recv.at[index],
                device_id=device(lax.rem(me + step, n_dev)), device_id_type=MESH,
            ).start()
            return carry

        lax.fori_loop(1, n_dev, send, 0)

    def spread_wait(window, index):
        done = pltpu.make_async_remote_copy(
            src_ref=window, dst_ref=window, send_sem=r_send.at[index], recv_sem=r_recv.at[index],
            device_id=device(me), device_id_type=MESH,
        )
        done.wait_send()
        done.wait_recv()

    def quad_copy(source, target, send, recv, step, s):
        return pltpu.make_async_remote_copy(
            src_ref=source, dst_ref=target, send_sem=send.at[step, s], recv_sem=recv.at[step, s],
            device_id=space_device(step), device_id_type=MESH,
        )

    def x_copy(step, s):
        return quad_copy(feat.at[slots * peer(step) + s], xq.at[space, s], x_send, x_recv, step, s)

    def c_copy(step, s):
        return quad_copy(cot.at[slots * peer(step) + s], xloc.at[space, s], c_send, c_recv, step, s)

    def o_copy(step, s):
        return quad_copy(xq.at[peer(step), s], out.at[slots * space + s], o_send, o_recv, step, s)

    def g_copy(step, s):
        return quad_copy(xloc.at[peer(step), s], ing.at[slots * space + s], g_send, g_recv, step, s)

    base = lax.div(me, GROUP) * GROUP
    place = lax.rem(me, GROUP)

    def group_copy(source, target, index, step):
        return pltpu.make_async_remote_copy(
            src_ref=source, dst_ref=target, send_sem=r_send.at[index], recv_sem=r_recv.at[index],
            device_id=device(base + lax.rem(place + step, GROUP)), device_id_type=MESH,
        )

    def bulk_scatter(which, heads, index):
        for i in range(GROUP):
            bulk[which, i] = heads[i][:, :LANES] if i < len(heads) else jnp.zeros((8, LANES), F32)
        ends = [head[:, LANES:] for head in heads]
        rest = jnp.zeros((8, LANES - (EXP - LANES) * len(heads)), F32)
        bulk[which, len(heads)] = jnp.concatenate(ends + [rest], axis=1)
        for step in range(1, GROUP):
            other = lax.rem(place + step, GROUP)
            group_copy(bulk.at[which, other], bulk_in.at[which, place], index, step).start()
        bulk_in[which, place] = bulk[which, place]

    def bulk_gather(which, index, out_index):
        window = bulk_in.at[which, pl.ds(0, GROUP - 1)]
        done = group_copy(window, window, index, 1)
        done.wait_send()
        done.wait_recv()
        bulk_all[which, me] = jnp.sum(bulk_in[which], axis=0)
        spread_start(bulk_all.at[which, me], bulk_all.at[which, me], out_index)

    def bulk_tiles(which, count, out_index):
        spread_wait(bulk_all.at[which, pl.ds(0, n_dev - 1)], out_index)
        summed = []
        for i in range(count + 1):
            tile = bulk_all[which, i]
            for g in range(1, n_dev // GROUP):
                tile = tile + bulk_all[which, g * GROUP + i]
            summed.append(tile)
        width = EXP - LANES
        return [
            jnp.concatenate([summed[i], summed[count][:, width * i : width * (i + 1)]], axis=1)
            for i in range(count)
        ]

    spread_start(rb1.at[me], rb1.at[me], 0)

    def x_start(s, carry):
        for step in range(1, QUADS):
            x_copy(step, s).start()
        return carry

    lax.fori_loop(0, slots, x_start, 0)

    lane = lax.broadcasted_iota(jnp.int32, (8, LANES), 1)
    low_bin = lax.rem(lane, 8) == 0
    high_bin = lax.rem(lane, 8) == 7
    first_row = lane < 8
    second_row = (lane >= 8) & (lane < 16)
    last_row = lane >= LANES - 8
    zero_tile = jnp.zeros((8, LANES), F32)

    half_lanes = HALF_W * LANES
    own_ids = ids_ref[pl.ds(pl.multiple_of(slots * space, 8), slots), :].astype(F32)
    spread = (
        lax.broadcasted_iota(jnp.int32, (FRAMES, half_lanes), 1) // 8
        == lax.broadcasted_iota(jnp.int32, (FRAMES, half_lanes), 0)
    )
    wide_ids = nn(own_ids.astype(BF16), spread.astype(F32).astype(BF16))
    wide_lane = lax.broadcasted_iota(jnp.int32, (slots, half_lanes), 1)
    before = pltpu.roll(wide_ids, 8, 1)
    after = pltpu.roll(wide_ids, half_lanes - 8, 1)
    from_ok = jnp.where((before == wide_ids) & (wide_lane >= 8), 1.0, 0.0)
    to_ok = jnp.where((after == wide_ids) & (wide_lane < half_lanes - 8), 1.0, 0.0)
    def both_halves(rows):
        turned = [pltpu.roll(rows[:, n * LANES : (n + 1) * LANES], 8, 1) for n in range(HALF_W)]
        return jnp.concatenate([rows] + turned, axis=1)

    marks = [both_halves(rows) for rows in (from_ok, to_ok)]
    regions = [both_halves((wide_ids == float(r)).astype(F32)) for r in range(REGIONS)]
    region_ids = both_halves(wide_ids)
    for s in range(slots):
        for i in range(2):
            msk[i, s] = jnp.broadcast_to(marks[i][s : s + 1], (8, WIDE * LANES))
        reg[s] = jnp.broadcast_to(region_ids[s : s + 1], (8, WIDE * LANES)).astype(jnp.int32)
    row_index = lax.broadcasted_iota(jnp.int32, (slots * REGIONS, WIDE * LANES), 0)
    counts = jnp.zeros((slots * REGIONS, 1), F32)
    for s in range(slots):
        row = jnp.zeros((slots * REGIONS, WIDE * LANES), F32)
        for r in range(REGIONS):
            row = jnp.where(row_index == REGIONS * s + r, regions[r][s : s + 1], row)
        counts = counts + jnp.sum(row, axis=1, keepdims=True)
        hot[s] = row.astype(BF16)
    taps = w_dep[...]
    for t in range(TAPS):
        tab[t] = column(taps, t, EXP)

    start = 0
    prm[...] = jnp.zeros((8, EXP), F32)
    for i, width in enumerate(PARTS):
        prm[i : i + 1, :width] = vec[pl.ds(start, width)].reshape(1, width)
        start = start + width

    spread_wait(rb1.at[pl.ds(0, n_dev - 1)], 0)
    gathered = jnp.sum(rb1[...], axis=0)
    means = rb1[:, 6, :]
    mean_row = jnp.sum(means, axis=0, keepdims=True) * (1.0 / n_dev)
    apart = means - mean_row
    between = tn(apart, apart, FULL)[:IN, :IN]
    for g in range(4):
        piece = gathered[0:6]
        piece = pltpu.roll(piece, LANES - 32 * g, 1) if g else piece
        fold[pl.ds(g, 6, stride=4), :] = piece
    moment = fold[:, :IN] + n_loc * between
    eye24 = (
        lax.broadcasted_iota(jnp.int32, (IN, IN), 0) == lax.broadcasted_iota(jnp.int32, (IN, IN), 1)
    )
    mean_col = nn(jnp.where(eye24, mean_row[:, :IN], 0.0), jnp.ones((IN, LANES), F32), FULL)
    weight = w_exp[...]
    moment_w = nn(moment, weight, FULL)
    scale1 = lax.rsqrt(jnp.sum(moment_w * weight, axis=0, keepdims=True) * (1.0 / total) + NORM_EPS)
    grow1 = prm[0:1, :] * scale1
    shaped = jnp.concatenate(
        [weight * (0.5 * grow1), 0.5 * prm[1:2, :], jnp.zeros((7, EXP), F32)], axis=0
    )
    shaped_high = shaped.astype(BF16).astype(F32)
    w1t[...] = jnp.transpose(
        jnp.concatenate([shaped_high, shaped_high, shaped - shaped_high], axis=0)
    ).astype(BF16)

    own_x.wait()
    for i in (0, 2, 3):
        acc[i] = jnp.zeros((EXP, LANES), F32)

    def fetch(quads, s, n):
        tile = quads[tile_quad(n), s, pl.ds(n % 3, IN, stride=3), :]
        return tile if n < HALF_W else pltpu.roll(tile, 8, 1)

    def add_to(quads, s, n, tile):
        tile = tile if n < HALF_W else pltpu.roll(tile, LANES - 8, 1)
        where = pl.ds(n % 3, IN, stride=3)
        quads[tile_quad(n), s, where, :] = quads[tile_quad(n), s, where, :] + tile

    def later_bin(low, high):
        return (
            pltpu.roll(jnp.where(low_bin, high, low), LANES - 1, 1),
            jnp.where(high_bin, 0.0, pltpu.roll(high, LANES - 1, 1)),
        )

    def earlier_bin(low, high):
        return (
            jnp.where(low_bin, 0.0, pltpu.roll(low, 1, 1)),
            pltpu.roll(jnp.where(high_bin, low, high), 1, 1),
        )

    def from_before(tiles, k, half):
        edge = first_row if half else last_row
        return pltpu.roll(jnp.where(edge, tiles[(k - 1) % HALF_W], tiles[k]), 8, 1)

    def from_after(tiles, k, half):
        edge = second_row if half else first_row
        return pltpu.roll(jnp.where(edge, tiles[(k + 1) % HALF_W], tiles[k]), LANES - 8, 1)

    def tile_rows(j, height=8):
        return pl.ds(height * j, height) if isinstance(j, int) else pl.ds(pl.multiple_of(height * j, height), height)

    def expand_slot(s):
        for n in range(WIDE):
            tile = fetch(xq, s, n)
            high, low = halves(jnp.concatenate([tile - mean_col, one_rows], axis=0))
            xs[s, 0:32, on_lane(n)] = high
            xs[s, 32:64, on_lane(n)] = low
            xs[s, 64:96, on_lane(n)] = high
        v1[s] = nn(w1t[...], xs[s])

    def x_arrived(s):
        for step in range(1, QUADS):
            x_copy(step, s).wait_recv()

    def forward_slot(s, carry):
        def bins_step(j, carry):
            rows = pl.ds(pl.multiple_of(8 * j, 8), 8)
            wt = [tab[t, rows, :] for t in range(TAPS)]
            for k in range(HALF_W):
                pair = []
                for half in range(2):
                    v = v1[s, rows, on_lane(half * HALF_W + k)]
                    pair.append(v + v * jnp.tanh(v))
                nxt = later_bin(*pair)
                prv = earlier_bin(*pair)
                for half in range(2):
                    for p, target in enumerate((dm, dh, dp)):
                        target[rows, on_lane(half * HALF_W + k)] = (
                            wt[3 * p] * prv[half] + wt[3 * p + 1] * pair[half] + wt[3 * p + 2] * nxt[half]
                        )
            return carry

        def frames_step(j, carry):
            rows = tile_rows(j)
            center = acc[3, rows, :]
            got, square = zero_tile, zero_tile
            for half in range(2):
                prior = [dm[rows, on_lane(half * HALF_W + k)] for k in range(HALF_W)]
                later = [dp[rows, on_lane(half * HALF_W + k)] for k in range(HALF_W)]
                for k in range(HALF_W):
                    where = on_lane(half * HALF_W + k)
                    value = (
                        dh[rows, where]
                        + msk[0, s, :, where] * from_before(prior, k, half)
                        + msk[1, s, :, where] * from_after(later, k, half)
                    )
                    a2[s, rows, where] = value
                    off = value - center
                    got = got + off
                    square = square + off * off
            acc[0, rows, :] = acc[0, rows, :] + got
            acc[2, rows, :] = acc[2, rows, :] + square
            return carry

        lax.fori_loop(0, EXP // 8, bins_step, 0, unroll=9)

        @pl.when(s < slots - 1)
        def _():
            x_arrived(s + 1)

        expand_slot(jnp.minimum(s + 1, slots - 1))
        for j in range(EXP // 8):
            frames_step(j, 0)

        @pl.when(s == 0)
        def _():
            acc[3] = nn(acc[0], jnp.ones((LANES, LANES), F32), FULL) * (1.0 / (FRAMES * BINS))

            def again(j, carry):
                rows = tile_rows(j)
                center = acc[3, rows, :]
                got, square = zero_tile, zero_tile
                for n in range(WIDE):
                    off = a2[0, rows, on_lane(n)] - center
                    got = got + off
                    square = square + off * off
                acc[0, rows, :] = got
                acc[2, rows, :] = square
                return carry

            lax.fori_loop(0, EXP // 8, again, 0, unroll=3)

        return carry

    x_arrived(0)
    expand_slot(0)

    lax.fori_loop(0, slots, forward_slot, 0)

    drift = lane_sums(acc[0]) * (1.0 / n_loc)
    rb[0, me, 0:2, :] = split_row(lane_sums(acc[3]) * (1.0 / LANES) + drift)
    rb[0, me, 2:4, :] = split_row(lane_sums(acc[2]) - n_loc * drift * drift)
    spread_start(rb.at[0, me], rb.at[0, me], 1)
    def c_start(t, carry):
        for step in range(1, QUADS):
            c_copy(step, t).start()
        return carry

    lax.fori_loop(0, slots, c_start, 0)
    own_c.start()
    spread_wait(rb.at[0, pl.ds(0, n_dev - 1)], 1)
    sums = jnp.sum(rb[0], axis=0)
    mean2 = sums[0:2] * (1.0 / n_dev)
    gaps = rb[0][:, 0:2, :] - mean2[None]
    spread2 = sums[2:4] + n_loc * jnp.sum(gaps * gaps, axis=0)
    scale2 = lax.rsqrt(join_row(spread2) * (1.0 / total) + NORM_EPS)
    mean2 = join_row(mean2)
    rows8 = jnp.concatenate(
        [mean2, 0.5 * prm[2:3, :] * scale2, 0.5 * prm[3:4, :], jnp.zeros((5, EXP), F32)], axis=0
    )
    for i in range(3):
        tab[TAPS + i] = column(rows8, i, EXP)

    pooled[...] = jnp.zeros((slots * REGIONS, EXP), F32)

    def activate(s):
        for j in range(EXP // 16):
            rows, low_rows = pl.ds(16 * j, 16), pl.ds(EXP + 16 * j, 16)
            center, grow, lift = (tab[TAPS + i, rows, :] for i in range(3))
            for n in range(WIDE):
                off = a2[s, rows, on_lane(n)] - center
                a2[s, rows, on_lane(n)] = off
                v = off * grow + lift
                high, low = halves(v + v * jnp.tanh(v))
                hh[s, rows, on_lane(n)] = high
                hh[s, low_rows, on_lane(n)] = low

    def pool(s):
        pooled[...] = pooled[...] + nt(hot[s], hh[s, 0:EXP, :]) + nt(hot[s], hh[s, EXP:, :])

    def activate_slot(s, carry):
        pool(s - 1)
        activate(s)
        return carry

    activate(0)
    lax.fori_loop(1, slots, activate_slot, 0)
    pool(slots - 1)

    per_count = 1.0 / counts
    mean_pool = pooled[...] * per_count
    squeeze = nt(mean_pool, w_red_t[...], FULL) + prm[6:7, :SQZ]
    squeeze_sig = jax.nn.sigmoid(squeeze)
    squeezed = squeeze * squeeze_sig
    gate = jax.nn.sigmoid(nn(squeezed, w_exc[...], FULL) + prm[7:8, :])
    for s in range(slots):
        gates[s] = gate[REGIONS * s : REGIONS * (s + 1)]

    def gated_weights(s):
        project = w_pro_t[...]
        rows = gates[s]
        return jnp.concatenate([project * rows[r : r + 1] for r in range(REGIONS)], axis=0)

    def region_tile(s, n):
        return jnp.concatenate([reg[s, :, on_lane(n)]] * (IN // 8), axis=0)

    def project_slot(s, carry):
        total_a, total_c = carry
        high, low = halves(gated_weights(s))
        body = nn(jnp.concatenate([high, low], axis=0), hh[s, 0:EXP, :])
        body = body[:96] + body[96:] + nn(high, hh[s, EXP:, :])
        for step in range(1, QUADS):
            c_copy(step, s).wait_recv()
        for n in range(WIDE):
            value = jnp.zeros((IN, LANES), F32)
            ids = region_tile(s, n)
            for r in range(REGIONS):
                value = jnp.where(ids == r, body[IN * r : IN * (r + 1), n * LANES : (n + 1) * LANES], value)
            a3[s, :, on_lane(n)] = value
            total_a = total_a + value
            upstream = fetch(xloc, s, n)
            total_c = total_c + upstream
        return total_a, total_c

    own_c.wait()
    zero24 = jnp.zeros((IN, LANES), F32)
    total_a, total_c = lax.fori_loop(0, slots, project_slot, (zero24, zero24))
    center3 = nn(total_a, jnp.ones((LANES, LANES), F32), FULL) * (1.0 / n_loc)

    def third_step(s, carry):
        square, cross = carry
        for n in range(WIDE):
            off = a3[s, :, on_lane(n)] - center3
            square = square + off * off
            cross = cross + off * fetch(xloc, s, n)
        return square, cross

    square3, cross3 = lax.fori_loop(0, slots, third_step, (zero24, zero24))

    def pad_row(row):
        return jnp.concatenate([row, jnp.zeros((1, LANES - IN), F32)], axis=1)

    rb[1, me] = jnp.concatenate(
        [
            pad_row(lane_sums(total_a) * (1.0 / n_loc)),
            pad_row(lane_sums(square3)),
            pad_row(lane_sums(total_c)),
            pad_row(lane_sums(cross3)),
        ],
        axis=0,
    )
    spread_start(rb.at[1, me], rb.at[1, me], 2)

    def region_parts(s):
        for n in range(WIDE):
            where = on_lane(n)
            ids = region_tile(s, n)
            masks = [ids == r for r in range(REGIONS)]
            upstream = fetch(xloc, s, n)
            off = a3[s, :, where] - center3
            high, low = halves(jnp.concatenate([jnp.where(mask, upstream, 0.0) for mask in masks], axis=0))
            dcat[s, 0:96, where] = high
            dcat[s, 128:224, where] = low
            high, low = halves(jnp.concatenate([jnp.where(mask, off, 0.0) for mask in masks], axis=0))
            dcat[s, 256:352, where] = high
            dcat[s, 352:448, where] = low
        dcat[s, 96:128, :] = hot[s]
        dcat[s, 224:256, :] = hot[s]

    def region_products(s):
        main = nt(dcat[s], hh[s, 0:EXP, :])
        rest = nt(jnp.concatenate([dcat[s, 0:96, :], dcat[s, 256:352, :]], axis=0), hh[s, EXP:, :])
        prods[0, s] = main[0:96] + main[128:224] + rest[:96]
        prods[1, s] = main[256:352] + main[352:448] + rest[96:]

    def region_slot(s, carry):
        region_products(s - 1)
        region_parts(s)
        return carry

    region_parts(0)
    lax.fori_loop(1, slots, region_slot, 0)
    region_products(slots - 1)
    spread_wait(rb.at[1, pl.ds(0, n_dev - 1)], 2)
    third = rb[1]
    sums = jnp.sum(third, axis=0)
    mean3 = sums[0:1] * (1.0 / n_dev)
    gaps = third[:, 0, :] - mean3
    spread3 = sums[1:2] + n_loc * jnp.sum(gaps * gaps, axis=0, keepdims=True)
    scale3 = lax.rsqrt(spread3 * (1.0 / total) + NORM_EPS)
    bias3_grad = sums[2:3]
    cross_sum = sums[3:4] + jnp.sum(third[:, 2, :] * gaps, axis=0, keepdims=True)
    gain3_grad = scale3 * cross_sum
    grow3 = prm[4:5, :LANES] * scale3
    rows8 = jnp.concatenate(
        [
            mean3,
            grow3,
            prm[5:6, :LANES],
            grow3 * bias3_grad * (1.0 / total),
            grow3 * scale3 * gain3_grad * (1.0 / total),
            jnp.zeros((3, LANES), F32),
        ],
        axis=0,
    )
    mean3_c, grow3_c, lift3_c, flat3_c, lean3_c = (column(rows8, i, IN) for i in range(5))
    flat3_c = -flat3_c - (center3 - mean3_c) * lean3_c

    grow3_w, lean3_w, flat3_w = (
        jnp.concatenate([tile, tile[:, : EXP - LANES]], axis=1) for tile in (grow3_c, lean3_c, flat3_c)
    )
    project = w_pro_t[...]
    sums_of_h = pooled[...]
    small[0] = jnp.zeros((IN, EXP), F32)
    gate_rows = []
    for s in range(slots):
        gp = small[0]
        for r in range(REGIONS):
            q = REGIONS * s + r
            part = (
                grow3_w * prods[0, s, IN * r : IN * (r + 1), :]
                - lean3_w * prods[1, s, IN * r : IN * (r + 1), :]
                + flat3_w * sums_of_h[q : q + 1]
            )
            gate_rows.append(jnp.sum(part * project, axis=0, keepdims=True))
            gp = gp + part * gate[q : q + 1]
        small[0] = gp
    dgate_rows = jnp.concatenate(gate_rows, axis=0)

    dpre_x = dgate_rows * gate * (1.0 - gate)
    excite_grad = tn(squeezed, dpre_x, FULL)
    excite_bias_grad = jnp.sum(dpre_x, axis=0, keepdims=True)
    dsqueezed = nt(dpre_x, w_exc[...], FULL)
    dpre_r = dsqueezed * squeeze_sig * (1.0 + squeeze * (1.0 - squeeze_sig))
    reduce_grad = tn(dpre_r, mean_pool, FULL)
    reduce_bias_grad = jnp.sum(dpre_r, axis=0, keepdims=True)
    dpool = nn(dpre_r, w_red_t[...], FULL) * per_count
    pooled[...] = 0.5 * dpool + 0.5 * gate * jnp.sum(project * flat3_w, axis=0, keepdims=True)

    side_rows = jnp.concatenate(
        [excite_bias_grad, jnp.concatenate([reduce_bias_grad, jnp.zeros((1, EXP - SQZ), F32)], axis=1)], axis=0
    )
    early = [small[0, 8 * i : 8 * i + 8, :] for i in range(3)] + [
        jnp.concatenate([part, jnp.zeros((8 - part.shape[0], EXP), F32)], axis=0)
        for part in (excite_grad, reduce_grad, side_rows)
    ]
    bulk_scatter(0, early, 4)

    acc[0] = jnp.zeros((EXP, LANES), F32)
    acc[1] = jnp.zeros((EXP, LANES), F32)

    grown_project = 0.5 * project * grow3_w
    lean_project = -0.5 * project * lean3_w

    def activation_back(s, target):
        rows = gates[s]
        high, low = halves(jnp.concatenate([grown_project * rows[r : r + 1] for r in range(REGIONS)], axis=0))
        lean_high, lean_low = halves(
            jnp.concatenate([lean_project * rows[r : r + 1] for r in range(REGIONS)], axis=0)
        )
        pool_high, pool_low = halves(pooled[...])
        left = jnp.concatenate([high, pool_high, high, pool_low], axis=0)
        target[...] = (
            tn(left, dcat[s, 0:256, :])
            + tn(jnp.concatenate([lean_high, lean_high], axis=0), dcat[s, 256:448, :])
            + tn(jnp.concatenate([low, lean_low], axis=0), jnp.concatenate([dcat[s, 0:96, :], dcat[s, 256:352, :]], axis=0))
        )

    def leave(s):
        for n in range(WIDE):
            off = a3[s, :, on_lane(n)] - mean3_c
            add_to(xq, s, n, off * grow3_c + lift3_c)

    def norm_back(s, source):
        for j in range(EXP // 8):
            rows = tile_rows(j)
            grow, lift = (tab[TAPS + i, rows, :] for i in (1, 2))
            plain, cross = zero_tile, zero_tile
            for n in range(WIDE):
                off = a2[s, rows, on_lane(n)]
                v = off * grow + lift
                u = 1.0 + jnp.tanh(v)
                d = source[rows, on_lane(n)] * (u + (v * u) * (2.0 - u))
                dn2[s, rows, on_lane(n)] = d
                plain = plain + d
                cross = cross + d * off
            acc[0, rows, :] = acc[0, rows, :] + plain
            acc[1, rows, :] = acc[1, rows, :] + cross

    def second_back_pair(i, carry):
        s = 2 * i
        activation_back(s + 1, dm)
        norm_back(s, dh)
        leave(s)
        activation_back(jnp.minimum(s + 2, slots - 1), dh)
        norm_back(s + 1, dm)
        leave(s + 1)
        return carry

    activation_back(0, dh)
    lax.fori_loop(0, slots // 2, second_back_pair, 0)
    rb[2, me, 0:2, :] = split_row(lane_sums(acc[0]))
    rb[2, me, 2:4, :] = split_row(lane_sums(acc[1]))
    spread_start(rb.at[2, me], rb.at[2, me], 3)

    def o_start(s, carry):
        for step in range(1, QUADS):
            o_copy(step, s).start()
        return carry

    lax.fori_loop(0, slots, o_start, 0)
    own_o = pltpu.make_async_copy(xq.at[space], out.at[pl.ds(slots * space, slots)], own_sem.at[2])
    own_o.start()
    spread_wait(rb.at[2, pl.ds(0, n_dev - 1)], 3)
    bulk_gather(0, 4, 5)
    sums = jnp.sum(rb[2], axis=0)
    bias2_grad = join_row(sums[0:2])
    cross2 = join_row(sums[2:4])
    gain2_grad = cross2 * scale2
    grow2 = prm[2:3, :] * scale2
    rows8 = jnp.concatenate(
        [
            grow2,
            -grow2 * scale2 * gain2_grad * (1.0 / total),
            -grow2 * bias2_grad * (1.0 / total),
            jnp.zeros((5, EXP), F32),
        ],
        axis=0,
    )
    for i in range(3):
        tab[TAPS + i] = column(rows8, i, EXP)

    for t in range(TAPS):
        acc[t] = jnp.zeros((EXP, LANES), F32)
    small[1] = jnp.zeros((IN, EXP), F32)
    small[2] = jnp.zeros((IN, EXP), F32)

    def frames_back(s, j, moved):
        fore, back, here = moved
        rows = tile_rows(j)
        k1, k2, k3 = (tab[TAPS + i, rows, :] for i in range(3))
        for half in range(2):
            grads = []
            for k in range(HALF_W):
                where = on_lane(half * HALF_W + k)
                grads.append(k1 * dn2[s, rows, where] + k2 * a2[s, rows, where] + k3)
            for k in range(HALF_W):
                where = on_lane(half * HALF_W + k)
                here[rows, where] = grads[k]
                fore[rows, where] = msk[1, s, :, where] * from_after(grads, k, half)
                back[rows, where] = msk[0, s, :, where] * from_before(grads, k, half)

    def bins_back(s, j, moved):
        fore, back, here = moved
        rows = tile_rows(j)
        out = [None] * WIDE
        wt = [tab[t, rows, :] for t in range(TAPS)]
        for k in range(HALF_W):
            mix = [[], [], []]
            us, hs = [], []
            for half in range(2):
                where = on_lane(half * HALF_W + k)
                shifts = [fore[rows, where], here[rows, where], back[rows, where]]
                for q in range(3):
                    mix[q].append(wt[q] * shifts[0] + wt[3 + q] * shifts[1] + wt[6 + q] * shifts[2])
                v = v1[s, rows, where]
                u = 1.0 + jnp.tanh(v)
                us.append(u)
                hs.append(v * u)
                hidden[rows, where] = hs[half]
            left = later_bin(*mix[0])
            right = earlier_bin(*mix[2])
            for half in range(2):
                out[half * HALF_W + k] = (left[half] + mix[1][half] + right[half]) * (
                    us[half] + hs[half] * (2.0 - us[half])
                )
        return out

    def taps_back(s, j, moved):
        fore, back, here = moved
        rows = tile_rows(j)
        sums = [zero_tile] * TAPS
        for k in range(HALF_W):
            hs = [hidden[rows, on_lane(half * HALF_W + k)] for half in range(2)]
            near = [earlier_bin(*hs), hs, later_bin(*hs)]
            for half in range(2):
                where = on_lane(half * HALF_W + k)
                shifts = [fore[rows, where], here[rows, where], back[rows, where]]
                for q in range(3):
                    for p in range(3):
                        sums[3 * p + q] = sums[3 * p + q] + shifts[p] * near[q][half]
        for t in range(TAPS):
            acc[t, rows, :] = acc[t, rows, :] + sums[t]

    def taps_back_slot(s, moved, later):
        for j in range(EXP // 16):
            rows, low_rows = pl.ds(16 * j, 16), pl.ds(EXP + 16 * j, 16)
            for n, pair in enumerate(zip(bins_back(s, 2 * j, moved), bins_back(s, 2 * j + 1, moved))):
                high, low = halves(jnp.concatenate(pair, axis=0))
                hh[s, rows, on_lane(n)] = high
                hh[s, low_rows, on_lane(n)] = low
            frames_back(jnp.minimum(s + 1, slots - 1), j, later)
        for j in range(EXP // 8):
            taps_back(s, j, moved)
            if j >= EXP // 16:
                frames_back(jnp.minimum(s + 1, slots - 1), j, later)
        main = nt(xs[s, 0:64, :], hh[s, 0:EXP, :])
        main = main[0:32] + main[32:64] + nt(xs[s, 0:32, :], hh[s, EXP:, :])
        small[1] = small[1] + 0.5 * main[0:IN]
        small[2, 0:8, :] = small[2, 0:8, :] + 0.5 * main[IN:32]

    evens, odds = (dm, dp, dh), (em, ep, eh)

    def taps_back_pair(i, carry):
        s = 2 * i
        taps_back_slot(s, evens, odds)
        taps_back_slot(s + 1, odds, evens)
        return carry

    for j in range(EXP // 8):
        frames_back(0, j, evens)
    lax.fori_loop(0, slots // 2, taps_back_pair, 0)

    cross1 = jnp.sum(small[1] * weight, axis=0, keepdims=True)
    rb[3, me, 0:2, :] = split_row(small[2, 0:1, :])
    rb[3, me, 2:4, :] = split_row(cross1)
    spread_start(rb.at[3, me], rb.at[3, me], 7)
    tap_rows = [lane_sums(acc[t]) for t in range(TAPS)]
    late = [small[1, 8 * i : 8 * i + 8, :] for i in range(3)]
    late.append(jnp.concatenate(tap_rows[:8], axis=0))
    late.append(jnp.concatenate([tap_rows[8], jnp.zeros((7, EXP), F32)], axis=0))
    bulk_scatter(1, late, 8)
    bulk_gather(1, 8, 9)
    spread_wait(rb.at[3, pl.ds(0, n_dev - 1)], 7)
    sums = jnp.sum(rb[3], axis=0)
    bias1_grad = join_row(sums[0:2])
    gain1_grad = scale1 * join_row(sums[2:4])
    lean1 = scale1 * gain1_grad * (1.0 / total)

    for step in range(1, QUADS):
        def o_done(s, carry, step=step):
            o_copy(step, s).wait_send()
            x_copy(step, s).wait_send()
            c_copy(step, s).wait_send()
            return carry

        lax.fori_loop(0, slots, o_done, 0)
    grown = 0.5 * weight * grow1
    grown_high = grown.astype(BF16)
    grown_both = jnp.concatenate([grown_high.astype(F32), grown - grown_high.astype(F32)], axis=0).astype(BF16)
    lean_map = -2.0 * nt(grown * lean1, weight, FULL)
    flat_col = -2.0 * jnp.sum(grown * (bias1_grad * (1.0 / total)), axis=1, keepdims=True)
    side = jnp.concatenate([lean_map, flat_col, jnp.zeros((IN, 7), F32)], axis=1)
    side_high = side.astype(BF16).astype(F32)
    wlow[...] = jnp.concatenate([side_high, side_high, side - side_high], axis=1).astype(BF16)

    def last_slot(s, carry):
        main = nn(grown_both, hh[s, 0:EXP, :])
        main = main[:IN] + main[IN:] + nn(grown_high, hh[s, EXP:, :]) + nn(wlow[...], xs[s])
        for n in range(WIDE):
            add_to(xloc, s, n, main[:, n * LANES : (n + 1) * LANES])
        for step in range(1, QUADS):
            g_copy(step, s).start()
        return carry

    lax.fori_loop(0, slots, last_slot, 0)
    own_g = pltpu.make_async_copy(xloc.at[space], ing.at[pl.ds(slots * space, slots)], own_sem.at[3])
    own_g.start()

    early = bulk_tiles(0, 6, 5)
    late = bulk_tiles(1, 5, 9)
    project_grad = jnp.concatenate(early[:3], axis=0)
    excite_tile, reduce_tile, side_tile = early[3:]
    expand_cross = jnp.concatenate(late[:3], axis=0)
    depth_tiles = jnp.concatenate(late[3:], axis=0)
    expand_grad = grow1 * (expand_cross - lean1 * moment_w)
    zero_rows = jnp.zeros((16, EXP), F32)
    gs_out[0] = expand_grad
    gs_out[1] = project_grad
    gs_out[2] = jnp.concatenate([reduce_tile, zero_rows], axis=0)
    gs_out[3] = jnp.concatenate([excite_tile, zero_rows], axis=0)
    gs_out[4] = jnp.concatenate([depth_tiles, zero_rows[:8]], axis=0)
    vr_out[...] = jnp.concatenate(
        [
            gain1_grad,
            bias1_grad,
            gain2_grad,
            bias2_grad,
            jnp.concatenate([gain3_grad, jnp.zeros((1, EXP - LANES), F32)], axis=1),
            jnp.concatenate([bias3_grad, jnp.zeros((1, EXP - LANES), F32)], axis=1),
            side_tile[1:2],
            side_tile[0:1],
        ],
        axis=0,
    )

    mine = jnp.minimum(place, 4)
    grad = gs_out[mine]
    turned = (mine == 1) | (mine == 2)
    small[...] = jnp.zeros(small.shape, F32)
    small[0, :, :IN] = in_st[0]
    small[1, :, :IN] = jnp.transpose(in_st[1])
    small[2, :SQZ, :SQZ] = jnp.transpose(sq_st[:, 0, :])
    small[3, :SQZ, :SQZ] = sq_st[:, 1, :]
    small[4, :TAPS, :TAPS] = tap_st[...]
    old_big = big[mine]
    old_big = jnp.where(turned, jnp.transpose(old_big), old_big)
    big_m = DECAY * old_big + FRESH * tn(grad, grad, MID)
    small_m = DECAY * small[mine][:, :IN] + FRESH * nt(grad, grad, MID)
    big_eye = (
        lax.broadcasted_iota(jnp.int32, (EXP, EXP), 0) == lax.broadcasted_iota(jnp.int32, (EXP, EXP), 1)
    ).astype(F32)
    small_eye = eye24.astype(F32)
    big_c = 2.5 * lax.rsqrt(jnp.sum(jnp.sum(big_m * big_m, axis=0, keepdims=True), axis=1, keepdims=True))
    small_c = 2.5 * lax.rsqrt(jnp.sum(jnp.sum(small_m * small_m, axis=0, keepdims=True), axis=1, keepdims=True))
    big_m = big_c * big_m
    small_m = small_c * small_m
    direction = jnp.sqrt(jnp.sqrt(big_c)) * grad
    small_h = jnp.sqrt(jnp.sqrt(small_c)) * small_eye

    def root_step(i, carry):
        big_m, small_m, direction, small_h = carry
        big_k = 1.25 * big_eye - 0.25 * big_m
        small_k = 1.25 * small_eye - 0.25 * small_m
        direction = nn(direction, big_k, MID)
        small_h = nn(small_h, small_k, MID)
        big_k = nn(big_k, big_k, MID)
        small_k = nn(small_k, small_k, MID)
        big_k = nn(big_k, big_k, MID)
        small_k = nn(small_k, small_k, MID)
        return nn(big_k, big_m, MID), nn(small_k, small_m, MID), direction, small_h

    big_m, small_m, direction, small_h = lax.fori_loop(
        0, ROOT_ITERS - 1, root_step, (big_m, small_m, direction, small_h)
    )
    direction = nn(direction, 1.25 * big_eye - 0.25 * big_m, MID)
    small_h = nn(small_h, 1.25 * small_eye - 0.25 * small_m, MID)
    direction = nn(small_h, direction, MID)
    short = jnp.where(mine < 2, float(IN), jnp.where(mine == 4, float(TAPS), float(SQZ)))
    lead = jnp.where(turned, float(EXP), short)
    power = jnp.sum(jnp.sum(direction * direction, axis=0, keepdims=True), axis=1, keepdims=True)
    power = power / jnp.full((1, 1), short * float(EXP), F32)
    step_size = STEP_FRACTION * lax.rsqrt(jnp.full((1, 1), lead, F32)) * lax.rsqrt(power + 1e-06)
    small[0] = weight
    small[1] = w_pro_t[...]
    for i, source in ((2, w_red_t), (3, w_exc), (4, w_dep)):
        small[i] = jnp.zeros((IN, EXP), F32)
        small[i, : source.shape[0], :] = source[...]
    nws[place] = small[mine] - step_size * direction
    for step in range(1, GROUP):
        group_copy(nws.at[place], nws.at[place], 6, step).start()
    done = group_copy(nws.at[pl.ds(0, GROUP - 1)], nws.at[pl.ds(0, GROUP - 1)], 6, 1)
    done.wait_send()
    done.wait_recv()
    nw_out[...] = nws[0:5]

    for step in range(1, QUADS):
        def all_done(s, carry, step=step):
            o_copy(step, s).wait_recv()
            g_copy(step, s).wait()
            return carry

        lax.fori_loop(0, slots, all_done, 0)
    own_o.wait()
    own_g.wait()


def finish_kernel(
    gs, nw, vr, big, in_st, sq_st, tap_st, vec, vec_m, field_a, field_b,
    out, ing, ge, gd, gr_t, gx, gp_t, ne, nd, nr_t, nx, np_t, big_new, in_new, sq_new, tap_new, vg, vm, vn, held, sem,
):
    fields = ((field_a, out), (field_b, ing))
    loads = [pltpu.make_async_copy(source, held.at[i], sem.at[i]) for i, (source, _) in enumerate(fields)]
    stores = [pltpu.make_async_copy(held.at[i], target, sem.at[i]) for i, (_, target) in enumerate(fields)]
    for load in loads:
        load.start()
    ge[...], gp_t[...], gr_t[...], gx[...], gd[...] = gs[0], gs[1], gs[2, :SQZ], gs[3, :SQZ], gs[4, :TAPS]
    ne[...], np_t[...], nr_t[...], nx[...], nd[...] = nw[0], nw[1], nw[2, :SQZ], nw[3, :SQZ], nw[4, :TAPS]
    start = 0
    for i, width in enumerate(PARTS):
        vg[pl.ds(start, width)] = vr[i : i + 1, :width].reshape(width)
        start = start + width
    grads = vg[...]
    moments = DECAY * vec_m[...] + FRESH * grads * grads
    vm[...] = moments
    vn[...] = vec[...] - VECTOR_RATE * grads / (jnp.sqrt(moments) + 1e-08)
    for load, store in zip(loads, stores):
        load.wait()
        store.start()
    for i in range(5):
        grad = gs[i]
        big_new[i] = DECAY * big[i] + FRESH * tn(grad, grad, MID)
        inner = FRESH * nt(grad, grad, MID)
        if i < 2:
            in_new[i] = DECAY * in_st[i] + inner
        elif i < 4:
            sq_new[:, i - 2, :] = DECAY * sq_st[:, i - 2, :] + inner[:SQZ, :SQZ]
        else:
            tap_new[...] = DECAY * tap_st[...] + inner[:TAPS, :TAPS]
    for store in stores:
        store.wait()


def on_device(
    n_dev, n_space,
    features, cotangent, segment_ids, w_expand, w_depth, w_reduce, w_excite, w_project,
    vector_params, vector_moments, big_stats, in_stats, sq_stats, tap_stats,
):
    slot_count = features.shape[0]
    slots = slot_count // QUADS
    n_pos = slot_count * (n_dev // n_space) * FRAMES * BINS
    vm = pl.BlockSpec(memory_space=pltpu.VMEM)
    sq_rows = sq_stats.transpose(1, 0, 2)
    hbm = pl.BlockSpec(memory_space=pl.ANY)
    grid_shape = jax.ShapeDtypeStruct((slot_count, ROWS, LANES), F32)
    wide = WIDE * LANES
    vmem = pltpu.VMEM
    dma = pltpu.SemaphoreType.DMA
    out, ing, gs, nw, vr = pl.pallas_call(
        functools.partial(block_kernel, n_dev, n_space, slots, n_pos),
        out_shape=(
            grid_shape,
            grid_shape,
            jax.ShapeDtypeStruct((5, IN, EXP), F32),
            jax.ShapeDtypeStruct((5, IN, EXP), F32),
            jax.ShapeDtypeStruct((8, EXP), F32),
        ),
        in_specs=[hbm, hbm] + [vm] * 11,
        out_specs=(hbm, hbm, vm, vm, vm),
        scratch_shapes=[
            vmem((QUADS, slots, ROWS, LANES), F32),
            vmem((QUADS, slots, ROWS, LANES), F32),
            vmem((slots, 96, wide), BF16),
            vmem((slots, EXP, wide), F32),
            vmem((slots, EXP, wide), F32),
            vmem((slots, 2 * EXP, wide), BF16),
            vmem((slots, EXP, wide), F32),
            vmem((EXP, wide), F32),
            vmem((EXP, wide), F32),
            vmem((EXP, wide), F32),
            vmem((EXP, wide), F32),
            vmem((EXP, wide), F32),
            vmem((EXP, wide), F32),
            vmem((EXP, wide), F32),
            vmem((slots, IN, wide), F32),
            vmem((slots, slots * REGIONS, wide), BF16),
            vmem((slots, 448, wide), BF16),
            vmem((2, slots, 96, EXP), F32),
            vmem((TAPS + 3, EXP, LANES), F32),
            vmem((2, slots, 8, wide), F32),
            vmem((slots, 8, wide), jnp.int32),
            vmem((TAPS, EXP, LANES), F32),
            vmem((EXP, 96), BF16),
            vmem((IN, 96), BF16),
            vmem((8, EXP), F32),
            vmem((5, IN, EXP), F32),
            vmem((slots * REGIONS, EXP), F32),
            vmem((slots, REGIONS, EXP), F32),
            vmem((2, GROUP, 8, LANES), F32),
            vmem((2, GROUP, 8, LANES), F32),
            vmem((2, n_dev, 8, LANES), F32),
            vmem((n_dev, 8, LANES), F32),
            vmem((4, n_dev, 4, LANES), F32),
            vmem((GROUP, IN, EXP), F32),
            vmem((IN, LANES), F32),
            dma((QUADS,)),
        ]
        + [dma((QUADS, slots))] * 8
        + [dma((10,)), dma((10,)), dma((4,))],
        compiler_params=pltpu.CompilerParams(
            collective_id=0, has_side_effects=True, vmem_limit_bytes=62 << 20
        ),
    )(
        features.reshape(slot_count, ROWS, LANES),
        cotangent.reshape(slot_count, ROWS, LANES),
        segment_ids, w_expand, w_depth, w_reduce.T, w_excite, w_project.T, vector_params,
        big_stats, in_stats, sq_rows, tap_stats,
    )
    shape = jax.ShapeDtypeStruct
    (
        out, ing, ge, gd, gr_t, gx, gp_t, ne, nd, nr_t, nx, np_t, big_new, in_new, sq_new, tap_new, vg, vm_new, vn
    ) = pl.pallas_call(
        finish_kernel,
        out_shape=(grid_shape, grid_shape) + tuple(
            shape(dims, F32)
            for dims in [(IN, EXP), (TAPS, EXP), (SQZ, EXP), (SQZ, EXP), (IN, EXP)] * 2
            + [(5, EXP, EXP), (2, IN, IN), (SQZ, 2, SQZ), (TAPS, TAPS)]
            + [vector_params.shape] * 3
        ),
        in_specs=[vm] * 9 + [hbm] * 2,
        out_specs=(hbm, hbm) + (vm,) * 17,
        scratch_shapes=[vmem((2,) + grid_shape.shape, F32), dma((2,))],
        compiler_params=pltpu.CompilerParams(vmem_limit_bytes=62 << 20),
    )(gs, nw, vr, big_stats, in_stats, sq_rows, tap_stats, vector_params, vector_moments, out, ing)
    return (
        out.reshape(features.shape), ing.reshape(features.shape),
        ge, gd, gr_t.T, gx, gp_t.T, ne, nd, nr_t.T, nx, np_t.T,
        big_new, in_new, sq_new.transpose(1, 0, 2), tap_new, vg, vm_new, vn,
    )


def solution(mesh):
    field = P("dp", None, "space", None)
    return jax.shard_map(
        functools.partial(on_device, mesh.shape["dp"] * mesh.shape["space"], mesh.shape["space"]),
        mesh=mesh,
        in_specs=(field, field, P("dp", None)) + (P(),) * 11,
        out_specs=(field, field) + (P(),) * 17,
        check_vma=False,
    )
```
